32 devices in a mesh: groups: 2 (over x), row: 8 (over z, y), col: 2 (over core).
Axes of the slice: x: 2, y: 2, z: 4, core: 2. Of those that a mesh axis runs over, the one named last changes fastest.
Arguments:
- gradient: bfloat16 [8192, 7168], P(('groups', 'row'), 'col'), parts along dimension 0, may hold values from -0.25 to 0.25
- left_old: float32 [8192, 4096], P(('groups', 'row'), 'col'), parts along dimension 0, may hold values from -6 to 6
- right_old: float32 [4, 3584, 3584], P(('groups', 'col'), 'row'), parts along dimension 0, may hold values from -6 to 6
- left_counts: int32 [16, 2], P(('groups', 'row'), 'col'), parts along dimension 0, may hold values from 0 to 29
- right_counts: int32 [4], P(('groups', 'col')), parts along dimension 0, may hold values from 0 to 29
Outputs:
- left_state: float32 [8192, 4096], P(('groups', 'row'), 'col'), parts along dimension 0
- left_fixed: float32 [8192, 4096], P(('groups', 'row'), 'col'), parts along dimension 0
- right_state: float32 [4, 3584, 3584], P(('groups', 'col'), 'row'), parts along dimension 0
- right_fixed: float32 [4, 3584, 3584], P(('groups', 'col'), 'row'), parts along dimension 0
The draws below stay inside these ranges and needn't reach their ends.
There are 2 independent parts, one for each index of `groups`. The reference program is written for one: setup_inputs(seed, part) draws one part's arguments, and reference() takes and returns one part's arrays. A program takes and returns all parts, laid end to end along the dimension named above; each array names one. Nothing has to cross between parts.
All inputs are finite; a program needn't handle non-finite values.
Results may differ from the reference program's by a relative error of at most 0.0003.
Values may be sent and summed in bfloat16 or wider, within the bound.
No kernel may reach another device: no remote copies, remote signals or barrier semaphores. Data moves between devices by JAX's collectives and lax.ppermute only.
A program may use at most 192 MiB of HBM per device.

```python
import jax
import jax.numpy as jnp
from jax import lax

DW = 4096
FFW = 7168
RBW = 3584
RB = 2
TILE_R = 512
TILE_C = 2048


def touch_ends(values, rng, least, high):
    spot = [jax.random.randint(jax.random.fold_in(rng, axis), (), 0, length) for axis, length in enumerate(values.shape)]
    main_axis = values.shape.index(max(values.shape))
    next_to = spot[:main_axis] + [(spot[main_axis] + 1) % values.shape[main_axis]] + spot[main_axis + 1:]
    return values.at[tuple(spot)].set(least).at[tuple(next_to)].set(high)


def steps_of(stream_key, shape, shards, least, high):
    def one(axis_at, parts):
        heights = jax.random.uniform(jax.random.fold_in(jax.random.fold_in(stream_key, 6), axis_at), (parts,), jnp.float32, least / len(shards), high / len(shards))
        return jnp.repeat(jnp.exp(heights), shape[axis_at] // parts).reshape((-1,) + (1,) * (len(shape) - axis_at - 1))

    level = one(*shards[0])
    for cut in shards[1:]:
        level = level * one(*cut)
    return level


def scatter_about(rng, extent, scale, most, shards=(), held_as=jnp.bfloat16):
    result = jax.random.normal(rng, extent, jnp.float32) * scale
    if len(shards) > 0:
        result = steps_of(rng, extent, shards, -0.22, 0.18) * result
    return jnp.clip(result, min=-most, max=most).astype(held_as)


def setup_inputs(seed: int = 0, part: int = 0) -> dict:
    key_list = jax.random.split(jax.random.key(seed), 6)
    part_keys = jax.random.split(jax.random.fold_in(key_list[5], part), 6)
    return {
        "gradient": scatter_about(part_keys[0], (DW, FFW), (FFW // 16) ** -0.5, 0.25, ((0, 8), (1, 2))),
        "left_old": scatter_about(part_keys[1], (DW, DW), 1.0, 6.0, ((0, 8), (1, 2)), jnp.float32),
        "right_old": scatter_about(part_keys[2], (RB, RBW, RBW), 1.0, 6.0, ((0, 2), (1, 8)), jnp.float32),
        "left_counts": touch_ends(jax.random.randint(part_keys[3], (DW // TILE_R, DW // TILE_C), 0, 30), jax.random.fold_in(part_keys[3], 1), 0, 29).astype(jnp.int32),
        "right_counts": jax.random.randint(part_keys[4], (RB,), 0, 30).astype(jnp.int32),
    }


BETA = 0.9


def denominator(counters):
    decay_power = jnp.power(jnp.float32(BETA), (counters + 1).astype(jnp.float32))
    return 1.0 - decay_power


def block_gram(block_cols):
    return jnp.dot(block_cols.T, block_cols, preferred_element_type=jnp.float32, precision=lax.Precision.HIGHEST)


def reference(gradient, left_old, right_old, left_counts, right_counts):
    widened = gradient.astype(jnp.float32)
    gram_left = jnp.dot(widened, widened.T, preferred_element_type=jnp.float32, precision=lax.Precision.HIGHEST)
    column_blocks = jnp.transpose(widened.reshape(DW, RB, RBW), (1, 0, 2))
    gram_right = lax.map(block_gram, column_blocks)
    left_state = BETA * left_old + (1.0 - BETA) * gram_left
    right_state = BETA * right_old + (1.0 - BETA) * gram_right
    tiles_down, tiles_across = left_counts.shape
    shaped = left_state.reshape(tiles_down, DW // tiles_down, tiles_across, DW // tiles_across)
    left_fixed = (shaped / denominator(left_counts)[:, None, :, None]).reshape(DW, DW)
    right_fixed = right_state / denominator(right_counts)[:, None, None]
    return left_state, left_fixed, right_state, right_fixed
```

```python
import jax
import jax.numpy as jnp
from jax import lax
from jax.sharding import PartitionSpec as P

BETA = 0.9


def denominator(counters):
    decay_power = jnp.power(jnp.float32(BETA), (counters + 1).astype(jnp.float32))
    return 1.0 - decay_power


def ring_order(count):
    if count == 8:
        return [0, 2, 4, 6, 7, 5, 3, 1]
    return list(range(count))


def local(gradient, left_old, right_old, left_counts, right_counts):
    tile_rows, half_wide = gradient.shape
    count = lax.axis_size("row")
    strip_wide = half_wide // count
    order = ring_order(count)
    place = {row: at for at, row in enumerate(order)}
    my_row = lax.axis_index("row")
    my_col = lax.axis_index("col")
    up = [(order[at], order[(at + 1) % count]) for at in range(count)]
    down = [(dest, source) for source, dest in up]
    piece = tile_rows // 2
    strip_at = my_row * strip_wide

    state = {"left": jnp.zeros((tile_rows, count * tile_rows), jnp.float32), "right": None}

    def consume(part, step, offset):
        sources = [order[(place[row] - step) % count] for row in range(count)]
        source = jnp.asarray(sources, jnp.int32)[my_row]
        product = lax.dot_general(
            gradient, part, (((1,), (1,)), ((), ())), preferred_element_type=jnp.float32
        )
        pairs = []
        for row in range(count):
            keeper = sources[row] * 2 // count
            pairs.append((row * 2 + 1 - keeper, row * 2 + keeper))
        other = lax.ppermute(product, ("row", "col"), pairs)
        state["left"] = lax.dynamic_update_slice(
            state["left"], product + other, (0, source * tile_rows + offset)
        )
        strip = lax.dynamic_slice_in_dim(part, strip_at, strip_wide, 1)
        term = lax.dot_general(
            strip, part, (((0,), (0,)), ((), ())), preferred_element_type=jnp.float32
        )
        state["right"] = term if state["right"] is None else state["right"] + term

    halves = [gradient[:piece], gradient[piece:]]
    going_up = list(halves)
    going_down = list(halves)
    last = count // 2
    for step in range(1, last + 1):
        if step < last:
            going_up = [lax.ppermute(part, "row", up) for part in going_up]
            going_down = [lax.ppermute(part, "row", down) for part in going_down]
        else:
            going_up = [lax.ppermute(going_up[0], "row", up)]
            going_down = [lax.ppermute(going_down[1], "row", down)]
        if step == 1:
            consume(halves[0], 0, 0)
            consume(halves[1], 0, piece)
        if step < last:
            for at in range(2):
                consume(going_up[at], step, at * piece)
                consume(going_down[at], -step, at * piece)
        else:
            consume(going_up[0], step, 0)
            consume(going_down[0], step, piece)

    width = count * tile_rows // 2
    gram_left = lax.dynamic_slice_in_dim(state["left"], my_col * width, width, 1)
    left_state = BETA * left_old + (1.0 - BETA) * gram_left
    left_fixed = left_state / denominator(left_counts)
    right_state = BETA * right_old + (1.0 - BETA) * state["right"][None]
    right_fixed = right_state / denominator(right_counts)[:, None, None]
    return (left_state, left_fixed, right_state, right_fixed)


def solution(mesh):
    return jax.shard_map(
        local,
        mesh=mesh,
        in_specs=(
            P(("groups", "row"), "col"),
            P(("groups", "row"), "col"),
            P(("groups", "col"), "row", None),
            P(("groups", "row"), "col"),
            P(("groups", "col")),
        ),
        out_specs=(
            P(("groups", "row"), "col"),
            P(("groups", "row"), "col"),
            P(("groups", "col"), "row", None),
            P(("groups", "col"), "row", None),
        ),
        check_vma=False,
    )
```

```python
import jax
import jax.numpy as jnp
from jax import lax
from jax.sharding import PartitionSpec as P

BETA = 0.9


def denominator(counters):
    decay_power = jnp.power(jnp.float32(BETA), (counters + 1).astype(jnp.float32))
    return 1.0 - decay_power


def ring_order(count):
    if count == 8:
        return [0, 2, 4, 6, 7, 5, 3, 1]
    return list(range(count))


def ring(gradient, left_old, right_old, left_counts, right_counts):
    tile_rows, half_wide = gradient.shape
    count = lax.axis_size("row")
    strip_wide = half_wide // count
    order = ring_order(count)
    place = {row: at for at, row in enumerate(order)}
    my_row = lax.axis_index("row")
    my_col = lax.axis_index("col")
    up = [(order[at], order[(at + 1) % count]) for at in range(count)]
    down = [(dest, source) for source, dest in up]
    piece = tile_rows // 2
    strip_at = my_row * strip_wide

    state = {"left": jnp.zeros((tile_rows, count * tile_rows), jnp.float32), "right": None}

    def consume(part, step, offset):
        sources = [order[(place[row] - step) % count] for row in range(count)]
        source = jnp.asarray(sources, jnp.int32)[my_row]
        product = lax.dot_general(
            gradient, part, (((1,), (1,)), ((), ())), preferred_element_type=jnp.float32
        )
        pairs = []
        for row in range(count):
            keeper = sources[row] * 2 // count
            pairs.append((row * 2 + 1 - keeper, row * 2 + keeper))
        other = lax.ppermute(product, ("row", "col"), pairs)
        state["left"] = lax.dynamic_update_slice(
            state["left"], product + other, (0, source * tile_rows + offset)
        )
        strip = lax.dynamic_slice_in_dim(part, strip_at, strip_wide, 1)
        term = lax.dot_general(
            strip, part, (((0,), (0,)), ((), ())), preferred_element_type=jnp.float32
        )
        state["right"] = term if state["right"] is None else state["right"] + term

    halves = [gradient[:piece], gradient[piece:]]
    going_up = list(halves)
    going_down = list(halves)
    last = count // 2
    for step in range(1, last + 1):
        if step < last:
            going_up = [lax.ppermute(part, "row", up) for part in going_up]
            going_down = [lax.ppermute(part, "row", down) for part in going_down]
        else:
            going_up = [lax.ppermute(going_up[0], "row", up)]
            going_down = [lax.ppermute(going_down[1], "row", down)]
        if step == 1:
            consume(halves[0], 0, 0)
            consume(halves[1], 0, piece)
        if step < last:
            for at in range(2):
                consume(going_up[at], step, at * piece)
                consume(going_down[at], -step, at * piece)
        else:
            consume(going_up[0], step, 0)
            consume(going_down[0], step, piece)

    width = count * tile_rows // 2
    gram_left = lax.dynamic_slice_in_dim(state["left"], my_col * width, width, 1)
    left_state = BETA * left_old + (1.0 - BETA) * gram_left
    left_fixed = left_state / denominator(left_counts)
    right_state = BETA * right_old + (1.0 - BETA) * state["right"][None]
    right_fixed = right_state / denominator(right_counts)[:, None, None]
    return (left_state, left_fixed, right_state, right_fixed)


GROUP = 64


def encode(values):
    rows, wide = values.shape
    grouped = values.reshape(rows // GROUP, GROUP, wide)
    most = jnp.maximum(jnp.max(jnp.abs(grouped), axis=1), 1e-34)
    level = jnp.ceil(jnp.log2(most) * 256.0)
    inverse = 32767.0 * jnp.exp2(level * (-1.0 / 256.0))
    coded = jnp.clip(jnp.round(grouped * inverse[:, None, :]), -32767.0, 32767.0)
    extra = -(-(rows // GROUP) // 16) * 16
    levels = jnp.pad(level, ((0, extra - rows // GROUP), (0, 0)))
    return jnp.concatenate(
        [coded.reshape(rows, wide).astype(jnp.int16), levels.astype(jnp.int16)], 0
    )


def decode(coded, rows):
    wide = coded.shape[1]
    level = coded[rows : rows + rows // GROUP].astype(jnp.float32)
    step = jnp.exp2(level * (1.0 / 256.0)) * (1.0 / 32767.0)
    grouped = coded[:rows].astype(jnp.float32).reshape(rows // GROUP, GROUP, wide)
    return (grouped * step[:, None, :]).reshape(rows, wide)


def dot(a, b, a_dim, b_dim):
    return lax.dot_general(
        a, b, (((a_dim,), (b_dim,)), ((), ())), preferred_element_type=jnp.float32
    )


AXES = ("row", "col")
CHIPS = [(z, y) for z in range(4) for y in range(2)]


def at(z, y, c):
    return (z * 2 + y) * 2 + c


MIDDLE = ((1, 0), (2, 3))


def moves(rule):
    pairs = []
    for z, y in CHIPS:
        for c in range(2):
            dest = rule(z, y, c)
            if dest is not None:
                pairs.append((at(z, y, c), at(*dest)))
    return pairs


def middle_planes(gradient, left_old, right_old, left_counts, right_counts):
    tile_rows, half_wide = gradient.shape
    chunk = half_wide // 4
    strip = half_wide // 8
    my_row = lax.axis_index("row")
    c = lax.axis_index("col")
    z, y = my_row // 2, my_row % 2
    side = (z >= 2).astype(jnp.int32)
    own, mate, near, far = 1 + side, 3 * side, 2 - side, 3 - 3 * side
    straight = c == y

    def send(value, rule):
        return lax.ppermute(value, AXES, moves(rule))

    def swap_rule(z, y, c):
        return (z, c, y) if c != y else None

    def inward(same):
        return lambda z, y, c: ({0: 1, 3: 2}[z], y, c) if z in (0, 3) and (c == y) == same else None

    def across(same):
        return lambda z, y, c: (3 - z, y, c) if z in (1, 2) and (same is None or (c == y) == same) else None

    def beside(z, y, c):
        return (z, y, 1 - c)

    def other_y(z, y, c):
        return (z, 1 - y, c) if z in (1, 2) else None

    swapped = send(gradient, swap_rule)
    mate_a = send(gradient, inward(True))
    near_a = send(gradient, across(True))
    mine = jnp.where(straight, gradient, swapped)
    mate_b = send(mine, inward(False))
    near_b = send(mine, across(False))
    mine_o = send(mine, beside)
    mates = jnp.where(straight, mate_a, mate_b)
    nears = jnp.where(straight, near_a, near_b)

    orders = (far, near, own, mate)
    chunks = []
    for plane in orders:
        part = lax.dynamic_slice_in_dim(mates, plane * chunk, chunk, 1)
        chunks.append(send(part, across(None)))
    mates_o = send(mates, beside)
    nears_o = send(nears, beside)
    held = jnp.concatenate([mine, mine_o, mates, mates_o, nears, nears_o], 0)
    plane_rows = 2 * tile_rows
    lefts = lax.dynamic_slice_in_dim(held, c * plane_rows, plane_rows, 0)
    kept_at = jnp.where(straight, 0, tile_rows)
    sent_at = tile_rows - kept_at

    def exchange(product):
        kept = lax.dynamic_slice_in_dim(product, kept_at, tile_rows, 0)
        gone = lax.dynamic_slice_in_dim(product, sent_at, tile_rows, 0)
        return kept, send(encode(gone), other_y)

    def finish_left(kept, coded, name):
        total = kept + decode(coded, tile_rows)
        total = jnp.where(
            c == 0, total, jnp.concatenate([total[:, tile_rows:], total[:, :tile_rows]], 1)
        )

        def rule(z, y, c):
            if z not in (1, 2):
                return None
            plane = {"own": z, "mate": {1: 0, 2: 3}[z], "near": 3 - z, "far": {1: 3, 2: 0}[z]}[name]
            half = plane // 2
            return (z, y, half) if c == 0 else ({1: 0, 2: 3}[z], y, half)

        return send(encode(total), rule)

    halves = {}
    for index, name in enumerate(("own", "mate", "near")):
        rows = held[index * plane_rows : (index + 1) * plane_rows]
        halves[name] = exchange(dot(lefts, rows, 1, 1))

    target = jnp.where(c == 0, own, mate)
    strips = lax.dynamic_slice_in_dim(held, target * chunk, chunk, 1)
    bases = [
        dot(strips, lax.dynamic_slice_in_dim(held, plane * chunk, chunk, 1), 0, 0)
        for plane in (mate, own, near, far)
    ]

    def same_rule(z, y, c):
        if z not in (1, 2):
            return None
        return (z, y, y) if c == 0 else ({1: 0, 2: 3}[z], y, y)

    def cross_rule(z, y, c):
        if z not in (1, 2):
            return None
        return (z, 1 - y, y) if c == 0 else ({1: 0, 2: 3}[z], 1 - y, y)

    def finish_right(value):
        same = lax.dynamic_slice_in_dim(value, y * strip, strip, 0)
        cross = lax.dynamic_slice_in_dim(value, (1 - y) * strip, strip, 0)
        same = send(encode(same), same_rule)
        cross = send(encode(cross), cross_rule)
        return jnp.where(straight, same, cross)

    lefts_out = {}
    rights = []
    far_rows = []
    far_product = None
    names = ["own", "mate", "near"]
    for index, plane in enumerate((mate, own, near, far)):
        part = jnp.concatenate([chunks[index], send(chunks[index], beside)], 0)
        far_rows.append(part)
        piece = lax.dynamic_slice_in_dim(lefts, plane * chunk, chunk, 1)
        term = dot(piece, part, 1, 1)
        far_product = term if far_product is None else far_product + term
        if index == 1:
            far_strips = jnp.where(c == 0, far_rows[1], far_rows[0])
            rights.append(finish_right(bases[0] + dot(far_strips, far_rows[0], 0, 0)))
        if index >= 1:
            rights.append(finish_right(bases[index] + dot(far_strips, part, 0, 0)))
            name = names[index - 1]
            lefts_out[name] = finish_left(*halves[name], name)
    halves["far"] = exchange(far_product)
    lefts_out["far"] = finish_left(*halves["far"], "far")

    same_half = c == side
    first = jnp.where(same_half, lefts_out["own"], lefts_out["near"])
    second = jnp.where(same_half, lefts_out["mate"], lefts_out["far"])
    first, second = decode(first, tile_rows), decode(second, tile_rows)
    ahead = c == 0
    gram_left = jnp.concatenate(
        [jnp.where(ahead, second, first), jnp.where(ahead, first, second)], 1
    )
    gram_right = jnp.concatenate(
        [
            decode(jnp.where(side == 0, rights[index], rights[3 - index]), strip)
            for index in range(4)
        ],
        1,
    )
    left_state = BETA * left_old + (1.0 - BETA) * gram_left
    left_fixed = left_state / denominator(left_counts)
    right_state = BETA * right_old + (1.0 - BETA) * gram_right[None]
    right_fixed = right_state / denominator(right_counts)[:, None, None]
    return (left_state, left_fixed, right_state, right_fixed)


def solution(mesh):
    local = middle_planes if mesh.shape["row"] == 8 else ring
    return jax.shard_map(
        local,
        mesh=mesh,
        in_specs=(
            P(("groups", "row"), "col"),
            P(("groups", "row"), "col"),
            P(("groups", "col"), "row", None),
            P(("groups", "row"), "col"),
            P(("groups", "col")),
        ),
        out_specs=(
            P(("groups", "row"), "col"),
            P(("groups", "row"), "col"),
            P(("groups", "col"), "row", None),
            P(("groups", "col"), "row", None),
        ),
        check_vma=False,
    )
```

```python
import jax
import jax.numpy as jnp
from jax import lax
from jax.experimental import pallas as pl
from jax.experimental.pallas import tpu as pltpu
from jax.sharding import PartitionSpec as P

BETA = 0.9


def denominator(counters):
    decay_power = jnp.power(jnp.float32(BETA), (counters + 1).astype(jnp.float32))
    return 1.0 - decay_power


def ring_order(count):
    if count == 8:
        return [0, 2, 4, 6, 7, 5, 3, 1]
    return list(range(count))


def ring(gradient, left_old, right_old, left_counts, right_counts):
    tile_rows, half_wide = gradient.shape
    count = lax.axis_size("row")
    strip_wide = half_wide // count
    order = ring_order(count)
    place = {row: at for at, row in enumerate(order)}
    my_row = lax.axis_index("row")
    my_col = lax.axis_index("col")
    up = [(order[at], order[(at + 1) % count]) for at in range(count)]
    down = [(dest, source) for source, dest in up]
    piece = tile_rows // 2
    strip_at = my_row * strip_wide

    state = {"left": jnp.zeros((tile_rows, count * tile_rows), jnp.float32), "right": None}

    def consume(part, step, offset):
        sources = [order[(place[row] - step) % count] for row in range(count)]
        source = jnp.asarray(sources, jnp.int32)[my_row]
        product = lax.dot_general(
            gradient, part, (((1,), (1,)), ((), ())), preferred_element_type=jnp.float32
        )
        pairs = []
        for row in range(count):
            keeper = sources[row] * 2 // count
            pairs.append((row * 2 + 1 - keeper, row * 2 + keeper))
        other = lax.ppermute(product, ("row", "col"), pairs)
        state["left"] = lax.dynamic_update_slice(
            state["left"], product + other, (0, source * tile_rows + offset)
        )
        strip = lax.dynamic_slice_in_dim(part, strip_at, strip_wide, 1)
        term = lax.dot_general(
            strip, part, (((0,), (0,)), ((), ())), preferred_element_type=jnp.float32
        )
        state["right"] = term if state["right"] is None else state["right"] + term

    halves = [gradient[:piece], gradient[piece:]]
    going_up = list(halves)
    going_down = list(halves)
    last = count // 2
    for step in range(1, last + 1):
        if step < last:
            going_up = [lax.ppermute(part, "row", up) for part in going_up]
            going_down = [lax.ppermute(part, "row", down) for part in going_down]
        else:
            going_up = [lax.ppermute(going_up[0], "row", up)]
            going_down = [lax.ppermute(going_down[1], "row", down)]
        if step == 1:
            consume(halves[0], 0, 0)
            consume(halves[1], 0, piece)
        if step < last:
            for at in range(2):
                consume(going_up[at], step, at * piece)
                consume(going_down[at], -step, at * piece)
        else:
            consume(going_up[0], step, 0)
            consume(going_down[0], step, piece)

    width = count * tile_rows // 2
    gram_left = lax.dynamic_slice_in_dim(state["left"], my_col * width, width, 1)
    left_state = BETA * left_old + (1.0 - BETA) * gram_left
    left_fixed = left_state / denominator(left_counts)
    right_state = BETA * right_old + (1.0 - BETA) * state["right"][None]
    right_fixed = right_state / denominator(right_counts)[:, None, None]
    return (left_state, left_fixed, right_state, right_fixed)


GROUP = 64
LEVELS = 16


def pack(values, out_ref, at, level_at):
    rows = values.shape[0]
    levels = []
    for first in range(0, rows, GROUP):
        block = values[first : first + GROUP]
        most = jnp.maximum(jnp.max(jnp.abs(block), axis=0, keepdims=True), 1e-34)
        level = jnp.ceil(jnp.log2(most) * 256.0)
        inverse = 32767.0 * jnp.exp2(level * (-1.0 / 256.0))
        coded = jnp.clip(jnp.round(block * inverse), -32767.0, 32767.0)
        out_ref[at + first : at + first + GROUP] = coded.astype(jnp.int32).astype(jnp.int16)
        levels.append(level)
    return levels


def put_levels(levels, out_ref, at):
    levels = levels + [jnp.zeros_like(levels[0])] * (LEVELS - len(levels))
    out_ref[at : at + LEVELS] = jnp.concatenate(levels, 0).astype(jnp.int32).astype(jnp.int16)


def unpack(ref, at, rows, level_at):
    wide = ref.shape[1]
    level = ref[level_at : level_at + LEVELS].astype(jnp.int32).astype(jnp.float32)
    step = jnp.exp2(level * (1.0 / 256.0)) * (1.0 / 32767.0)
    parts = []
    for index in range(rows // GROUP):
        block = ref[at + index * GROUP : at + (index + 1) * GROUP]
        parts.append(block.astype(jnp.int32).astype(jnp.float32) * step[index : index + 1])
    return jnp.concatenate(parts, 0)


def decode(coded, rows):
    wide = coded.shape[1]
    level = coded[rows : rows + rows // GROUP].astype(jnp.float32)
    step = jnp.exp2(level * (1.0 / 256.0)) * (1.0 / 32767.0)
    grouped = coded[:rows].astype(jnp.float32).reshape(rows // GROUP, GROUP, wide)
    return (grouped * step[:, None, :]).reshape(rows, wide)


PARAMS = pltpu.CompilerParams(vmem_limit_bytes=40 * 2**20)
WHOLE = pl.BlockSpec(memory_space=pltpu.VMEM)
SCALAR = pl.BlockSpec(memory_space=pltpu.SMEM)


def kernel_call(body, flags, arrays, outs):
    size = sum(a.size * a.dtype.itemsize for a in arrays) + sum(
        s[0] * s[1] * jnp.dtype(d).itemsize for s, d in outs
    )
    return pl.pallas_call(
        body,
        in_specs=[SCALAR] + [WHOLE] * len(arrays),
        out_specs=[WHOLE] * len(outs),
        out_shape=[jax.ShapeDtypeStruct(s, d) for s, d in outs],
        compiler_params=PARAMS,
        cost_estimate=pl.CostEstimate(flops=0, bytes_accessed=size, transcendentals=0),
    )(flags, *arrays)


def pick(flag, size):
    return pl.multiple_of(flag * size, 64)


def give_away(flags, products):
    rows, wide = products[0].shape[0] // 2, products[0].shape[1]

    def body(flag_ref, *refs):
        out_ref = refs[-1]
        gone = 1 - flag_ref[0]
        levels = []
        for index, ref in enumerate(refs[:-1]):
            part = ref[pl.ds(pick(gone, rows), rows), :]
            levels += pack(part, out_ref, index * rows, None)
        put_levels(levels, out_ref, len(products) * rows)

    return kernel_call(body, flags, products, [((len(products) * rows + LEVELS, wide), jnp.int16)])[0]


def add_up(flags, products, coded):
    rows, wide = products[0].shape[0] // 2, products[0].shape[1]
    many = len(products)

    def body(flag_ref, *refs):
        coded_ref, outs = refs[many], refs[many + 1 :]
        totals = []
        for index in range(many):
            kept = refs[index][pl.ds(pick(flag_ref[0], rows), rows), :]
            got = unpack_at(coded_ref, index, rows, many)
            totals.append(kept + got)
        for index in range(many):
            put_levels(pack(totals[index], outs[index], 0, None), outs[index], rows)
        if many == 2:
            first = jnp.where(flag_ref[1] == 1, totals[1], totals[0])
            put_levels(pack(first, outs[2], 0, None), outs[2], rows)

    def unpack_at(ref, index, rows, many):
        level = ref[many * rows : many * rows + LEVELS].astype(jnp.int32).astype(jnp.float32)
        step = jnp.exp2(level * (1.0 / 256.0)) * (1.0 / 32767.0)
        parts = []
        for group in range(rows // GROUP):
            at = index * rows + group * GROUP
            row = index * (rows // GROUP) + group
            block = ref[at : at + GROUP].astype(jnp.int32).astype(jnp.float32)
            parts.append(block * step[row : row + 1])
        return jnp.concatenate(parts, 0)

    shape = ((rows + LEVELS, wide), jnp.int16)
    return kernel_call(body, flags, list(products) + [coded], [shape] * (many + (many == 2)))


def code_strips(flags, value):
    rows, wide = value.shape[0] // 2, value.shape[1]

    def body(flag_ref, ref, first_ref, second_ref):
        for out_ref, which in ((first_ref, flag_ref[2]), (second_ref, 1 - flag_ref[2])):
            part = ref[pl.ds(pick(which, rows), rows), :]
            put_levels(pack(part, out_ref, 0, None), out_ref, rows)

    return kernel_call(body, flags, [value], [((rows + LEVELS, wide), jnp.int16)] * 2)


def dot(a, b, a_dim, b_dim):
    return lax.dot_general(
        a, b, (((a_dim,), (b_dim,)), ((), ())), preferred_element_type=jnp.float32
    )


AXES = ("row", "col")
CHIPS = [(z, y) for z in range(4) for y in range(2)]
END_OF = {1: 0, 2: 3}


def at(z, y, c):
    return (z * 2 + y) * 2 + c


def send(value, rule):
    pairs = []
    for z, y in CHIPS:
        for c in range(2):
            dest = rule(z, y, c)
            if dest is not None:
                pairs.append((at(z, y, c), at(*dest)))
    return lax.ppermute(value, AXES, pairs)


def middle(z):
    return z in (1, 2)


def to_line(z, y, c):
    return (z, c, y)


def inward(z, y, c):
    return None if middle(z) else ({0: 1, 3: 2}[z], c, y)


def across(z, y, c):
    return (3 - z, c, y) if middle(z) else None


def far_across(z, y, c):
    return None if middle(z) else ({0: 2, 3: 1}[z], c, y)


def beside(z, y, c):
    return (z, y, 1 - c)


def other_y(z, y, c):
    return (z, 1 - y, c)


def other_y_middle(z, y, c):
    return (z, 1 - y, c) if middle(z) else None


def half_own(z, y, c):
    return (z, y, z // 2) if c != z // 2 else None


def left_first(near_side):
    def rule(z, y, c):
        if not middle(z):
            return None
        half = z // 2 if near_side else 1 - z // 2
        return (END_OF[z], y, half) if c == half else (z, y, half)

    return rule


def left_second(near_side):
    def rule(z, y, c):
        if not middle(z):
            return None
        half = z // 2 if near_side else 1 - z // 2
        return None if c == half else (END_OF[z], y, half)

    return rule


def right_first(z, y, c):
    if not middle(z):
        return None
    return (z, 1 - y, y) if c == 0 else (END_OF[z], y, y)


def right_second(z, y, c):
    if not middle(z):
        return None
    return (z, y, y) if c == 0 else (END_OF[z], 1 - y, y)


def middle_planes(gradient, left_old, right_old, left_counts, right_counts):
    tile_rows, half_wide = gradient.shape
    chunk = half_wide // 4
    strip = half_wide // 8
    my_row = lax.axis_index("row")
    c = lax.axis_index("col")
    z, y = my_row // 2, my_row % 2
    side = (z >= 2).astype(jnp.int32)
    is_middle = (z == 1) | (z == 2)
    own, mate, near, far = 1 + side, 3 * side, 2 - side, 3 - 3 * side
    straight = c == y
    kept = jnp.where(straight, 0, 1)
    first_strip = jnp.where(c == 0, 1 - y, y)
    flags_near = jnp.stack([kept, (c == side).astype(jnp.int32), first_strip]).astype(jnp.int32)
    flags_far = jnp.stack([kept, (c != side).astype(jnp.int32), first_strip]).astype(jnp.int32)

    clock = [None]

    def gate(*values):
        if clock[0] is None:
            return values if len(values) > 1 else values[0]
        out = lax.optimization_barrier(tuple(values) + (clock[0],))[:-1]
        return out if len(values) > 1 else out[0]

    def mark(value):
        clock[0] = value

    def columns(value, plane):
        return lax.dynamic_slice_in_dim(value, plane * chunk, chunk, 1)

    nears = send(gradient, across)
    mates = send(gradient, inward)
    mine = send(gradient, to_line)
    far_end = 3 * (1 - side)
    order_out = (far_end, jnp.where(side == 0, 2, 1), jnp.where(side == 0, 1, 2), 3 * side)
    parts_out = [columns(gradient, plane) for plane in order_out]
    order_in = (mate, own, near, far)

    mine_o = send(mine, beside)
    own_rows = jnp.concatenate([mine, mine_o], 0)
    self_product = dot(own_rows, mine, 1, 1)
    self_coded = give_away(flags_near, [self_product])
    self_got = send(self_coded, other_y)
    mark(self_coded)
    target = jnp.where(c == 0, own, mate)
    own_g = gate(own_rows)
    strips_own = lax.optimization_barrier(columns(own_g, target).T)
    base = dot(strips_own, own_g, 1, 0)
    mark(base)

    fars = [None] * 4
    fars[0] = send(gate(parts_out[0]), far_across)
    mates, nears = gate(mates, nears)
    mates_o = send(mates, beside)
    nears_o = send(nears, beside)
    fars[1] = send(lax.optimization_barrier((parts_out[1], nears))[0], far_across)
    beyond = jnp.concatenate([mates, mates_o, nears, nears_o], 0)
    mate_rows = beyond[: 2 * tile_rows]
    near_products = [dot(own_rows, mates, 1, 1), dot(mate_rows, mine, 1, 1)]
    near_coded = give_away(flags_near, near_products)
    near_got = send(near_coded, other_y_middle)
    mark(near_coded)
    fars[2] = send(gate(parts_out[2]), far_across)
    own_g, mate_g, nears_g, self_got = gate(own_rows, mate_rows, nears, self_got)
    next_products = [dot(own_g, nears_g, 1, 1), dot(mate_g, nears_g, 1, 1)]
    next_coded = give_away(flags_far, next_products)
    next_got = send(next_coded, other_y_middle)
    self_sum = add_up(flags_near, [self_product], self_got)[0]
    self_other = send(self_sum, half_own)
    mark(next_coded)
    fars[3] = send(gate(parts_out[3]), far_across)
    beyond_g = gate(beyond)
    strips_beyond = lax.optimization_barrier(columns(beyond_g, target).T)
    base = base + dot(strips_beyond, beyond_g, 1, 0)
    mark(base)

    rights = []

    def finish_right(value):
        first, second = code_strips(flags_near, value)
        mark(first)
        first = send(first, right_first)
        second = send(second, right_second)
        rights.append(jnp.where(is_middle == straight, second, first))

    def far_terms(index, part):
        own_g, mate_g = gate(own_rows, mate_rows)
        plane = order_in[index]
        return [
            dot(columns(own_g, plane), part, 1, 1),
            dot(columns(mate_g, plane), part, 1, 1),
        ]

    parts = [None] * 4
    parts[0], near_got = gate(fars[0], near_got)
    far_products = far_terms(0, parts[0])
    others = [None] * 4
    others[0] = send(parts[0], beside)
    near_sums = add_up(flags_near, near_products, near_got)
    near_first = send(near_sums[2], left_first(True))
    near_second = send(near_sums[1], left_second(True))
    mark(near_sums[0])

    parts[1] = gate(fars[1])
    others[1] = send(parts[1], beside)
    far_products = [a + b for a, b in zip(far_products, far_terms(1, parts[1]))]
    mark(far_products[0])
    full = [gate(jnp.concatenate([parts[index], others[index]], 0)) for index in range(2)]
    strips_far = lax.optimization_barrier(jnp.where(c == 0, full[1], full[0]).T)
    finish_right(columns(base, order_in[0]) + dot(strips_far, full[0], 1, 0))
    finish_right(columns(base, order_in[1]) + dot(strips_far, full[1], 1, 0))

    parts[2], next_got = gate(fars[2], next_got)
    others[2] = send(parts[2], beside)
    next_sums = add_up(flags_far, next_products, next_got)
    next_first = send(next_sums[2], left_first(False))
    next_second = send(next_sums[1], left_second(False))
    far_products = [a + b for a, b in zip(far_products, far_terms(2, parts[2]))]
    mark(far_products[0])
    full_2 = gate(jnp.concatenate([parts[2], others[2]], 0))
    finish_right(columns(base, order_in[2]) + dot(strips_far, full_2, 1, 0))

    parts[3] = gate(fars[3])
    others[3] = send(parts[3], beside)
    far_products = [a + b for a, b in zip(far_products, far_terms(3, parts[3]))]
    far_coded = give_away(flags_far, far_products)
    far_got = send(far_coded, other_y_middle)
    mark(far_coded)
    full_3 = gate(jnp.concatenate([parts[3], others[3]], 0))
    finish_right(columns(base, order_in[3]) + dot(strips_far, full_3, 1, 0))
    far_got = gate(far_got)
    far_sums = add_up(flags_far, far_products, far_got)
    far_first = send(far_sums[2], left_first(False))
    far_second = send(far_sums[1], left_second(False))
    mark(far_sums[0])

    gram_right = jnp.concatenate(
        [
            decode(jnp.where(side == 0, rights[index], rights[3 - index]), strip)
            for index in range(4)
        ],
        1,
    )
    right_old, gram_right = gate(right_old, gram_right)
    right_state = BETA * right_old + (1.0 - BETA) * gram_right[None]
    right_fixed = right_state / denominator(right_counts)[:, None, None]

    same_half = c == side
    self_block = (self_sum, self_other)
    near_block = (
        jnp.where(is_middle, near_sums[0], near_first),
        jnp.where(is_middle, near_first, near_second),
    )
    next_block = (
        jnp.where(is_middle, next_sums[0], next_first),
        jnp.where(is_middle, next_first, next_second),
    )
    far_block = (
        jnp.where(is_middle, far_sums[0], far_first),
        jnp.where(is_middle, far_first, far_second),
    )
    inner, outer = [], []
    for index in range(2):
        home_inner = jnp.where(is_middle, self_block[index], near_block[index])
        home_outer = jnp.where(is_middle, near_block[index], self_block[index])
        inner.append(decode(jnp.where(same_half, home_inner, next_block[index]), tile_rows))
        outer.append(decode(jnp.where(same_half, home_outer, far_block[index]), tile_rows))
    inner = [jnp.where(c == 0, inner[0], inner[1]), jnp.where(c == 0, inner[1], inner[0])]
    outer = [jnp.where(c == 0, outer[0], outer[1]), jnp.where(c == 0, outer[1], outer[0])]
    ahead = c == 0
    gram_left = jnp.concatenate(
        [jnp.where(ahead, outer[i], inner[i]) for i in range(2)]
        + [jnp.where(ahead, inner[i], outer[i]) for i in range(2)],
        1,
    )
    left_state = BETA * left_old + (1.0 - BETA) * gram_left
    left_fixed = left_state / denominator(left_counts)
    return (left_state, left_fixed, right_state, right_fixed)


def solution(mesh):
    local = middle_planes if mesh.shape["row"] == 8 else ring
    return jax.shard_map(
        local,
        mesh=mesh,
        in_specs=(
            P(("groups", "row"), "col"),
            P(("groups", "row"), "col"),
            P(("groups", "col"), "row", None),
            P(("groups", "row"), "col"),
            P(("groups", "col")),
        ),
        out_specs=(
            P(("groups", "row"), "col"),
            P(("groups", "row"), "col"),
            P(("groups", "col"), "row", None),
            P(("groups", "col"), "row", None),
        ),
        check_vma=False,
    )
```

```python
import math

import jax
import jax.numpy as jnp
from jax import lax
from jax.experimental import pallas as pl
from jax.experimental.pallas import tpu as pltpu
from jax.sharding import PartitionSpec as P

BETA = 0.9


def denominator(counters):
    decay_power = jnp.power(jnp.float32(BETA), (counters + 1).astype(jnp.float32))
    return 1.0 - decay_power


def ring_order(count):
    if count == 8:
        return [0, 2, 4, 6, 7, 5, 3, 1]
    return list(range(count))


def ring(gradient, left_old, right_old, left_counts, right_counts):
    tile_rows, half_wide = gradient.shape
    count = lax.axis_size("row")
    strip_wide = half_wide // count
    order = ring_order(count)
    place = {row: at for at, row in enumerate(order)}
    my_row = lax.axis_index("row")
    my_col = lax.axis_index("col")
    up = [(order[at], order[(at + 1) % count]) for at in range(count)]
    down = [(dest, source) for source, dest in up]
    piece = tile_rows // 2
    strip_at = my_row * strip_wide

    state = {"left": jnp.zeros((tile_rows, count * tile_rows), jnp.float32), "right": None}

    def consume(part, step, offset):
        sources = [order[(place[row] - step) % count] for row in range(count)]
        source = jnp.asarray(sources, jnp.int32)[my_row]
        product = lax.dot_general(
            gradient, part, (((1,), (1,)), ((), ())), preferred_element_type=jnp.float32
        )
        pairs = []
        for row in range(count):
            keeper = sources[row] * 2 // count
            pairs.append((row * 2 + 1 - keeper, row * 2 + keeper))
        other = lax.ppermute(product, ("row", "col"), pairs)
        state["left"] = lax.dynamic_update_slice(
            state["left"], product + other, (0, source * tile_rows + offset)
        )
        strip = lax.dynamic_slice_in_dim(part, strip_at, strip_wide, 1)
        term = lax.dot_general(
            strip, part, (((0,), (0,)), ((), ())), preferred_element_type=jnp.float32
        )
        state["right"] = term if state["right"] is None else state["right"] + term

    halves = [gradient[:piece], gradient[piece:]]
    going_up = list(halves)
    going_down = list(halves)
    last = count // 2
    for step in range(1, last + 1):
        if step < last:
            going_up = [lax.ppermute(part, "row", up) for part in going_up]
            going_down = [lax.ppermute(part, "row", down) for part in going_down]
        else:
            going_up = [lax.ppermute(going_up[0], "row", up)]
            going_down = [lax.ppermute(going_down[1], "row", down)]
        if step == 1:
            consume(halves[0], 0, 0)
            consume(halves[1], 0, piece)
        if step < last:
            for at in range(2):
                consume(going_up[at], step, at * piece)
                consume(going_down[at], -step, at * piece)
        else:
            consume(going_up[0], step, 0)
            consume(going_down[0], step, piece)

    width = count * tile_rows // 2
    gram_left = lax.dynamic_slice_in_dim(state["left"], my_col * width, width, 1)
    left_state = BETA * left_old + (1.0 - BETA) * gram_left
    left_fixed = left_state / denominator(left_counts)
    right_state = BETA * right_old + (1.0 - BETA) * state["right"][None]
    right_fixed = right_state / denominator(right_counts)[:, None, None]
    return (left_state, left_fixed, right_state, right_fixed)


GROUP = 64
LEVELS = 16


def pack(values, out_ref, at):
    levels = []
    for first in range(0, values.shape[0], GROUP):
        block = values[first : first + GROUP]
        most = jnp.maximum(jnp.max(jnp.abs(block), axis=0, keepdims=True), 1e-34)
        level = jnp.ceil(jnp.log2(most) * 256.0)
        inverse = 32767.0 * jnp.exp2(level * (-1.0 / 256.0))
        coded = jnp.clip(jnp.round(block * inverse), -32767.0, 32767.0)
        out_ref[at + first : at + first + GROUP] = coded.astype(jnp.int32).astype(jnp.int16)
        levels.append(level)
    return levels


def put_levels(levels, out_ref, at):
    levels = levels + [jnp.zeros_like(levels[0])] * (LEVELS - len(levels))
    out_ref[at : at + LEVELS] = jnp.concatenate(levels, 0).astype(jnp.int32).astype(jnp.int16)


def unpack(ref, index, rows, many):
    level = ref[many * rows : many * rows + LEVELS].astype(jnp.int32).astype(jnp.float32)
    step = jnp.exp2(level * (1.0 / 256.0)) * (1.0 / 32767.0)
    parts = []
    for group in range(rows // GROUP):
        at = index * rows + group * GROUP
        row = index * (rows // GROUP) + group
        block = ref[at : at + GROUP].astype(jnp.int32).astype(jnp.float32)
        parts.append(block * step[row : row + 1])
    return jnp.concatenate(parts, 0)


def decode(coded, rows):
    wide = coded.shape[1]
    level = coded[rows : rows + rows // GROUP].astype(jnp.float32)
    step = jnp.exp2(level * (1.0 / 256.0)) * (1.0 / 32767.0)
    grouped = coded[:rows].astype(jnp.float32).reshape(rows // GROUP, GROUP, wide)
    return (grouped * step[:, None, :]).reshape(rows, wide)


PARAMS = pltpu.CompilerParams(vmem_limit_bytes=48 * 2**20)
FREE = pl.CostEstimate(flops=1, bytes_accessed=1, transcendentals=0)
WHOLE = pl.BlockSpec(memory_space=pltpu.VMEM)
SCALAR = pl.BlockSpec(memory_space=pltpu.SMEM)


def kernel_call(body, flags, arrays, outs):
    return pl.pallas_call(
        body,
        in_specs=[SCALAR] + [WHOLE] * len(arrays),
        out_specs=[WHOLE] * len(outs),
        out_shape=[jax.ShapeDtypeStruct(s, d) for s, d in outs],
        compiler_params=PARAMS,
        cost_estimate=FREE,
    )(flags, *arrays)


def pick(flag, size):
    return pl.multiple_of(flag * size, GROUP)


def left_terms(flags, rows, slots, before=None, last=True):
    many, pieces = len(slots), len(rows)
    tall, wide = rows[0][0].shape
    block = math.gcd(wide, 896)
    size = 2 * tall

    def body(flag_ref, *refs):
        rows_in, refs = refs[: 2 * pieces], refs[2 * pieces :]
        slots_in, refs = refs[: many * pieces], refs[many * pieces :]
        if before is not None:
            before_in, refs = refs[:many], refs[many:]
        outs = refs[:many]
        step = pl.program_id(0)

        @pl.when(step == 0)
        def _():
            for index in range(many):
                outs[index][...] = jnp.zeros_like(outs[index]) if before is None else before_in[index][...]

        for index in range(many):
            for piece in range(pieces):
                for half in range(2):
                    outs[index][half * tall : (half + 1) * tall] += dot(
                        rows_in[2 * piece + half][...], slots_in[index * pieces + piece][...], 1, 1
                    )

        if last:

            @pl.when(step == pl.num_programs(0) - 1)
            def _():
                gone = 1 - flag_ref[0]
                levels = []
                for index in range(many):
                    part = outs[index][pl.ds(pick(gone, tall), tall), :]
                    levels += pack(part, refs[many], index * tall)
                put_levels(levels, refs[many], many * tall)

    moving = pl.BlockSpec((tall, block), lambda k: (0, k))
    still = pl.BlockSpec((size, tall), lambda k: (0, 0))
    arrays = [a for pair in rows for a in pair] + [b for slot in slots for b in slot]
    specs = [SCALAR] + [moving] * len(arrays)
    if before is not None:
        arrays += before
        specs += [still] * many
    out_shape = [jax.ShapeDtypeStruct((size, tall), jnp.float32)] * many
    out_specs = [still] * many
    if last:
        out_shape.append(jax.ShapeDtypeStruct((many * tall + LEVELS, tall), jnp.int16))
        out_specs.append(pl.BlockSpec((many * tall + LEVELS, tall), lambda k: (0, 0)))
    return pl.pallas_call(
        body,
        grid=(wide // block,),
        in_specs=specs,
        out_specs=out_specs,
        out_shape=out_shape,
        compiler_params=PARAMS,
        cost_estimate=FREE,
    )(flags, *arrays)


def right_terms(terms, before=None, last=False):
    wide = terms[0][1].shape[1]
    strip = terms[0][0].shape[1]
    block = math.gcd(wide, 896)

    def body(*refs):
        total = None if before is None else refs[2 * len(terms)][...]
        for index in range(len(terms)):
            term = dot(refs[2 * index][...], refs[2 * index + 1][...], 0, 0)
            total = term if total is None else total + term
        outs = refs[2 * len(terms) + (before is not None) :]
        outs[0][...] = total
        if last:
            put_levels(pack(total, outs[1], 0), outs[1], strip)

    specs = []
    arrays = []
    for strips, columns in terms:
        arrays += [strips, columns]
        specs += [
            pl.BlockSpec(strips.shape, lambda k: (0, 0)),
            pl.BlockSpec((columns.shape[0], block), lambda k: (0, k)),
        ]
    out = pl.BlockSpec((strip, block), lambda k: (0, k))
    if before is not None:
        arrays.append(before)
        specs.append(out)
    out_shape = [jax.ShapeDtypeStruct((strip, wide), jnp.float32)]
    out_specs = [out]
    if last:
        out_shape.append(jax.ShapeDtypeStruct((strip + LEVELS, wide), jnp.int16))
        out_specs.append(pl.BlockSpec((strip + LEVELS, block), lambda k: (0, k)))
    return pl.pallas_call(
        body,
        grid=(wide // block,),
        in_specs=specs,
        out_specs=out_specs,
        out_shape=out_shape,
        compiler_params=PARAMS,
        cost_estimate=FREE,
    )(*arrays)


def add_up(flags, products, coded):
    rows, wide = products[0].shape[0] // 2, products[0].shape[1]
    many = len(products)

    def body(flag_ref, *refs):
        coded_ref, total_ref, out_ref = refs[many:]
        levels = []
        for index in range(many):
            kept = refs[index][pl.ds(pick(flag_ref[0], rows), rows), :]
            total = kept + unpack(coded_ref, index, rows, many)
            total_ref[index * rows : (index + 1) * rows] = total
            levels += pack(total, out_ref, index * rows)
        put_levels(levels, out_ref, many * rows)

    outs = [((many * rows, wide), jnp.float32), ((many * rows + LEVELS, wide), jnp.int16)]
    return kernel_call(body, flags, list(products) + [coded], outs)


def dot(a, b, a_dim, b_dim):
    return lax.dot_general(
        a, b, (((a_dim,), (b_dim,)), ((), ())), preferred_element_type=jnp.float32
    )


AXES = ("row", "col")
CHIPS = [(z, y) for z in range(4) for y in range(2)]


def at(z, y, c):
    return (z * 2 + y) * 2 + c


def send(value, rule):
    pairs = []
    for z, y in CHIPS:
        for c in range(2):
            dest = rule(z, y, c)
            if dest is not None:
                pairs.append((at(z, y, c), at(*dest)))
    return lax.ppermute(value, AXES, pairs)


def middle(z):
    return z in (1, 2)


def to_line(z, y, c):
    return (z, c, y) if c != y else None


def pair_line(z, y, c):
    return (z ^ 1, c, y)


def across_line(z, y, c):
    return (3 - z, c, y) if middle(z) else None


def across(z, y, c):
    return (3 - z, y, c) if middle(z) else None


def outward(z, y, c):
    return (z ^ 1, y, c) if middle(z) else None


def beside(z, y, c):
    return (z, y, 1 - c)


def other_y(z, y, c):
    return (z, 1 - y, c)


def to_home(z, y, c):
    return (z, y, 1 - c) if c != z // 2 else None


def to_away(z, y, c):
    return (z, y, 1 - c) if c == z // 2 else None


def line_gather(gradient, left_old, right_old, left_counts, right_counts):
    tile_rows, half_wide = gradient.shape
    wide = half_wide // 2
    chunk = half_wide // 4
    strip = half_wide // 8
    my_row = lax.axis_index("row")
    c = lax.axis_index("col")
    z, y = my_row // 2, my_row % 2
    side = (z >= 2).astype(jnp.int32)
    is_middle = (z == 1) | (z == 2)
    straight = c == y
    flags = jnp.stack([jnp.where(straight, 0, 1)]).astype(jnp.int32)
    strip_at = (2 * (z - 2 * side) + c) * strip

    def tie(*values):
        return lax.optimization_barrier(tuple(values))

    def strips_of(pair):
        return [lax.dynamic_slice_in_dim(part, strip_at + side * wide, strip, 1) for part in pair]

    def half_of(value, which):
        return lax.dynamic_slice_in_dim(value, which * wide, wide, 1)

    def terms(strips, pair):
        return list(zip(strips, pair))

    mate = send(gradient, pair_line)
    cross = send(gradient, across_line)
    gradient_t, mate, cross = tie(gradient, mate, cross)
    far = send(mate, across)
    near = send(cross, outward)
    swapped = send(gradient_t, to_line)
    mates = (mate, send(mate, beside))
    [right] = right_terms(terms(strips_of(mates), mates))

    right, swapped = tie(right, swapped)
    mine = jnp.where(straight, gradient, swapped)
    own = (mine, jnp.concatenate([send(mine[:, at : at + chunk], beside) for at in range(0, half_wide, chunk)], 1))
    own_product, mate_product, same_coded = left_terms(flags, [own], [[mine], [mate]])
    same_products = [own_product, mate_product]
    same_got = send(same_coded, other_y)
    [right] = right_terms(terms(strips_of(own), own), right)
    own_home = tuple(half_of(part, side) for part in own)
    own_away = tuple(half_of(part, 1 - side) for part in own)

    right, same_coded, near, far = tie(right, same_coded, near, far)
    far_home, far_away = half_of(far, side), half_of(far, 1 - side)
    far_first, far_second = far_away[:, :chunk], far_away[:, chunk:]
    end_home = send(far_home, outward)
    near = jnp.where(is_middle, cross, near)
    nears = (near, send(near, beside))
    same_total, same_out = add_up(flags, same_products, same_got)
    same_other = send(same_out, to_home)
    near_product, near_coded = left_terms(flags, [own], [[near]])
    near_got = send(near_coded, other_y)
    far_first, far_second, near_coded, same_out = tie(far_first, far_second, near_coded, same_out)
    end_first = send(far_first, outward)
    end_second = send(far_second, outward)
    [right] = right_terms(terms(strips_of(nears), nears), right)
    right_home, right_away = half_of(right, side), half_of(right, 1 - side)

    right_home, right_away, end_home = tie(right_home, right_away, end_home)
    end_home = jnp.where(is_middle, far_home, end_home)
    ends_home = (end_home, send(end_home, beside))
    [far_product] = left_terms(flags, [own_home], [[end_home]], last=False)
    near_total, near_out = add_up(flags, [near_product], near_got)
    near_other = send(near_out, to_away)
    strips = [lax.dynamic_slice_in_dim(part, strip_at, strip, 1) for part in ends_home]
    right_home, home_coded = right_terms(terms(strips, ends_home), right_home, last=True)
    home_got = send(home_coded, to_line)

    home_coded, far_product, end_first = tie(home_coded, far_product, end_first)
    end_first = jnp.where(is_middle, far_first, end_first)
    ends_first = (end_first, send(end_first, beside))
    first_rows = tuple(part[:, :chunk] for part in own_away)
    [far_product] = left_terms(flags, [first_rows], [[end_first]], [far_product], last=False)
    right_first, first_coded = right_terms(terms(strips, ends_first), right_away[:, :chunk], last=True)
    first_got = send(first_coded, to_line)

    first_coded, far_product, end_second = tie(first_coded, far_product, end_second)
    end_second = jnp.where(is_middle, far_second, end_second)
    ends_second = (end_second, send(end_second, beside))
    second_rows = tuple(part[:, chunk:] for part in own_away)
    far_product, far_coded = left_terms(flags, [second_rows], [[end_second]], [far_product])
    far_got = send(far_coded, other_y)
    right_second, second_coded = right_terms(terms(strips, ends_second), right_away[:, chunk:], last=True)
    second_coded, far_got = tie(second_coded, far_got)
    second_got = send(second_coded, to_line)
    far_total, far_out = add_up(flags, [far_product], far_got)
    far_other = send(far_out, to_away)

    home = jnp.where(straight, right_home, decode(home_got, strip))
    away = jnp.concatenate(
        [
            jnp.where(straight, right_first, decode(first_got, strip)),
            jnp.where(straight, right_second, decode(second_got, strip)),
        ],
        1,
    )
    gram_right = jnp.concatenate(
        [jnp.where(side == 0, home, away), jnp.where(side == 0, away, home)], 1
    )
    right_state = BETA * right_old + (1.0 - BETA) * gram_right[None]
    right_fixed = right_state / denominator(right_counts)[:, None, None]

    same_decoded = decode(jnp.concatenate([same_other[:tile_rows], same_other[2 * tile_rows : 2 * tile_rows + LEVELS]], 0), tile_rows), decode(
        jnp.concatenate([same_other[tile_rows : 2 * tile_rows], same_other[2 * tile_rows + tile_rows // GROUP : 2 * tile_rows + LEVELS]], 0), tile_rows
    )
    own_pair = (same_total[:tile_rows], same_decoded[0])
    mate_pair = (same_total[tile_rows:], same_decoded[1])
    near_pair = (near_total, decode(near_other, tile_rows))
    far_pair = (far_total, decode(far_other, tile_rows))
    keeps_home = c == side
    inner, outer = [], []
    for index in range(2):
        home_inner = jnp.where(is_middle, own_pair[index], mate_pair[index])
        home_outer = jnp.where(is_middle, mate_pair[index], own_pair[index])
        inner.append(jnp.where(keeps_home, home_inner, near_pair[index]))
        outer.append(jnp.where(keeps_home, home_outer, far_pair[index]))
    first_core = c == 0
    inner = [jnp.where(first_core, inner[0], inner[1]), jnp.where(first_core, inner[1], inner[0])]
    outer = [jnp.where(first_core, outer[0], outer[1]), jnp.where(first_core, outer[1], outer[0])]
    gram_left = jnp.concatenate(
        [jnp.where(first_core, outer[i], inner[i]) for i in range(2)]
        + [jnp.where(first_core, inner[i], outer[i]) for i in range(2)],
        1,
    )
    left_state = BETA * left_old + (1.0 - BETA) * gram_left
    left_fixed = left_state / denominator(left_counts)
    return (left_state, left_fixed, right_state, right_fixed)


def solution(mesh):
    local = line_gather if mesh.shape["row"] == 8 else ring
    return jax.shard_map(
        local,
        mesh=mesh,
        in_specs=(
            P(("groups", "row"), "col"),
            P(("groups", "row"), "col"),
            P(("groups", "col"), "row", None),
            P(("groups", "row"), "col"),
            P(("groups", "col")),
        ),
        out_specs=(
            P(("groups", "row"), "col"),
            P(("groups", "row"), "col"),
            P(("groups", "col"), "row", None),
            P(("groups", "col"), "row", None),
        ),
        check_vma=False,
    )
```

```python
import math

import jax
import jax.numpy as jnp
from jax import lax
from jax.experimental import pallas as pl
from jax.experimental.pallas import tpu as pltpu
from jax.sharding import PartitionSpec as P

BETA = 0.9


def denominator(counters):
    decay_power = jnp.power(jnp.float32(BETA), (counters + 1).astype(jnp.float32))
    return 1.0 - decay_power


def ring_order(count):
    if count == 8:
        return [0, 2, 4, 6, 7, 5, 3, 1]
    return list(range(count))


def ring(gradient, left_old, right_old, left_counts, right_counts):
    tile_rows, half_wide = gradient.shape
    count = lax.axis_size("row")
    strip_wide = half_wide // count
    order = ring_order(count)
    place = {row: at for at, row in enumerate(order)}
    my_row = lax.axis_index("row")
    my_col = lax.axis_index("col")
    up = [(order[at], order[(at + 1) % count]) for at in range(count)]
    down = [(dest, source) for source, dest in up]
    piece = tile_rows // 2
    strip_at = my_row * strip_wide

    state = {"left": jnp.zeros((tile_rows, count * tile_rows), jnp.float32), "right": None}

    def consume(part, step, offset):
        sources = [order[(place[row] - step) % count] for row in range(count)]
        source = jnp.asarray(sources, jnp.int32)[my_row]
        product = lax.dot_general(
            gradient, part, (((1,), (1,)), ((), ())), preferred_element_type=jnp.float32
        )
        pairs = []
        for row in range(count):
            keeper = sources[row] * 2 // count
            pairs.append((row * 2 + 1 - keeper, row * 2 + keeper))
        other = lax.ppermute(product, ("row", "col"), pairs)
        state["left"] = lax.dynamic_update_slice(
            state["left"], product + other, (0, source * tile_rows + offset)
        )
        strip = lax.dynamic_slice_in_dim(part, strip_at, strip_wide, 1)
        term = lax.dot_general(
            strip, part, (((0,), (0,)), ((), ())), preferred_element_type=jnp.float32
        )
        state["right"] = term if state["right"] is None else state["right"] + term

    halves = [gradient[:piece], gradient[piece:]]
    going_up = list(halves)
    going_down = list(halves)
    last = count // 2
    for step in range(1, last + 1):
        if step < last:
            going_up = [lax.ppermute(part, "row", up) for part in going_up]
            going_down = [lax.ppermute(part, "row", down) for part in going_down]
        else:
            going_up = [lax.ppermute(going_up[0], "row", up)]
            going_down = [lax.ppermute(going_down[1], "row", down)]
        if step == 1:
            consume(halves[0], 0, 0)
            consume(halves[1], 0, piece)
        if step < last:
            for at in range(2):
                consume(going_up[at], step, at * piece)
                consume(going_down[at], -step, at * piece)
        else:
            consume(going_up[0], step, 0)
            consume(going_down[0], step, piece)

    width = count * tile_rows // 2
    gram_left = lax.dynamic_slice_in_dim(state["left"], my_col * width, width, 1)
    left_state = BETA * left_old + (1.0 - BETA) * gram_left
    left_fixed = left_state / denominator(left_counts)
    right_state = BETA * right_old + (1.0 - BETA) * state["right"][None]
    right_fixed = right_state / denominator(right_counts)[:, None, None]
    return (left_state, left_fixed, right_state, right_fixed)


GROUP = 64
LEVELS = 16


def pack(values, out_ref, at):
    levels = []
    for first in range(0, values.shape[0], GROUP):
        block = values[first : first + GROUP]
        most = jnp.maximum(jnp.max(jnp.abs(block), axis=0, keepdims=True), 1e-34)
        level = jnp.ceil(jnp.log2(most) * 256.0)
        inverse = 32767.0 * jnp.exp2(level * (-1.0 / 256.0))
        coded = jnp.clip(jnp.round(block * inverse), -32767.0, 32767.0)
        out_ref[at + first : at + first + GROUP] = coded.astype(jnp.int32).astype(jnp.int16)
        levels.append(level)
    return levels


def put_levels(levels, out_ref, at):
    levels = levels + [jnp.zeros_like(levels[0])] * (LEVELS - len(levels))
    out_ref[at : at + LEVELS] = jnp.concatenate(levels, 0).astype(jnp.int32).astype(jnp.int16)


def unpack(ref, index, rows, many):
    level = ref[many * rows : many * rows + LEVELS].astype(jnp.int32).astype(jnp.float32)
    step = jnp.exp2(level * (1.0 / 256.0)) * (1.0 / 32767.0)
    parts = []
    for group in range(rows // GROUP):
        at = index * rows + group * GROUP
        row = index * (rows // GROUP) + group
        block = ref[at : at + GROUP].astype(jnp.int32).astype(jnp.float32)
        parts.append(block * step[row : row + 1])
    return jnp.concatenate(parts, 0)


def decode(coded, rows):
    wide = coded.shape[1]
    level = coded[rows : rows + rows // GROUP].astype(jnp.float32)
    step = jnp.exp2(level * (1.0 / 256.0)) * (1.0 / 32767.0)
    grouped = coded[:rows].astype(jnp.float32).reshape(rows // GROUP, GROUP, wide)
    return (grouped * step[:, None, :]).reshape(rows, wide)


PARAMS = pltpu.CompilerParams(vmem_limit_bytes=48 * 2**20)
FREE = pl.CostEstimate(flops=1, bytes_accessed=1, transcendentals=0)
KEPT, PIECE_A, PIECE_B, SAME_HALF, MIDDLE, CORE = range(6)


def spec(shape, index=None):
    if index is None:
        return pl.BlockSpec(shape, lambda k, flags: (0, 0))
    return pl.BlockSpec(shape, lambda k, flags: (0, index(k, flags)))


def whole(array):
    return spec(array.shape)


def kernel_call(body, flags, steps, ins, outs, aliases=None):
    results = pl.pallas_call(
        body,
        grid_spec=pltpu.PrefetchScalarGridSpec(
            num_scalar_prefetch=1,
            grid=(steps,),
            in_specs=[s for _, s in ins],
            out_specs=[s for _, _, s in outs],
        ),
        out_shape=[jax.ShapeDtypeStruct(shape, dtype) for shape, dtype, _ in outs],
        input_output_aliases=aliases or {},
        compiler_params=PARAMS,
        cost_estimate=FREE,
    )(flags, *[array for array, _ in ins])
    return list(results)


def pick(flag, size):
    return pl.multiple_of(flag * size, GROUP)


def left_terms(flags, rows, slots, block, steps, at=None, before=None, last=True):
    many = len(slots)
    tall = rows[0].shape[0]
    size = 2 * tall

    def body(flag_ref, first_ref, second_ref, *refs):
        slots_in, refs = refs[:many], refs[many:]
        if before is not None:
            before_in, refs = refs[:many], refs[many:]
        outs = refs[:many]
        step = pl.program_id(0)

        @pl.when(step == 0)
        def _():
            for index in range(many):
                outs[index][...] = jnp.zeros_like(outs[index]) if before is None else before_in[index][...]

        for index in range(many):
            for half, ref in enumerate((first_ref, second_ref)):
                outs[index][half * tall : (half + 1) * tall] += dot(ref[...], slots_in[index][...], 1, 1)

        if last:

            @pl.when(step == pl.num_programs(0) - 1)
            def _():
                gone = 1 - flag_ref[KEPT]
                levels = []
                for index in range(many):
                    part = outs[index][pl.ds(pick(gone, tall), tall), :]
                    levels += pack(part, refs[many], index * tall)
                put_levels(levels, refs[many], many * tall)

    from_flag = lambda k, flags: k if at is None else k + flags[at]
    ins = [(part, spec((tall, block), from_flag)) for part in rows]
    ins += [(slot, spec((tall, block), lambda k, flags: k)) for slot in slots]
    if before is not None:
        ins += [(part, whole(part)) for part in before]
    outs = [((size, tall), jnp.float32, spec((size, tall)))] * many
    if last:
        shape = (many * tall + LEVELS, tall)
        outs.append((shape, jnp.int16, spec(shape)))
    return kernel_call(body, flags, steps, ins, outs)


def right_terms(flags, terms, block, steps, at=None, before=None, last=False):
    wide = block * steps
    strip = terms[0][0].shape[1]

    def body(flag_ref, *refs):
        total = None if before is None else refs[2 * len(terms)][...]
        for index in range(len(terms)):
            term = dot(refs[2 * index][...], refs[2 * index + 1][...], 0, 0)
            total = term if total is None else total + term
        outs = refs[2 * len(terms) + (before is not None) :]
        outs[0][...] = total
        if last:
            put_levels(pack(total, outs[1], 0), outs[1], strip)

    here = lambda k, flags: k
    from_flag = lambda k, flags: k if at is None else k + flags[at]
    ins = []
    for strips, columns in terms:
        ins += [(strips, whole(strips)), (columns, spec((columns.shape[0], block), here))]
    if before is not None:
        ins.append((before, spec((strip, block), from_flag)))
    outs = [((strip, wide), jnp.float32, spec((strip, block), here))]
    if last:
        outs.append(((strip + LEVELS, wide), jnp.int16, spec((strip + LEVELS, block), here)))
    return kernel_call(body, flags, steps, ins, outs)


def add_up(flags, products, coded):
    rows, wide = products[0].shape[0] // 2, products[0].shape[1]
    many = len(products)

    def body(flag_ref, *refs):
        coded_ref, total_ref, out_ref = refs[many:]
        levels = []
        for index in range(many):
            kept = refs[index][pl.ds(pick(flag_ref[KEPT], rows), rows), :]
            total = kept + unpack(coded_ref, index, rows, many)
            total_ref[index * rows : (index + 1) * rows] = total
            levels += pack(total, out_ref, index * rows)
        put_levels(levels, out_ref, many * rows)

    ins = [(array, whole(array)) for array in list(products) + [coded]]
    shapes = [((many * rows, wide), jnp.float32), ((many * rows + LEVELS, wide), jnp.int16)]
    return kernel_call(body, flags, 1, ins, [(s, d, spec(s)) for s, d in shapes])


def write_states(old, gram, scale, state_ref, fixed_ref, where):
    state = BETA * old + (1.0 - BETA) * gram
    state_ref[:, where] = state
    fixed_ref[:, where] = state * scale


def finish_right(flags, scale, old, value, coded, at, block, steps, written=None):
    strip, wide = old.shape

    def body(flag_ref, scale_ref, old_ref, value_ref, coded_ref, *refs):
        state_ref, fixed_ref = refs[-2:]
        everything = slice(None)

        @pl.when(flag_ref[KEPT] == 0)
        def _():
            write_states(old_ref[...], value_ref[...], scale_ref[0], state_ref, fixed_ref, everything)

        @pl.when(flag_ref[KEPT] == 1)
        def _():
            write_states(
                old_ref[...], unpack(coded_ref, 0, strip, 1), scale_ref[0], state_ref, fixed_ref, everything
            )

    here = lambda k, flags: k
    there = lambda k, flags: k + flags[at]
    ins = [
        (scale, pl.BlockSpec(memory_space=pltpu.SMEM)),
        (old, spec((strip, block), there)),
        (value, spec((strip, block), here)),
        (coded, spec((strip + LEVELS, block), here)),
    ]
    aliases = None
    if written is not None:
        ins += [(array, pl.BlockSpec(memory_space=pl.ANY)) for array in written]
        aliases = {5: 0, 6: 1}
    outs = [((strip, wide), jnp.float32, spec((strip, block), there))] * 2
    return kernel_call(body, flags, steps, ins, outs, aliases)


def finish_left(flags, scale, old, same_total, same_other, total, other, inner, written=None):
    tall, wide = total.shape
    plane = 2 * wide

    def body(flag_ref, scale_ref, old_ref, same_ref, same_other_ref, total_ref, other_ref, *refs):
        state_ref, fixed_ref = refs[-2:]

        def put(core, value):
            where = slice(core * wide, (core + 1) * wide)
            write_states(old_ref[:, where], value, scale_ref[0], state_ref, fixed_ref, where)

        is_mate = 1 - flag_ref[MIDDLE] if inner else flag_ref[MIDDLE]
        for core in range(2):
            mine = flag_ref[CORE] == core
            same = flag_ref[SAME_HALF] == 1

            @pl.when(mine & same)
            def _():
                put(core, same_ref[pl.ds(pick(is_mate, tall), tall), :])

            @pl.when(mine & jnp.logical_not(same))
            def _():
                put(core, total_ref[...])

            for index in range(2):

                @pl.when(jnp.logical_not(mine) & same & (is_mate == index))
                def _():
                    put(core, unpack(same_other_ref, index, tall, 2))

            @pl.when(jnp.logical_not(mine) & jnp.logical_not(same))
            def _():
                put(core, unpack(other_ref, 0, tall, 1))

    there = (lambda k, flags: 1 - flags[CORE]) if inner else (lambda k, flags: flags[CORE])
    ins = [(scale, pl.BlockSpec(memory_space=pltpu.SMEM)), (old, spec((tall, plane), there))]
    ins += [(array, whole(array)) for array in (same_total, same_other, total, other)]
    aliases = None
    if written is not None:
        ins += [(array, pl.BlockSpec(memory_space=pl.ANY)) for array in written]
        aliases = {7: 0, 8: 1}
    outs = [(old.shape, jnp.float32, spec((tall, plane), there))] * 2
    return kernel_call(body, flags, 1, ins, outs, aliases)


def dot(a, b, a_dim, b_dim):
    return lax.dot_general(
        a, b, (((a_dim,), (b_dim,)), ((), ())), preferred_element_type=jnp.float32
    )


AXES = ("row", "col")
CHIPS = [(z, y) for z in range(4) for y in range(2)]


def at(z, y, c):
    return (z * 2 + y) * 2 + c


def send(value, rule):
    pairs = []
    for z, y in CHIPS:
        for c in range(2):
            dest = rule(z, y, c)
            if dest is not None:
                pairs.append((at(z, y, c), at(*dest)))
    return lax.ppermute(value, AXES, pairs)


def middle(z):
    return z in (1, 2)


def to_line(z, y, c):
    return (z, c, y) if c != y else None


def pair_line(z, y, c):
    return (z ^ 1, c, y)


def across_line(z, y, c):
    return (3 - z, c, y) if middle(z) else None


def across(z, y, c):
    return (3 - z, y, c) if middle(z) else None


def outward(z, y, c):
    return (z ^ 1, y, c) if middle(z) else None


def beside(z, y, c):
    return (z, y, 1 - c)


def other_y(z, y, c):
    return (z, 1 - y, c)


def to_home(z, y, c):
    return (z, y, 1 - c) if c != z // 2 else None


def to_away(z, y, c):
    return (z, y, 1 - c) if c == z // 2 else None


def line_gather(gradient, left_old, right_old, left_counts, right_counts):
    tile_rows, half_wide = gradient.shape
    block = half_wide // 4
    strip = half_wide // 8
    my_row = lax.axis_index("row")
    c = lax.axis_index("col")
    z, y = my_row // 2, my_row % 2
    side = (z >= 2).astype(jnp.int32)
    is_middle = (z == 1) | (z == 2)
    straight = c == y
    flags = jnp.stack(
        [
            jnp.where(straight, 0, 1),
            side,
            3 * (1 - side),
            (c == side).astype(jnp.int32),
            is_middle.astype(jnp.int32),
            c,
        ]
    ).astype(jnp.int32)
    strip_at = (2 * z + c) * strip

    def tie(*values):
        return lax.optimization_barrier(tuple(values))

    def columns(value, first, count):
        return lax.dynamic_slice_in_dim(value, first * block, count * block, 1)

    def strips_of(pair, first=0):
        return [lax.dynamic_slice_in_dim(part, strip_at - first, strip, 1) for part in pair]

    def terms(strips, pair):
        return list(zip(strips, pair))

    mate_b = send(columns(gradient, 3 * side, 1), pair_line)
    mate_a = send(columns(gradient, 1 - side, 3), pair_line)
    cross = send(gradient, across_line)
    gradient_t, mate_a, mate_b, cross = tie(gradient, mate_a, mate_b, cross)
    far_a = send(mate_a, across)
    far_b = send(mate_b, across)
    near = send(cross, outward)
    swapped = send(gradient_t, to_line)

    def in_order(part_a, part_b):
        return jnp.where(
            side == 0, jnp.concatenate([part_b, part_a], 1), jnp.concatenate([part_a, part_b], 1)
        )

    mate = in_order(mate_a, mate_b)
    mates = (mate, send(mate, beside))
    mine = jnp.where(straight, gradient, swapped)
    starts = range(0, half_wide, block)
    own = (
        mine,
        jnp.concatenate(
            [send(mine[:, first : first + block], beside) for first in starts], 1
        ),
    )
    own_product, mate_product, same_coded = left_terms(flags, own, [mine, mate], block, 4)
    same_products = [own_product, mate_product]
    same_got = send(same_coded, other_y)
    [right] = right_terms(
        flags, terms(strips_of(own), own) + terms(strips_of(mates), mates), block, 4
    )

    right, same_coded, near, far_a, far_b = tie(right, same_coded, near, far_a, far_b)
    end_a = send(far_a, outward)
    near = jnp.where(is_middle, cross, near)
    nears = (near, send(near, beside))
    near_product, near_coded = left_terms(flags, own, [near], block, 4)
    near_got = send(near_coded, other_y)
    [right] = right_terms(flags, terms(strips_of(nears), nears), block, 4, before=right)
    same_total, same_out = add_up(flags, same_products, same_got)
    same_other = send(same_out, to_home)
    near_got, right, same_out = tie(near_got, right, same_out)
    near_total, near_out = add_up(flags, [near_product], near_got)
    near_other = send(near_out, to_away)

    right, near_out, end_a, same_other, near_other = tie(right, near_out, end_a, same_other, near_other)
    far_b, end_a = tie(far_b, end_a)
    end_b = send(far_b, outward)
    end_a = jnp.where(is_middle, far_a, end_a)
    ends_a = (end_a, send(end_a, beside))
    [far_product] = left_terms(flags, own, [end_a], block, 3, at=PIECE_A, last=False)
    strips = strips_of(ends_a, side * block)
    right_a, coded_a = right_terms(
        flags, terms(strips, ends_a), block, 3, at=PIECE_A, before=right, last=True
    )
    got_a = send(coded_a, to_line)
    left_scale = 1.0 / denominator(left_counts).reshape(1)
    right_scale = 1.0 / denominator(right_counts)
    coded_a, near_other, same_other = tie(coded_a, near_other, same_other)
    left_done = finish_left(
        flags, left_scale, left_old, same_total, same_other, near_total, near_other, True
    )

    left_done[0], coded_a, far_product, end_b = tie(left_done[0], coded_a, far_product, end_b)
    end_b = jnp.where(is_middle, far_b, end_b)
    ends_b = (end_b, send(end_b, beside))
    far_product, far_coded = left_terms(
        flags, own, [end_b], block, 1, at=PIECE_B, before=[far_product]
    )
    far_got = send(far_coded, other_y)
    right_b, coded_b = right_terms(
        flags, terms(strips, ends_b), block, 1, at=PIECE_B, before=right, last=True
    )
    got_b = send(coded_b, to_line)
    old = right_old[0]
    coded_b, far_got = tie(coded_b, far_got)
    far_total, far_out = add_up(flags, [far_product], far_got)
    far_other = send(far_out, to_away)
    far_out, got_a = tie(far_out, got_a)
    right_done = finish_right(flags, right_scale, old, right_a, got_a, PIECE_A, block, 3)
    right_done[0], got_b = tie(right_done[0], got_b)
    right_state, right_fixed = finish_right(
        flags, right_scale, old, right_b, got_b, PIECE_B, block, 1, right_done
    )
    far_other, right_state = tie(far_other, right_state)
    left_state, left_fixed = finish_left(
        flags, left_scale, left_old, same_total, same_other, far_total, far_other, False, left_done
    )
    return (left_state, left_fixed, right_state[None], right_fixed[None])


def solution(mesh):
    local = line_gather if mesh.shape["row"] == 8 else ring
    return jax.shard_map(
        local,
        mesh=mesh,
        in_specs=(
            P(("groups", "row"), "col"),
            P(("groups", "row"), "col"),
            P(("groups", "col"), "row", None),
            P(("groups", "row"), "col"),
            P(("groups", "col")),
        ),
        out_specs=(
            P(("groups", "row"), "col"),
            P(("groups", "row"), "col"),
            P(("groups", "col"), "row", None),
            P(("groups", "col"), "row", None),
        ),
        check_vma=False,
    )
```

```python
import functools

import jax
import jax.numpy as jnp
from jax import lax
from jax.experimental import pallas as pl
from jax.experimental.pallas import tpu as pltpu
from jax.sharding import PartitionSpec as P

BETA = 0.9


def denominator(counters):
    decay_power = jnp.power(jnp.float32(BETA), (counters + 1).astype(jnp.float32))
    return 1.0 - decay_power


def ring_order(count):
    if count == 8:
        return [0, 2, 4, 6, 7, 5, 3, 1]
    return list(range(count))


def ring(gradient, left_old, right_old, left_counts, right_counts):
    tile_rows, half_wide = gradient.shape
    count = lax.axis_size("row")
    strip_wide = half_wide // count
    order = ring_order(count)
    place = {row: at for at, row in enumerate(order)}
    my_row = lax.axis_index("row")
    my_col = lax.axis_index("col")
    up = [(order[at], order[(at + 1) % count]) for at in range(count)]
    down = [(dest, source) for source, dest in up]
    piece = tile_rows // 2
    strip_at = my_row * strip_wide

    state = {"left": jnp.zeros((tile_rows, count * tile_rows), jnp.float32), "right": None}

    def consume(part, step, offset):
        sources = [order[(place[row] - step) % count] for row in range(count)]
        source = jnp.asarray(sources, jnp.int32)[my_row]
        product = lax.dot_general(
            gradient, part, (((1,), (1,)), ((), ())), preferred_element_type=jnp.float32
        )
        pairs = []
        for row in range(count):
            keeper = sources[row] * 2 // count
            pairs.append((row * 2 + 1 - keeper, row * 2 + keeper))
        other = lax.ppermute(product, ("row", "col"), pairs)
        state["left"] = lax.dynamic_update_slice(
            state["left"], product + other, (0, source * tile_rows + offset)
        )
        strip = lax.dynamic_slice_in_dim(part, strip_at, strip_wide, 1)
        term = lax.dot_general(
            strip, part, (((0,), (0,)), ((), ())), preferred_element_type=jnp.float32
        )
        state["right"] = term if state["right"] is None else state["right"] + term

    halves = [gradient[:piece], gradient[piece:]]
    going_up = list(halves)
    going_down = list(halves)
    last = count // 2
    for step in range(1, last + 1):
        if step < last:
            going_up = [lax.ppermute(part, "row", up) for part in going_up]
            going_down = [lax.ppermute(part, "row", down) for part in going_down]
        else:
            going_up = [lax.ppermute(going_up[0], "row", up)]
            going_down = [lax.ppermute(going_down[1], "row", down)]
        if step == 1:
            consume(halves[0], 0, 0)
            consume(halves[1], 0, piece)
        if step < last:
            for at in range(2):
                consume(going_up[at], step, at * piece)
                consume(going_down[at], -step, at * piece)
        else:
            consume(going_up[0], step, 0)
            consume(going_down[0], step, piece)

    width = count * tile_rows // 2
    gram_left = lax.dynamic_slice_in_dim(state["left"], my_col * width, width, 1)
    left_state = BETA * left_old + (1.0 - BETA) * gram_left
    left_fixed = left_state / denominator(left_counts)
    right_state = BETA * right_old + (1.0 - BETA) * state["right"][None]
    right_fixed = right_state / denominator(right_counts)[:, None, None]
    return (left_state, left_fixed, right_state, right_fixed)


GROUP = 64
LEVELS = 16


def pack(values, out_ref, at):
    levels = []
    for first in range(0, values.shape[0], GROUP):
        block = values[first : first + GROUP]
        most = jnp.maximum(jnp.max(jnp.abs(block), axis=0, keepdims=True), 1e-34)
        level = jnp.ceil(jnp.log2(most) * 256.0)
        inverse = 32767.0 * jnp.exp2(level * (-1.0 / 256.0))
        coded = jnp.clip(jnp.round(block * inverse), -32767.0, 32767.0)
        out_ref[at + first : at + first + GROUP] = coded.astype(jnp.int32).astype(jnp.int16)
        levels.append(level)
    return levels


def put_levels(levels, out_ref, at):
    levels = levels + [jnp.zeros_like(levels[0])] * (LEVELS - len(levels))
    out_ref[at : at + LEVELS] = jnp.concatenate(levels, 0).astype(jnp.int32).astype(jnp.int16)


def unpack(ref, index, rows, many):
    level = ref[many * rows : many * rows + LEVELS].astype(jnp.int32).astype(jnp.float32)
    step = jnp.exp2(level * (1.0 / 256.0)) * (1.0 / 32767.0)
    parts = []
    for group in range(rows // GROUP):
        at = index * rows + group * GROUP
        row = index * (rows // GROUP) + group
        block = ref[at : at + GROUP].astype(jnp.int32).astype(jnp.float32)
        parts.append(block * step[row : row + 1])
    return jnp.concatenate(parts, 0)


def decode(coded, rows):
    wide = coded.shape[1]
    level = coded[rows : rows + rows // GROUP].astype(jnp.float32)
    step = jnp.exp2(level * (1.0 / 256.0)) * (1.0 / 32767.0)
    grouped = coded[:rows].astype(jnp.float32).reshape(rows // GROUP, GROUP, wide)
    return (grouped * step[:, None, :]).reshape(rows, wide)


PARAMS = pltpu.CompilerParams(vmem_limit_bytes=48 * 2**20)
FREE = pl.CostEstimate(flops=1, bytes_accessed=1, transcendentals=0)
KEPT, START, HOME, AWAY, LAST, SAME_HALF, MIDDLE, CORE = range(8)


def spec(shape, index=None):
    if index is None:
        return pl.BlockSpec(shape, lambda k, flags: (0, 0))
    return pl.BlockSpec(shape, lambda k, flags: (0, index(k, flags)))


def whole(array):
    return spec(array.shape)


def kernel_call(body, flags, steps, ins, outs, aliases=None, scratch=()):
    results = pl.pallas_call(
        body,
        grid_spec=pltpu.PrefetchScalarGridSpec(
            num_scalar_prefetch=1,
            grid=(steps,),
            in_specs=[s for _, s in ins],
            out_specs=[s for _, _, s in outs],
            scratch_shapes=list(scratch),
        ),
        out_shape=[jax.ShapeDtypeStruct(shape, dtype) for shape, dtype, _ in outs],
        input_output_aliases=aliases or {},
        compiler_params=PARAMS,
        cost_estimate=FREE,
    )(flags, *[array for array, _ in ins])
    return list(results)


def pick(flag, size):
    return pl.multiple_of(flag * size, GROUP)


def blocks_from(at):
    return lambda k, flags: k + flags[at]


def left_terms(flags, rows, slots, block, steps, at=START, before=None, last=True):
    many = len(slots)
    choices = [len(slot) for slot in slots]
    tall = rows[0].shape[0]
    size = 2 * tall

    def body(flag_ref, first_ref, second_ref, *refs):
        slots_in = []
        for count in choices:
            slots_in.append(refs[:count])
            refs = refs[count:]
        if before is not None:
            before_in, refs = refs[:many], refs[many:]
        outs = refs[:many]
        step = pl.program_id(0)

        @pl.when(step == 0)
        def _():
            for index in range(many):
                outs[index][...] = jnp.zeros_like(outs[index]) if before is None else before_in[index][...]

        def add(index, ref):
            for half, row_ref in enumerate((first_ref, second_ref)):
                outs[index][half * tall : (half + 1) * tall] += dot(row_ref[...], ref[...], 1, 1)

        for index in range(many):
            if choices[index] == 1:
                add(index, slots_in[index][0])
            else:
                for choice in range(2):
                    pl.when(flag_ref[MIDDLE] == choice)(
                        functools.partial(add, index, slots_in[index][choice])
                    )

        if last:

            @pl.when(step == pl.num_programs(0) - 1)
            def _():
                gone = 1 - flag_ref[KEPT]
                levels = []
                for index in range(many):
                    part = outs[index][pl.ds(pick(gone, tall), tall), :]
                    levels += pack(part, refs[many], index * tall)
                put_levels(levels, refs[many], many * tall)

    ins = [(part, spec((tall, block), blocks_from(at))) for part in rows]
    for slot in slots:
        ins += [(array, spec((tall, block), blocks_from(start))) for array, start in slot]
    if before is not None:
        ins += [(part, whole(part)) for part in before]
    outs = [((size, tall), jnp.float32, spec((size, tall)))] * many
    if last:
        shape = (many * tall + LEVELS, tall)
        outs.append((shape, jnp.int16, spec(shape)))
    return kernel_call(body, flags, steps, ins, outs)


def right_terms(flags, strips, columns, block, steps, at=START, before=None, last=False):
    wide = block * steps
    rows, strip = strips[0].shape
    many = len(strips)

    def body(flag_ref, *refs):
        strips_in, refs = refs[:many], refs[many:]
        columns_in = []
        for choice in columns:
            columns_in.append(refs[: len(choice)])
            refs = refs[len(choice) :]
        if before is not None:
            before_in, refs = refs[0], refs[1:]
        outs, turned = refs[:-1], refs[-1]

        @pl.when(pl.program_id(0) == 0)
        def _():
            for index in range(many):
                turned[index] = strips_in[index][...].T

        def add(choice):
            total = None if before is None else before_in[...]
            for index in range(many):
                refs_here = columns_in[index]
                ref = refs_here[choice if len(refs_here) == 2 else 0]
                term = dot(turned[index], ref[...], 1, 0)
                total = term if total is None else total + term
            outs[0][...] = total

        if max(len(choice) for choice in columns) == 1:
            add(0)
        else:
            for choice in range(2):
                pl.when(flag_ref[MIDDLE] == choice)(functools.partial(add, choice))
        if last:
            put_levels(pack(outs[0][...], outs[1], 0), outs[1], strip)

    here = lambda k, flags: k
    ins = [(part, whole(part)) for part in strips]
    for choice in columns:
        ins += [(array, spec((rows, block), blocks_from(start))) for array, start in choice]
    if before is not None:
        ins.append((before, spec((strip, block), blocks_from(at))))
    outs = [((strip, wide), jnp.float32, spec((strip, block), here))]
    if last:
        outs.append(((strip + LEVELS, wide), jnp.int16, spec((strip + LEVELS, block), here)))
    scratch = [pltpu.VMEM((many, strip, rows), jnp.bfloat16)]
    return kernel_call(body, flags, steps, ins, outs, scratch=scratch)


def add_up(flags, products, coded):
    rows, wide = products[0].shape[0] // 2, products[0].shape[1]
    many = len(products)

    def body(flag_ref, *refs):
        coded_ref, total_ref, out_ref = refs[many:]
        levels = []
        for index in range(many):
            kept = refs[index][pl.ds(pick(flag_ref[KEPT], rows), rows), :]
            total = kept + unpack(coded_ref, index, rows, many)
            total_ref[index * rows : (index + 1) * rows] = total
            levels += pack(total, out_ref, index * rows)
        put_levels(levels, out_ref, many * rows)

    ins = [(array, whole(array)) for array in list(products) + [coded]]
    shapes = [((many * rows, wide), jnp.float32), ((many * rows + LEVELS, wide), jnp.int16)]
    return kernel_call(body, flags, 1, ins, [(s, d, spec(s)) for s, d in shapes])


def write_states(old, gram, scale, state_ref, fixed_ref, where):
    state = BETA * old + (1.0 - BETA) * gram
    state_ref[:, where] = state
    fixed_ref[:, where] = state * scale


def finish_right(flags, scale, old, value, coded, at, block, steps, written=None):
    strip, wide = old.shape

    def body(flag_ref, scale_ref, old_ref, value_ref, coded_ref, *refs):
        state_ref, fixed_ref = refs[-2:]
        everything = slice(None)

        @pl.when(flag_ref[KEPT] == 0)
        def _():
            write_states(old_ref[...], value_ref[...], scale_ref[0], state_ref, fixed_ref, everything)

        @pl.when(flag_ref[KEPT] == 1)
        def _():
            write_states(
                old_ref[...], unpack(coded_ref, 0, strip, 1), scale_ref[0], state_ref, fixed_ref, everything
            )

    here = lambda k, flags: k
    there = lambda k, flags: k + flags[at]
    ins = [
        (scale, pl.BlockSpec(memory_space=pltpu.SMEM)),
        (old, spec((strip, block), there)),
        (value, spec((strip, block), here)),
        (coded, spec((strip + LEVELS, block), here)),
    ]
    aliases = None
    if written is not None:
        ins += [(array, pl.BlockSpec(memory_space=pl.ANY)) for array in written]
        aliases = {5: 0, 6: 1}
    outs = [((strip, wide), jnp.float32, spec((strip, block), there))] * 2
    return kernel_call(body, flags, steps, ins, outs, aliases)


def finish_left(flags, scale, old, same_total, same_other, total, other, inner, written=None):
    tall, wide = total.shape
    plane = 2 * wide

    def body(flag_ref, scale_ref, old_ref, same_ref, same_other_ref, total_ref, other_ref, *refs):
        state_ref, fixed_ref = refs[-2:]

        def put(core, value):
            where = slice(core * wide, (core + 1) * wide)
            write_states(old_ref[:, where], value, scale_ref[0], state_ref, fixed_ref, where)

        is_mate = 1 - flag_ref[MIDDLE] if inner else flag_ref[MIDDLE]
        for core in range(2):
            mine = flag_ref[CORE] == core
            same = flag_ref[SAME_HALF] == 1

            @pl.when(mine & same)
            def _():
                put(core, same_ref[pl.ds(pick(is_mate, tall), tall), :])

            @pl.when(mine & jnp.logical_not(same))
            def _():
                put(core, total_ref[...])

            for index in range(2):

                @pl.when(jnp.logical_not(mine) & same & (is_mate == index))
                def _():
                    put(core, unpack(same_other_ref, index, tall, 2))

            @pl.when(jnp.logical_not(mine) & jnp.logical_not(same))
            def _():
                put(core, unpack(other_ref, 0, tall, 1))

    there = (lambda k, flags: 1 - flags[CORE]) if inner else (lambda k, flags: flags[CORE])
    ins = [(scale, pl.BlockSpec(memory_space=pltpu.SMEM)), (old, spec((tall, plane), there))]
    ins += [(array, whole(array)) for array in (same_total, same_other, total, other)]
    aliases = None
    if written is not None:
        ins += [(array, pl.BlockSpec(memory_space=pl.ANY)) for array in written]
        aliases = {7: 0, 8: 1}
    outs = [(old.shape, jnp.float32, spec((tall, plane), there))] * 2
    return kernel_call(body, flags, 1, ins, outs, aliases)


def dot(a, b, a_dim, b_dim):
    return lax.dot_general(
        a, b, (((a_dim,), (b_dim,)), ((), ())), preferred_element_type=jnp.float32
    )


AXES = ("row", "col")
CHIPS = [(z, y) for z in range(4) for y in range(2)]


def at(z, y, c):
    return (z * 2 + y) * 2 + c


def send(value, rule):
    pairs = []
    for z, y in CHIPS:
        for c in range(2):
            dest = rule(z, y, c)
            if dest is not None:
                pairs.append((at(z, y, c), at(*dest)))
    return lax.ppermute(value, AXES, pairs)


def middle(z):
    return z in (1, 2)


def to_line(z, y, c):
    return (z, c, y) if c != y else None


def pair_line(z, y, c):
    return (z ^ 1, c, y)


def across_line(z, y, c):
    return (3 - z, c, y) if middle(z) else None


def across(z, y, c):
    return (3 - z, y, c) if middle(z) else None


def outward(z, y, c):
    return (z ^ 1, y, c) if middle(z) else None


def beside(z, y, c):
    return (z, y, 1 - c)


def other_y(z, y, c):
    return (z, 1 - y, c)


def to_home(z, y, c):
    return (z, y, 1 - c) if c != z // 2 else None


def to_away(z, y, c):
    return (z, y, 1 - c) if c == z // 2 else None


def line_gather(gradient, left_old, right_old, left_counts, right_counts):
    tile_rows, half_wide = gradient.shape
    block = half_wide // 4
    strip = half_wide // 8
    my_row = lax.axis_index("row")
    c = lax.axis_index("col")
    z, y = my_row // 2, my_row % 2
    side = (z >= 2).astype(jnp.int32)
    is_middle = (z == 1) | (z == 2)
    straight = c == y
    flags = jnp.stack(
        [
            jnp.where(straight, 0, 1),
            0,
            2 * side,
            2 * (1 - side),
            2 * (1 - side) + 1,
            (c == side).astype(jnp.int32),
            is_middle.astype(jnp.int32),
            c,
        ]
    ).astype(jnp.int32)
    strip_at = (2 * z + c) * strip

    def tie(*values):
        return lax.optimization_barrier(tuple(values))

    def columns(value, first, count):
        return lax.dynamic_slice_in_dim(value, first * block, count * block, 1)

    def strips_of(pair, first=0):
        return [lax.dynamic_slice_in_dim(part, strip_at - first, strip, 1) for part in pair]

    def one(array, at=START):
        return [(array, at)]

    mate = send(gradient, pair_line)
    cross = send(gradient, across_line)
    gradient_t, mate, cross = tie(gradient, mate, cross)
    far = send(mate, across)
    near = send(cross, outward)
    swapped = send(gradient_t, to_line)
    mates = (mate, send(mate, beside))
    cross_o = send(cross, beside)
    mine = jnp.where(straight, gradient, swapped)
    starts = range(0, half_wide, block)
    own = (
        mine,
        jnp.concatenate(
            [send(mine[:, first : first + block], beside) for first in starts], 1
        ),
    )
    own_product, mate_product, same_coded = left_terms(flags, own, [one(mine), one(mate)], block, 4)
    same_products = [own_product, mate_product]
    same_got = send(same_coded, other_y)
    [right] = right_terms(
        flags, strips_of(own) + strips_of(mates), [one(part) for part in own + mates], block, 4
    )

    right, same_coded, near, far, cross_o = tie(right, same_coded, near, far, cross_o)
    end_home = send(columns(far, 2 * side, 2), outward)
    near_o = send(near, beside)
    far_o = send(far, beside)
    near_product, near_coded = left_terms(
        flags, own, [[(near, START), (cross, START)]], block, 4
    )
    near_got = send(near_coded, other_y)
    near_strips = strips_of((jnp.where(is_middle, cross, near), jnp.where(is_middle, cross_o, near_o)))
    [right] = right_terms(
        flags,
        near_strips,
        [[(near, START), (cross, START)], [(near_o, START), (cross_o, START)]],
        block,
        4,
        before=right,
    )
    same_got, right = tie(same_got, right)
    same_total, same_out = add_up(flags, same_products, same_got)
    same_other = send(same_out, to_home)

    right, same_out, end_home, far_o = tie(right, same_out, end_home, far_o)
    far, end_home = tie(far, end_home)
    end_first = send(columns(far, 2 * (1 - side), 1), outward)
    end_home_o = send(end_home, beside)
    [far_product] = left_terms(
        flags, own, [[(end_home, START), (far, HOME)]], block, 2, at=HOME, last=False
    )
    strips = [
        jnp.where(is_middle, strips_of([a])[0], strips_of([b], 2 * side * block)[0])
        for a, b in ((far, end_home), (far_o, end_home_o))
    ]
    right_home, home_coded = right_terms(
        flags,
        strips,
        [[(end_home, START), (far, HOME)], [(end_home_o, START), (far_o, HOME)]],
        block,
        2,
        at=HOME,
        before=right,
        last=True,
    )
    home_got = send(home_coded, to_line)
    near_got, home_coded = tie(near_got, home_coded)
    near_total, near_out = add_up(flags, [near_product], near_got)
    near_other = send(near_out, to_away)

    def quarter(end, at, far_product, last):
        end_o = send(end, beside)
        lefts = left_terms(
            flags, own, [[(end, START), (far, at)]], block, 1, at=at, before=[far_product], last=last
        )
        value, coded = right_terms(
            flags,
            strips,
            [[(end, START), (far, at)], [(end_o, START), (far_o, at)]],
            block,
            1,
            at=at,
            before=right,
            last=True,
        )
        return lefts, value, coded

    left_scale = 1.0 / denominator(left_counts).reshape(1)
    right_scale = 1.0 / denominator(right_counts)
    old = right_old[0]
    near_out, far_product, end_first = tie(near_out, far_product, end_first)
    far, end_first = tie(far, end_first)
    end_last = send(columns(far, 2 * (1 - side) + 1, 1), outward)
    [far_product], right_first, first_coded = quarter(end_first, AWAY, far_product, False)
    first_got = send(first_coded, to_line)
    first_coded, home_got = tie(first_coded, home_got)
    right_done = finish_right(flags, right_scale, old, right_home, home_got, HOME, block, 2)
    right_done[0], near_other, same_other = tie(right_done[0], near_other, same_other)
    left_done = finish_left(
        flags, left_scale, left_old, same_total, same_other, near_total, near_other, True
    )

    left_done[0], far_product, end_last = tie(left_done[0], far_product, end_last)
    [far_product, far_coded], right_last, last_coded = quarter(end_last, LAST, far_product, True)
    far_got = send(far_coded, other_y)
    last_got = send(last_coded, to_line)
    last_coded, first_got = tie(last_coded, first_got)
    right_done = finish_right(
        flags, right_scale, old, right_first, first_got, AWAY, block, 1, right_done
    )
    right_done[0], far_got = tie(right_done[0], far_got)
    far_total, far_out = add_up(flags, [far_product], far_got)
    far_other = send(far_out, to_away)
    far_out, last_got = tie(far_out, last_got)
    right_state, right_fixed = finish_right(
        flags, right_scale, old, right_last, last_got, LAST, block, 1, right_done
    )
    far_other, right_state = tie(far_other, right_state)
    left_state, left_fixed = finish_left(
        flags, left_scale, left_old, same_total, same_other, far_total, far_other, False, left_done
    )
    return (left_state, left_fixed, right_state[None], right_fixed[None])


def solution(mesh):
    local = line_gather if mesh.shape["row"] == 8 else ring
    return jax.shard_map(
        local,
        mesh=mesh,
        in_specs=(
            P(("groups", "row"), "col"),
            P(("groups", "row"), "col"),
            P(("groups", "col"), "row", None),
            P(("groups", "row"), "col"),
            P(("groups", "col")),
        ),
        out_specs=(
            P(("groups", "row"), "col"),
            P(("groups", "row"), "col"),
            P(("groups", "col"), "row", None),
            P(("groups", "col"), "row", None),
        ),
        check_vma=False,
    )
```

```python
import functools

import jax
import jax.numpy as jnp
from jax import lax
from jax.experimental import pallas as pl
from jax.experimental.pallas import tpu as pltpu
from jax.sharding import PartitionSpec as P

BETA = 0.9


def denominator(counters):
    decay_power = jnp.power(jnp.float32(BETA), (counters + 1).astype(jnp.float32))
    return 1.0 - decay_power


def ring_order(count):
    if count == 8:
        return [0, 2, 4, 6, 7, 5, 3, 1]
    return list(range(count))


def ring(gradient, left_old, right_old, left_counts, right_counts):
    tile_rows, half_wide = gradient.shape
    count = lax.axis_size("row")
    strip_wide = half_wide // count
    order = ring_order(count)
    place = {row: at for at, row in enumerate(order)}
    my_row = lax.axis_index("row")
    my_col = lax.axis_index("col")
    up = [(order[at], order[(at + 1) % count]) for at in range(count)]
    down = [(dest, source) for source, dest in up]
    piece = tile_rows // 2
    strip_at = my_row * strip_wide

    state = {"left": jnp.zeros((tile_rows, count * tile_rows), jnp.float32), "right": None}

    def consume(part, step, offset):
        sources = [order[(place[row] - step) % count] for row in range(count)]
        source = jnp.asarray(sources, jnp.int32)[my_row]
        product = lax.dot_general(
            gradient, part, (((1,), (1,)), ((), ())), preferred_element_type=jnp.float32
        )
        pairs = []
        for row in range(count):
            keeper = sources[row] * 2 // count
            pairs.append((row * 2 + 1 - keeper, row * 2 + keeper))
        other = lax.ppermute(product, ("row", "col"), pairs)
        state["left"] = lax.dynamic_update_slice(
            state["left"], product + other, (0, source * tile_rows + offset)
        )
        strip = lax.dynamic_slice_in_dim(part, strip_at, strip_wide, 1)
        term = lax.dot_general(
            strip, part, (((0,), (0,)), ((), ())), preferred_element_type=jnp.float32
        )
        state["right"] = term if state["right"] is None else state["right"] + term

    halves = [gradient[:piece], gradient[piece:]]
    going_up = list(halves)
    going_down = list(halves)
    last = count // 2
    for step in range(1, last + 1):
        if step < last:
            going_up = [lax.ppermute(part, "row", up) for part in going_up]
            going_down = [lax.ppermute(part, "row", down) for part in going_down]
        else:
            going_up = [lax.ppermute(going_up[0], "row", up)]
            going_down = [lax.ppermute(going_down[1], "row", down)]
        if step == 1:
            consume(halves[0], 0, 0)
            consume(halves[1], 0, piece)
        if step < last:
            for at in range(2):
                consume(going_up[at], step, at * piece)
                consume(going_down[at], -step, at * piece)
        else:
            consume(going_up[0], step, 0)
            consume(going_down[0], step, piece)

    width = count * tile_rows // 2
    gram_left = lax.dynamic_slice_in_dim(state["left"], my_col * width, width, 1)
    left_state = BETA * left_old + (1.0 - BETA) * gram_left
    left_fixed = left_state / denominator(left_counts)
    right_state = BETA * right_old + (1.0 - BETA) * state["right"][None]
    right_fixed = right_state / denominator(right_counts)[:, None, None]
    return (left_state, left_fixed, right_state, right_fixed)


GROUP = 64
LEVELS = 16


def pack(values, out_ref, at):
    levels = []
    for first in range(0, values.shape[0], GROUP):
        block = values[first : first + GROUP]
        most = jnp.maximum(jnp.max(jnp.abs(block), axis=0, keepdims=True), 1e-34)
        level = jnp.ceil(jnp.log2(most) * 256.0)
        inverse = 32767.0 * jnp.exp2(level * (-1.0 / 256.0))
        coded = jnp.clip(jnp.round(block * inverse), -32767.0, 32767.0)
        out_ref[at + first : at + first + GROUP] = coded.astype(jnp.int32).astype(jnp.int16)
        levels.append(level)
    return levels


def put_levels(levels, out_ref, at):
    levels = levels + [jnp.zeros_like(levels[0])] * (LEVELS - len(levels))
    out_ref[at : at + LEVELS] = jnp.concatenate(levels, 0).astype(jnp.int32).astype(jnp.int16)


def unpack(ref, index, rows, many):
    level = ref[many * rows : many * rows + LEVELS].astype(jnp.int32).astype(jnp.float32)
    step = jnp.exp2(level * (1.0 / 256.0)) * (1.0 / 32767.0)
    parts = []
    for group in range(rows // GROUP):
        at = index * rows + group * GROUP
        row = index * (rows // GROUP) + group
        block = ref[at : at + GROUP].astype(jnp.int32).astype(jnp.float32)
        parts.append(block * step[row : row + 1])
    return jnp.concatenate(parts, 0)


def decode(coded, rows):
    wide = coded.shape[1]
    level = coded[rows : rows + rows // GROUP].astype(jnp.float32)
    step = jnp.exp2(level * (1.0 / 256.0)) * (1.0 / 32767.0)
    grouped = coded[:rows].astype(jnp.float32).reshape(rows // GROUP, GROUP, wide)
    return (grouped * step[:, None, :]).reshape(rows, wide)


PARAMS = pltpu.CompilerParams(vmem_limit_bytes=48 * 2**20)
FREE = pl.CostEstimate(flops=1, bytes_accessed=1, transcendentals=0)
KEPT, START, HOME, AWAY, LAST, SAME_HALF, MIDDLE, CORE = range(8)


def spec(shape, index=None):
    if index is None:
        return pl.BlockSpec(shape, lambda k, flags: (0, 0))
    return pl.BlockSpec(shape, lambda k, flags: (0, index(k, flags)))


def whole(array):
    return spec(array.shape)


def kernel_call(body, flags, steps, ins, outs, aliases=None, scratch=()):
    results = pl.pallas_call(
        body,
        grid_spec=pltpu.PrefetchScalarGridSpec(
            num_scalar_prefetch=1,
            grid=(steps,),
            in_specs=[s for _, s in ins],
            out_specs=[s for _, _, s in outs],
            scratch_shapes=list(scratch),
        ),
        out_shape=[jax.ShapeDtypeStruct(shape, dtype) for shape, dtype, _ in outs],
        input_output_aliases=aliases or {},
        compiler_params=PARAMS,
        cost_estimate=FREE,
    )(flags, *[array for array, _ in ins])
    return list(results)


def pick(flag, size):
    return pl.multiple_of(flag * size, GROUP)


def blocks_from(at, choice=None):
    if choice is None:
        return lambda k, flags: k + flags[at]
    return lambda k, flags: jnp.where(flags[MIDDLE] == choice, k, 0) + flags[at]


def choice_of(options, index):
    return None if len(options) == 1 else index


def left_terms(flags, rows, slots, block, steps, at=START, before=None, last=True):
    many = len(slots)
    choices = [len(slot) for slot in slots]
    tall = rows[0].shape[0]
    size = 2 * tall

    def body(flag_ref, first_ref, second_ref, *refs):
        slots_in = []
        for count in choices:
            slots_in.append(refs[:count])
            refs = refs[count:]
        if before is not None:
            before_in, refs = refs[:many], refs[many:]
        outs = refs[:many]
        step = pl.program_id(0)

        @pl.when(step == 0)
        def _():
            for index in range(many):
                outs[index][...] = jnp.zeros_like(outs[index]) if before is None else before_in[index][...]

        def add(index, ref):
            for half, row_ref in enumerate((first_ref, second_ref)):
                outs[index][half * tall : (half + 1) * tall] += dot(row_ref[...], ref[...], 1, 1)

        for index in range(many):
            if choices[index] == 1:
                add(index, slots_in[index][0])
            else:
                for choice in range(2):
                    pl.when(flag_ref[MIDDLE] == choice)(
                        functools.partial(add, index, slots_in[index][choice])
                    )

        if last:

            @pl.when(step == pl.num_programs(0) - 1)
            def _():
                gone = 1 - flag_ref[KEPT]
                levels = []
                for index in range(many):
                    part = outs[index][pl.ds(pick(gone, tall), tall), :]
                    levels += pack(part, refs[many], index * tall)
                put_levels(levels, refs[many], many * tall)

    ins = [(part, spec((tall, block), blocks_from(at))) for part in rows]
    for slot in slots:
        ins += [
            (array, spec((tall, block), blocks_from(start, choice_of(slot, index))))
            for index, (array, start) in enumerate(slot)
        ]
    if before is not None:
        ins += [(part, whole(part)) for part in before]
    outs = [((size, tall), jnp.float32, spec((size, tall)))] * many
    if last:
        shape = (many * tall + LEVELS, tall)
        outs.append((shape, jnp.int16, spec(shape)))
    return kernel_call(body, flags, steps, ins, outs)


def right_terms(flags, strips, columns, block, steps, at=START, before=None, last=False):
    wide = block * steps
    rows, strip = strips[0].shape
    many = len(strips)

    def body(flag_ref, *refs):
        strips_in, refs = refs[:many], refs[many:]
        columns_in = []
        for choice in columns:
            columns_in.append(refs[: len(choice)])
            refs = refs[len(choice) :]
        if before is not None:
            before_in, refs = refs[0], refs[1:]
        outs, turned = refs[:-1], refs[-1]

        @pl.when(pl.program_id(0) == 0)
        def _():
            for index in range(many):
                turned[index] = strips_in[index][...].T

        def add(choice):
            total = None if before is None else before_in[...]
            for index in range(many):
                refs_here = columns_in[index]
                ref = refs_here[choice if len(refs_here) == 2 else 0]
                term = dot(turned[index], ref[...], 1, 0)
                total = term if total is None else total + term
            outs[0][...] = total

        if max(len(choice) for choice in columns) == 1:
            add(0)
        else:
            for choice in range(2):
                pl.when(flag_ref[MIDDLE] == choice)(functools.partial(add, choice))
        if last:
            put_levels(pack(outs[0][...], outs[1], 0), outs[1], strip)

    here = lambda k, flags: k
    ins = [(part, whole(part)) for part in strips]
    for choice in columns:
        ins += [
            (array, spec((rows, block), blocks_from(start, choice_of(choice, index))))
            for index, (array, start) in enumerate(choice)
        ]
    if before is not None:
        ins.append((before, spec((strip, block), blocks_from(at))))
    outs = [((strip, wide), jnp.float32, spec((strip, block), here))]
    if last:
        outs.append(((strip + LEVELS, wide), jnp.int16, spec((strip + LEVELS, block), here)))
    scratch = [pltpu.VMEM((many, strip, rows), jnp.bfloat16)]
    return kernel_call(body, flags, steps, ins, outs, scratch=scratch)


def add_up(flags, products, coded):
    rows, wide = products[0].shape[0] // 2, products[0].shape[1]
    many = len(products)

    def body(flag_ref, *refs):
        coded_ref, total_ref, out_ref = refs[many:]
        levels = []
        for index in range(many):
            kept = refs[index][pl.ds(pick(flag_ref[KEPT], rows), rows), :]
            total = kept + unpack(coded_ref, index, rows, many)
            total_ref[index * rows : (index + 1) * rows] = total
            levels += pack(total, out_ref, index * rows)
        put_levels(levels, out_ref, many * rows)

    ins = [(array, whole(array)) for array in list(products) + [coded]]
    shapes = [((many * rows, wide), jnp.float32), ((many * rows + LEVELS, wide), jnp.int16)]
    return kernel_call(body, flags, 1, ins, [(s, d, spec(s)) for s, d in shapes])


def write_states(old, gram, scale, state_ref, fixed_ref, where):
    state = BETA * old + (1.0 - BETA) * gram
    state_ref[:, where] = state
    fixed_ref[:, where] = state * scale


def finish_right(flags, scale, old, value, coded, at, block, steps, written=None):
    strip, wide = old.shape

    def body(flag_ref, scale_ref, old_ref, value_ref, coded_ref, *refs):
        state_ref, fixed_ref = refs[-2:]
        everything = slice(None)

        @pl.when(flag_ref[KEPT] == 0)
        def _():
            write_states(old_ref[...], value_ref[...], scale_ref[0], state_ref, fixed_ref, everything)

        @pl.when(flag_ref[KEPT] == 1)
        def _():
            write_states(
                old_ref[...], unpack(coded_ref, 0, strip, 1), scale_ref[0], state_ref, fixed_ref, everything
            )

    here = lambda k, flags: k
    there = lambda k, flags: k + flags[at]
    ins = [
        (scale, pl.BlockSpec(memory_space=pltpu.SMEM)),
        (old, spec((strip, block), there)),
        (value, spec((strip, block), here)),
        (coded, spec((strip + LEVELS, block), here)),
    ]
    aliases = None
    if written is not None:
        ins += [(array, pl.BlockSpec(memory_space=pl.ANY)) for array in written]
        aliases = {5: 0, 6: 1}
    outs = [((strip, wide), jnp.float32, spec((strip, block), there))] * 2
    return kernel_call(body, flags, steps, ins, outs, aliases)


def finish_left(flags, scale, old, same_total, same_other, total, other, inner, written=None):
    tall, wide = total.shape
    plane = 2 * wide

    def body(flag_ref, scale_ref, old_ref, same_ref, same_other_ref, total_ref, other_ref, *refs):
        state_ref, fixed_ref = refs[-2:]

        def put(core, value):
            where = slice(core * wide, (core + 1) * wide)
            write_states(old_ref[:, where], value, scale_ref[0], state_ref, fixed_ref, where)

        is_mate = 1 - flag_ref[MIDDLE] if inner else flag_ref[MIDDLE]
        for core in range(2):
            mine = flag_ref[CORE] == core
            same = flag_ref[SAME_HALF] == 1

            @pl.when(mine & same)
            def _():
                put(core, same_ref[pl.ds(pick(is_mate, tall), tall), :])

            @pl.when(mine & jnp.logical_not(same))
            def _():
                put(core, total_ref[...])

            for index in range(2):

                @pl.when(jnp.logical_not(mine) & same & (is_mate == index))
                def _():
                    put(core, unpack(same_other_ref, index, tall, 2))

            @pl.when(jnp.logical_not(mine) & jnp.logical_not(same))
            def _():
                put(core, unpack(other_ref, 0, tall, 1))

    there = (lambda k, flags: 1 - flags[CORE]) if inner else (lambda k, flags: flags[CORE])
    ins = [(scale, pl.BlockSpec(memory_space=pltpu.SMEM)), (old, spec((tall, plane), there))]
    ins += [(array, whole(array)) for array in (same_total, same_other, total, other)]
    aliases = None
    if written is not None:
        ins += [(array, pl.BlockSpec(memory_space=pl.ANY)) for array in written]
        aliases = {7: 0, 8: 1}
    outs = [(old.shape, jnp.float32, spec((tall, plane), there))] * 2
    return kernel_call(body, flags, 1, ins, outs, aliases)


def dot(a, b, a_dim, b_dim):
    return lax.dot_general(
        a, b, (((a_dim,), (b_dim,)), ((), ())), preferred_element_type=jnp.float32
    )


AXES = ("row", "col")
CHIPS = [(z, y) for z in range(4) for y in range(2)]


def at(z, y, c):
    return (z * 2 + y) * 2 + c


def send(value, rule):
    pairs = []
    for z, y in CHIPS:
        for c in range(2):
            dest = rule(z, y, c)
            if dest is not None:
                pairs.append((at(z, y, c), at(*dest)))
    return lax.ppermute(value, AXES, pairs)


def middle(z):
    return z in (1, 2)


def to_line(z, y, c):
    return (z, c, y) if c != y else None


def pair_line(z, y, c):
    return (z ^ 1, c, y)


def across_line(z, y, c):
    return (3 - z, c, y) if middle(z) else None


def across(z, y, c):
    return (3 - z, y, c) if middle(z) else None


def outward(z, y, c):
    return (z ^ 1, y, c) if middle(z) else None


def beside(z, y, c):
    return (z, y, 1 - c)


def other_y(z, y, c):
    return (z, 1 - y, c)


def to_home(z, y, c):
    return (z, y, 1 - c) if c != z // 2 else None


def to_away(z, y, c):
    return (z, y, 1 - c) if c == z // 2 else None


def line_gather(gradient, left_old, right_old, left_counts, right_counts):
    tile_rows, half_wide = gradient.shape
    block = half_wide // 4
    strip = half_wide // 8
    my_row = lax.axis_index("row")
    c = lax.axis_index("col")
    z, y = my_row // 2, my_row % 2
    side = (z >= 2).astype(jnp.int32)
    is_middle = (z == 1) | (z == 2)
    straight = c == y
    flags = jnp.stack(
        [
            jnp.where(straight, 0, 1),
            0,
            2 * side,
            2 * (1 - side),
            2 * (1 - side) + 1,
            (c == side).astype(jnp.int32),
            is_middle.astype(jnp.int32),
            c,
        ]
    ).astype(jnp.int32)
    strip_at = (2 * z + c) * strip

    def tie(*values):
        return lax.optimization_barrier(tuple(values))

    def columns(value, first, count):
        return lax.dynamic_slice_in_dim(value, first * block, count * block, 1)

    def strips_of(pair, first=0):
        return [lax.dynamic_slice_in_dim(part, strip_at - first, strip, 1) for part in pair]

    def one(array, at=START):
        return [(array, at)]

    mate = send(gradient, pair_line)
    cross = send(gradient, across_line)
    gradient_t, mate, cross = tie(gradient, mate, cross)
    far = send(mate, across)
    near = send(cross, outward)
    swapped = send(gradient_t, to_line)
    mates = (mate, send(mate, beside))
    cross_o = send(cross, beside)
    mine = jnp.where(straight, gradient, swapped)
    half = half_wide // 2
    own = (
        mine,
        jnp.concatenate([send(mine[:, :half], beside), send(mine[:, half:], beside)], 1),
    )
    own_product, mate_product, same_coded = left_terms(
        flags, own, [one(mine), one(mate)], half, 2
    )
    same_products = [own_product, mate_product]
    same_got = send(same_coded, other_y)

    same_coded, near, far, cross_o = tie(same_coded, near, far, cross_o)
    end_home = send(columns(far, 2 * side, 2), outward)
    near_o = send(near, beside)
    far_o = send(far, beside)
    near_product, near_coded = left_terms(
        flags, own, [[(near, START), (cross, START)]], half, 2
    )
    near_got = send(near_coded, other_y)
    near_coded, near_o, own_o, mate_o = tie(near_coded, near_o, own[1], mates[1])
    own, mates = (mine, own_o), (mate, mate_o)
    near_strips = strips_of((jnp.where(is_middle, cross, near), jnp.where(is_middle, cross_o, near_o)))
    [right] = right_terms(
        flags,
        strips_of(own) + strips_of(mates) + near_strips,
        [one(part) for part in own + mates]
        + [[(near, START), (cross, START)], [(near_o, START), (cross_o, START)]],
        block,
        4,
    )
    same_got, right = tie(same_got, right)
    same_total, same_out = add_up(flags, same_products, same_got)
    same_other = send(same_out, to_home)

    right, same_out, end_home, far_o = tie(right, same_out, end_home, far_o)
    far, end_home = tie(far, end_home)
    end_first = send(columns(far, 2 * (1 - side), 1), outward)
    far_next, _ = tie(far, end_first)
    end_last = send(columns(far_next, 2 * (1 - side) + 1, 1), outward)
    end_home_o = send(end_home, beside)
    strips = [
        jnp.where(is_middle, strips_of([a])[0], strips_of([b], 2 * side * block)[0])
        for a, b in ((far, end_home), (far_o, end_home_o))
    ]
    right_home, home_coded = right_terms(
        flags,
        strips,
        [[(end_home, START), (far, HOME)], [(end_home_o, START), (far_o, HOME)]],
        block,
        2,
        at=HOME,
        before=right,
        last=True,
    )
    home_got = send(home_coded, to_line)
    home_coded, end_home = tie(home_coded, end_home)
    [far_product] = left_terms(
        flags, own, [[(end_home, START), (far, HOME)]], block, 2, at=HOME, last=False
    )

    def quarter(end, at, far_product, last):
        end_o = send(end, beside)
        lefts = left_terms(
            flags, own, [[(end, START), (far, at)]], block, 1, at=at, before=[far_product], last=last
        )
        value, coded = right_terms(
            flags,
            strips,
            [[(end, START), (far, at)], [(end_o, START), (far_o, at)]],
            block,
            1,
            at=at,
            before=right,
            last=True,
        )
        return lefts, value, coded

    left_scale = 1.0 / denominator(left_counts).reshape(1)
    right_scale = 1.0 / denominator(right_counts)
    old = right_old[0]
    far_product, end_first = tie(far_product, end_first)
    [far_product], right_first, first_coded = quarter(end_first, AWAY, far_product, False)
    first_got = send(first_coded, to_line)
    first_coded, near_got = tie(first_coded, near_got)
    near_total, near_out = add_up(flags, [near_product], near_got)
    near_other = send(near_out, to_away)
    near_out, home_got = tie(near_out, home_got)
    right_done = finish_right(flags, right_scale, old, right_home, home_got, HOME, block, 2)
    right_done[0], near_other, same_other, first_got = tie(
        right_done[0], near_other, same_other, first_got
    )
    left_done = finish_left(
        flags, left_scale, left_old, same_total, same_other, near_total, near_other, True
    )

    left_done[0], far_product, end_last = tie(left_done[0], far_product, end_last)
    [far_product, far_coded], right_last, last_coded = quarter(end_last, LAST, far_product, True)
    far_got = send(far_coded, other_y)
    last_got = send(last_coded, to_line)
    last_coded, first_got = tie(last_coded, first_got)
    right_done = finish_right(
        flags, right_scale, old, right_first, first_got, AWAY, block, 1, right_done
    )
    right_done[0], far_got = tie(right_done[0], far_got)
    far_total, far_out = add_up(flags, [far_product], far_got)
    far_other = send(far_out, to_away)
    far_out, last_got = tie(far_out, last_got)
    right_state, right_fixed = finish_right(
        flags, right_scale, old, right_last, last_got, LAST, block, 1, right_done
    )
    far_other, right_state = tie(far_other, right_state)
    left_state, left_fixed = finish_left(
        flags, left_scale, left_old, same_total, same_other, far_total, far_other, False, left_done
    )
    return (left_state, left_fixed, right_state[None], right_fixed[None])


def solution(mesh):
    local = line_gather if mesh.shape["row"] == 8 else ring
    return jax.shard_map(
        local,
        mesh=mesh,
        in_specs=(
            P(("groups", "row"), "col"),
            P(("groups", "row"), "col"),
            P(("groups", "col"), "row", None),
            P(("groups", "row"), "col"),
            P(("groups", "col")),
        ),
        out_specs=(
            P(("groups", "row"), "col"),
            P(("groups", "row"), "col"),
            P(("groups", "col"), "row", None),
            P(("groups", "col"), "row", None),
        ),
        check_vma=False,
    )
```

```python
import functools
import math

import jax
import jax.numpy as jnp
from jax import lax
from jax.experimental import pallas as pl
from jax.experimental.pallas import tpu as pltpu
from jax.sharding import PartitionSpec as P

BETA = 0.9


def denominator(counters):
    decay_power = jnp.power(jnp.float32(BETA), (counters + 1).astype(jnp.float32))
    return 1.0 - decay_power


def ring_order(count):
    if count == 8:
        return [0, 2, 4, 6, 7, 5, 3, 1]
    return list(range(count))


def ring(gradient, left_old, right_old, left_counts, right_counts):
    tile_rows, half_wide = gradient.shape
    count = lax.axis_size("row")
    strip_wide = half_wide // count
    order = ring_order(count)
    place = {row: at for at, row in enumerate(order)}
    my_row = lax.axis_index("row")
    my_col = lax.axis_index("col")
    up = [(order[at], order[(at + 1) % count]) for at in range(count)]
    down = [(dest, source) for source, dest in up]
    piece = tile_rows // 2
    strip_at = my_row * strip_wide

    state = {"left": jnp.zeros((tile_rows, count * tile_rows), jnp.float32), "right": None}

    def consume(part, step, offset):
        sources = [order[(place[row] - step) % count] for row in range(count)]
        source = jnp.asarray(sources, jnp.int32)[my_row]
        product = lax.dot_general(
            gradient, part, (((1,), (1,)), ((), ())), preferred_element_type=jnp.float32
        )
        pairs = []
        for row in range(count):
            keeper = sources[row] * 2 // count
            pairs.append((row * 2 + 1 - keeper, row * 2 + keeper))
        other = lax.ppermute(product, ("row", "col"), pairs)
        state["left"] = lax.dynamic_update_slice(
            state["left"], product + other, (0, source * tile_rows + offset)
        )
        strip = lax.dynamic_slice_in_dim(part, strip_at, strip_wide, 1)
        term = lax.dot_general(
            strip, part, (((0,), (0,)), ((), ())), preferred_element_type=jnp.float32
        )
        state["right"] = term if state["right"] is None else state["right"] + term

    halves = [gradient[:piece], gradient[piece:]]
    going_up = list(halves)
    going_down = list(halves)
    last = count // 2
    for step in range(1, last + 1):
        if step < last:
            going_up = [lax.ppermute(part, "row", up) for part in going_up]
            going_down = [lax.ppermute(part, "row", down) for part in going_down]
        else:
            going_up = [lax.ppermute(going_up[0], "row", up)]
            going_down = [lax.ppermute(going_down[1], "row", down)]
        if step == 1:
            consume(halves[0], 0, 0)
            consume(halves[1], 0, piece)
        if step < last:
            for at in range(2):
                consume(going_up[at], step, at * piece)
                consume(going_down[at], -step, at * piece)
        else:
            consume(going_up[0], step, 0)
            consume(going_down[0], step, piece)

    width = count * tile_rows // 2
    gram_left = lax.dynamic_slice_in_dim(state["left"], my_col * width, width, 1)
    left_state = BETA * left_old + (1.0 - BETA) * gram_left
    left_fixed = left_state / denominator(left_counts)
    right_state = BETA * right_old + (1.0 - BETA) * state["right"][None]
    right_fixed = right_state / denominator(right_counts)[:, None, None]
    return (left_state, left_fixed, right_state, right_fixed)


GROUP = 64
LEVELS = 16


def pack(values, out_ref, at):
    levels = []
    for first in range(0, values.shape[0], GROUP):
        block = values[first : first + GROUP]
        most = jnp.maximum(jnp.max(jnp.abs(block), axis=0, keepdims=True), 1e-34)
        level = jnp.ceil(jnp.log2(most) * 256.0)
        inverse = 32767.0 * jnp.exp2(level * (-1.0 / 256.0))
        coded = jnp.clip(jnp.round(block * inverse), -32767.0, 32767.0)
        out_ref[at + first : at + first + GROUP] = coded.astype(jnp.int32).astype(jnp.int16)
        levels.append(level)
    return levels


def put_levels(levels, out_ref, at):
    levels = levels + [jnp.zeros_like(levels[0])] * (LEVELS - len(levels))
    out_ref[at : at + LEVELS] = jnp.concatenate(levels, 0).astype(jnp.int32).astype(jnp.int16)


def unpack(ref, index, rows, many):
    level = ref[many * rows : many * rows + LEVELS].astype(jnp.int32).astype(jnp.float32)
    step = jnp.exp2(level * (1.0 / 256.0)) * (1.0 / 32767.0)
    parts = []
    for group in range(rows // GROUP):
        at = index * rows + group * GROUP
        row = index * (rows // GROUP) + group
        block = ref[at : at + GROUP].astype(jnp.int32).astype(jnp.float32)
        parts.append(block * step[row : row + 1])
    return jnp.concatenate(parts, 0)


def decode(coded, rows):
    wide = coded.shape[1]
    level = coded[rows : rows + rows // GROUP].astype(jnp.float32)
    step = jnp.exp2(level * (1.0 / 256.0)) * (1.0 / 32767.0)
    grouped = coded[:rows].astype(jnp.float32).reshape(rows // GROUP, GROUP, wide)
    return (grouped * step[:, None, :]).reshape(rows, wide)


PARAMS = pltpu.CompilerParams(vmem_limit_bytes=48 * 2**20)
FREE = pl.CostEstimate(flops=1, bytes_accessed=1, transcendentals=0)
KEPT, START, NEXT, HOME, AWAY, LAST, SAME_HALF, MIDDLE, CORE = range(9)


def spec(shape, index=None):
    if index is None:
        return pl.BlockSpec(shape, lambda k, flags: (0, 0))
    return pl.BlockSpec(shape, lambda k, flags: (0, index(k, flags)))


def whole(array):
    return spec(array.shape)


def kernel_call(body, flags, steps, ins, outs, aliases=None, scratch=()):
    results = pl.pallas_call(
        body,
        grid_spec=pltpu.PrefetchScalarGridSpec(
            num_scalar_prefetch=1,
            grid=(steps,),
            in_specs=[s for _, s in ins],
            out_specs=[s for _, _, s in outs],
            scratch_shapes=list(scratch),
        ),
        out_shape=[jax.ShapeDtypeStruct(shape, dtype) for shape, dtype, _ in outs],
        input_output_aliases=aliases or {},
        compiler_params=PARAMS,
        cost_estimate=FREE,
    )(flags, *[array for array, _ in ins])
    return list(results)


def pick(flag, size):
    return pl.multiple_of(flag * size, GROUP)


def blocks_from(at, choice=None):
    if choice is None:
        return lambda k, flags: k + flags[at]
    return lambda k, flags: jnp.where(flags[MIDDLE] == choice, k, 0) + flags[at]


def choice_of(options, index):
    return None if len(options) == 1 else index


def left_terms(flags, rows, slots, block, steps, at=START, before=None, last=True):
    many = len(slots)
    choices = [len(slot) for slot in slots]
    tall = rows[0].shape[0]
    size = 2 * tall

    def body(flag_ref, first_ref, second_ref, *refs):
        slots_in = []
        for count in choices:
            slots_in.append(refs[:count])
            refs = refs[count:]
        if before is not None:
            before_in, refs = refs[:many], refs[many:]
        outs = refs[:many]
        step = pl.program_id(0)

        @pl.when(step == 0)
        def _():
            for index in range(many):
                outs[index][...] = jnp.zeros_like(outs[index]) if before is None else before_in[index][...]

        def add(index, ref):
            for half, row_ref in enumerate((first_ref, second_ref)):
                outs[index][half * tall : (half + 1) * tall] += dot(row_ref[...], ref[...], 1, 1)

        for index in range(many):
            if choices[index] == 1:
                add(index, slots_in[index][0])
            else:
                for choice in range(2):
                    pl.when(flag_ref[MIDDLE] == choice)(
                        functools.partial(add, index, slots_in[index][choice])
                    )

        if last:

            @pl.when(step == pl.num_programs(0) - 1)
            def _():
                gone = 1 - flag_ref[KEPT]
                levels = []
                for index in range(many):
                    part = outs[index][pl.ds(pick(gone, tall), tall), :]
                    levels += pack(part, refs[many], index * tall)
                put_levels(levels, refs[many], many * tall)

    ins = [(part, spec((tall, block), blocks_from(at))) for part in rows]
    for slot in slots:
        ins += [
            (array, spec((tall, block), blocks_from(start, choice_of(slot, index))))
            for index, (array, start) in enumerate(slot)
        ]
    if before is not None:
        ins += [(part, whole(part)) for part in before]
    outs = [((size, tall), jnp.float32, spec((size, tall)))] * many
    if last:
        shape = (many * tall + LEVELS, tall)
        outs.append((shape, jnp.int16, spec(shape)))
    return kernel_call(body, flags, steps, ins, outs)


def right_terms(flags, strips, columns, block, steps, at=START, before=None, last=False):
    wide = block * steps
    rows, strip = strips[0].shape
    many = len(strips)

    def body(flag_ref, *refs):
        strips_in, refs = refs[:many], refs[many:]
        columns_in = []
        for choice in columns:
            columns_in.append(refs[: len(choice)])
            refs = refs[len(choice) :]
        if before is not None:
            before_in, refs = refs[0], refs[1:]
        outs, turned = refs[:-1], refs[-1]

        @pl.when(pl.program_id(0) == 0)
        def _():
            for index in range(many):
                turned[index] = strips_in[index][...].T

        def add(choice):
            total = None if before is None else before_in[...]
            for index in range(many):
                refs_here = columns_in[index]
                ref = refs_here[choice if len(refs_here) == 2 else 0]
                term = dot(turned[index], ref[...], 1, 0)
                total = term if total is None else total + term
            outs[0][...] = total

        if max(len(choice) for choice in columns) == 1:
            add(0)
        else:
            for choice in range(2):
                pl.when(flag_ref[MIDDLE] == choice)(functools.partial(add, choice))
        if last:
            put_levels(pack(outs[0][...], outs[1], 0), outs[1], strip)

    here = lambda k, flags: k
    ins = [(part, whole(part)) for part in strips]
    for choice in columns:
        ins += [
            (array, spec((rows, block), blocks_from(start, choice_of(choice, index))))
            for index, (array, start) in enumerate(choice)
        ]
    if before is not None:
        ins.append((before, spec((strip, block), blocks_from(at))))
    outs = [((strip, wide), jnp.float32, spec((strip, block), here))]
    if last:
        outs.append(((strip + LEVELS, wide), jnp.int16, spec((strip + LEVELS, block), here)))
    scratch = [pltpu.VMEM((many, strip, rows), jnp.bfloat16)]
    return kernel_call(body, flags, steps, ins, outs, scratch=scratch)


def add_up(flags, products, coded):
    rows, wide = products[0].shape[0] // 2, products[0].shape[1]
    many = len(products)

    def body(flag_ref, *refs):
        coded_ref, total_ref, out_ref = refs[many:]
        levels = []
        for index in range(many):
            kept = refs[index][pl.ds(pick(flag_ref[KEPT], rows), rows), :]
            total = kept + unpack(coded_ref, index, rows, many)
            total_ref[index * rows : (index + 1) * rows] = total
            levels += pack(total, out_ref, index * rows)
        put_levels(levels, out_ref, many * rows)

    ins = [(array, whole(array)) for array in list(products) + [coded]]
    shapes = [((many * rows, wide), jnp.float32), ((many * rows + LEVELS, wide), jnp.int16)]
    return kernel_call(body, flags, 1, ins, [(s, d, spec(s)) for s, d in shapes])


def write_states(old, gram, scale, state_ref, fixed_ref, where):
    state = BETA * old + (1.0 - BETA) * gram
    state_ref[:, where] = state
    fixed_ref[:, where] = state * scale


def finish_right(flags, scale, old, value, coded, at, block, steps, written=None):
    strip, wide = old.shape

    def body(flag_ref, scale_ref, old_ref, value_ref, coded_ref, *refs):
        state_ref, fixed_ref = refs[-2:]
        everything = slice(None)

        @pl.when(flag_ref[KEPT] == 0)
        def _():
            write_states(old_ref[...], value_ref[...], scale_ref[0], state_ref, fixed_ref, everything)

        @pl.when(flag_ref[KEPT] == 1)
        def _():
            write_states(
                old_ref[...], unpack(coded_ref, 0, strip, 1), scale_ref[0], state_ref, fixed_ref, everything
            )

    part = math.gcd(block * steps, 256)
    there = lambda k, flags: k + flags[at] * block // part
    ins = [
        (scale, pl.BlockSpec(memory_space=pltpu.SMEM)),
        (old, spec((strip, part), there)),
        (value, spec((strip, part), lambda k, flags: k * (1 - flags[KEPT]))),
        (coded, spec((strip + LEVELS, part), lambda k, flags: k * flags[KEPT])),
    ]
    aliases = None
    if written is not None:
        ins += [(array, pl.BlockSpec(memory_space=pl.ANY)) for array in written]
        aliases = {5: 0, 6: 1}
    outs = [((strip, wide), jnp.float32, spec((strip, part), there))] * 2
    return kernel_call(body, flags, steps * block // part, ins, outs, aliases)


def finish_left(flags, scale, old, same_total, same_other, total, other, inner, written=None):
    tall, wide = total.shape

    def body(flag_ref, scale_ref, old_ref, same_ref, same_other_ref, total_ref, other_ref, *refs):
        state_ref, fixed_ref = refs[-2:]

        def put(value):
            write_states(old_ref[...], value, scale_ref[0], state_ref, fixed_ref, slice(None))

        is_mate = 1 - flag_ref[MIDDLE] if inner else flag_ref[MIDDLE]
        mine = flag_ref[CORE] == pl.program_id(0)
        same = flag_ref[SAME_HALF] == 1

        @pl.when(mine & same)
        def _():
            put(same_ref[pl.ds(pick(is_mate, tall), tall), :])

        @pl.when(mine & jnp.logical_not(same))
        def _():
            put(total_ref[...])

        for index in range(2):

            @pl.when(jnp.logical_not(mine) & same & (is_mate == index))
            def _():
                put(unpack(same_other_ref, index, tall, 2))

        @pl.when(jnp.logical_not(mine) & jnp.logical_not(same))
        def _():
            put(unpack(other_ref, 0, tall, 1))

    there = lambda k, flags: 2 * (1 - flags[CORE] if inner else flags[CORE]) + k
    ins = [(scale, pl.BlockSpec(memory_space=pltpu.SMEM)), (old, spec((tall, wide), there))]
    ins += [(array, whole(array)) for array in (same_total, same_other, total, other)]
    aliases = None
    if written is not None:
        ins += [(array, pl.BlockSpec(memory_space=pl.ANY)) for array in written]
        aliases = {7: 0, 8: 1}
    outs = [(old.shape, jnp.float32, spec((tall, wide), there))] * 2
    return kernel_call(body, flags, 2, ins, outs, aliases)


def dot(a, b, a_dim, b_dim):
    return lax.dot_general(
        a, b, (((a_dim,), (b_dim,)), ((), ())), preferred_element_type=jnp.float32
    )


AXES = ("row", "col")
CHIPS = [(z, y) for z in range(4) for y in range(2)]


def at(z, y, c):
    return (z * 2 + y) * 2 + c


def send(value, rule):
    pairs = []
    for z, y in CHIPS:
        for c in range(2):
            dest = rule(z, y, c)
            if dest is not None:
                pairs.append((at(z, y, c), at(*dest)))
    return lax.ppermute(value, AXES, pairs)


def middle(z):
    return z in (1, 2)


def to_line(z, y, c):
    return (z, c, y) if c != y else None


def pair_line(z, y, c):
    return (z ^ 1, c, y)


def across_line(z, y, c):
    return (3 - z, c, y) if middle(z) else None


def across(z, y, c):
    return (3 - z, y, c) if middle(z) else None


def outward(z, y, c):
    return (z ^ 1, y, c) if middle(z) else None


def beside(z, y, c):
    return (z, y, 1 - c)


def other_y(z, y, c):
    return (z, 1 - y, c)


def to_home(z, y, c):
    return (z, y, 1 - c) if c != z // 2 else None


def to_away(z, y, c):
    return (z, y, 1 - c) if c == z // 2 else None


def line_gather(gradient, left_old, right_old, left_counts, right_counts):
    tile_rows, half_wide = gradient.shape
    block = half_wide // 4
    strip = half_wide // 8
    my_row = lax.axis_index("row")
    c = lax.axis_index("col")
    z, y = my_row // 2, my_row % 2
    side = (z >= 2).astype(jnp.int32)
    is_middle = (z == 1) | (z == 2)
    straight = c == y
    flags = jnp.stack(
        [
            jnp.where(straight, 0, 1),
            0,
            1,
            2 * side,
            2 * (1 - side),
            2 * (1 - side) + 1,
            (c == side).astype(jnp.int32),
            is_middle.astype(jnp.int32),
            c,
        ]
    ).astype(jnp.int32)
    strip_at = (2 * z + c) * strip

    def tie(*values):
        return lax.optimization_barrier(tuple(values))

    def columns(value, first, count):
        return lax.dynamic_slice_in_dim(value, first * block, count * block, 1)

    def strips_of(pair, first=0):
        return [lax.dynamic_slice_in_dim(part, strip_at - first, strip, 1) for part in pair]

    def one(array, at=START):
        return [(array, at)]

    mate = send(gradient, pair_line)
    cross = send(gradient, across_line)
    gradient_t, mate, cross = tie(gradient, mate, cross)
    far = send(mate, across)
    near = send(cross, outward)
    swapped = send(gradient_t, to_line)
    mates = (mate, send(mate, beside))
    crosses = (cross, send(cross, beside))
    [right] = right_terms(
        flags,
        strips_of(mates) + strips_of(crosses),
        [one(part) for part in mates + crosses],
        block,
        4,
    )
    right, swapped = tie(right, swapped)
    mine = jnp.where(straight, gradient, swapped)
    half = half_wide // 2
    own = (
        mine,
        jnp.concatenate([send(mine[:, :half], beside), send(mine[:, half:], beside)], 1),
    )
    own_product, mate_product, same_coded = left_terms(
        flags, own, [one(mine), one(mate)], half, 2
    )
    same_products = [own_product, mate_product]
    same_got = send(same_coded, other_y)
    same_coded, own_o = tie(same_coded, own[1])
    own = (mine, own_o)
    [right] = right_terms(
        flags, strips_of(own), [one(part) for part in own], block, 4, before=right
    )

    right, near, far = tie(right, near, far)
    end_home = send(columns(far, 2 * side, 2), outward)
    nears = (near, send(near, beside))
    far_o = send(far, beside)
    near_product, near_coded = left_terms(
        flags, own, [[(near, START), (cross, START)]], half, 2
    )
    near_got = send(near_coded, other_y)
    near_coded, near, near_o = tie(near_coded, *nears)
    nears = (near, near_o)
    [right] = right_terms(
        flags, strips_of(nears), [one(part) for part in nears], block, 4, before=right
    )
    same_got, right = tie(same_got, right)
    same_total, same_out = add_up(flags, same_products, same_got)
    same_other = send(same_out, to_home)
    same_out, near_got = tie(same_out, near_got)
    near_total, near_out = add_up(flags, [near_product], near_got)
    near_other = send(near_out, to_away)

    right, near_out, end_home, far_o = tie(right, near_out, end_home, far_o)
    far, end_home = tie(far, end_home)
    end_away = send(columns(far, 2 * (1 - side), 2), outward)
    end_home_o = send(end_home, beside)
    strips = [
        jnp.where(is_middle, strips_of([a])[0], strips_of([b], 2 * side * block)[0])
        for a, b in ((far, end_home), (far_o, end_home_o))
    ]

    def last_right(end, end_o, start, at, steps):
        return right_terms(
            flags,
            strips,
            [[(end, start), (far, at)], [(end_o, start), (far_o, at)]],
            block,
            steps,
            at=at,
            before=right,
            last=True,
        )

    right_home, home_coded = last_right(end_home, end_home_o, START, HOME, 2)
    home_got = send(home_coded, to_line)
    home_coded, end_home = tie(home_coded, end_home)
    [far_product] = left_terms(
        flags, own, [[(end_home, START), (far, HOME)]], block, 2, at=HOME, last=False
    )
    left_scale = 1.0 / denominator(left_counts).reshape(1)
    right_scale = 1.0 / denominator(right_counts)
    old = right_old[0]
    far_product, near_other, same_other = tie(far_product, near_other, same_other)
    left_done = finish_left(
        flags, left_scale, left_old, same_total, same_other, near_total, near_other, True
    )
    left_done[0], home_got = tie(left_done[0], home_got)
    right_done = finish_right(flags, right_scale, old, right_home, home_got, HOME, block, 2)

    right_done[0], far_product, end_away = tie(right_done[0], far_product, end_away)
    end_away_o = send(end_away, beside)
    far_product, far_coded = left_terms(
        flags, own, [[(end_away, START), (far, AWAY)]], block, 2, at=AWAY, before=[far_product]
    )
    far_got = send(far_coded, other_y)
    far_coded, end_away_o = tie(far_coded, end_away_o)
    right_away, away_coded = last_right(end_away, end_away_o, START, AWAY, 1)
    away_got = send(away_coded, to_line)
    away_coded, end_away_o = tie(away_coded, end_away_o)
    right_last, last_coded = last_right(end_away, end_away_o, NEXT, LAST, 1)
    last_got = send(last_coded, to_line)
    last_coded, far_got = tie(last_coded, far_got)
    far_total, far_out = add_up(flags, [far_product], far_got)
    far_other = send(far_out, to_away)
    far_out, away_got = tie(far_out, away_got)
    right_done = finish_right(
        flags, right_scale, old, right_away, away_got, AWAY, block, 1, right_done
    )
    right_done[0], far_other = tie(right_done[0], far_other)
    left_state, left_fixed = finish_left(
        flags, left_scale, left_old, same_total, same_other, far_total, far_other, False, left_done
    )
    left_state, last_got = tie(left_state, last_got)
    right_state, right_fixed = finish_right(
        flags, right_scale, old, right_last, last_got, LAST, block, 1, right_done
    )
    return (left_state, left_fixed, right_state[None], right_fixed[None])


def solution(mesh):
    local = line_gather if mesh.shape["row"] == 8 else ring
    return jax.shard_map(
        local,
        mesh=mesh,
        in_specs=(
            P(("groups", "row"), "col"),
            P(("groups", "row"), "col"),
            P(("groups", "col"), "row", None),
            P(("groups", "row"), "col"),
            P(("groups", "col")),
        ),
        out_specs=(
            P(("groups", "row"), "col"),
            P(("groups", "row"), "col"),
            P(("groups", "col"), "row", None),
            P(("groups", "col"), "row", None),
        ),
        check_vma=False,
    )
```

```python
import functools
import math

import jax
import jax.numpy as jnp
from jax import lax
from jax.experimental import pallas as pl
from jax.experimental.pallas import tpu as pltpu
from jax.sharding import PartitionSpec as P

BETA = 0.9


def denominator(counters):
    decay_power = jnp.power(jnp.float32(BETA), (counters + 1).astype(jnp.float32))
    return 1.0 - decay_power


def ring_order(count):
    if count == 8:
        return [0, 2, 4, 6, 7, 5, 3, 1]
    return list(range(count))


def ring(gradient, left_old, right_old, left_counts, right_counts):
    tile_rows, half_wide = gradient.shape
    count = lax.axis_size("row")
    strip_wide = half_wide // count
    order = ring_order(count)
    place = {row: at for at, row in enumerate(order)}
    my_row = lax.axis_index("row")
    my_col = lax.axis_index("col")
    up = [(order[at], order[(at + 1) % count]) for at in range(count)]
    down = [(dest, source) for source, dest in up]
    piece = tile_rows // 2
    strip_at = my_row * strip_wide

    state = {"left": jnp.zeros((tile_rows, count * tile_rows), jnp.float32), "right": None}

    def consume(part, step, offset):
        sources = [order[(place[row] - step) % count] for row in range(count)]
        source = jnp.asarray(sources, jnp.int32)[my_row]
        product = lax.dot_general(
            gradient, part, (((1,), (1,)), ((), ())), preferred_element_type=jnp.float32
        )
        pairs = []
        for row in range(count):
            keeper = sources[row] * 2 // count
            pairs.append((row * 2 + 1 - keeper, row * 2 + keeper))
        other = lax.ppermute(product, ("row", "col"), pairs)
        state["left"] = lax.dynamic_update_slice(
            state["left"], product + other, (0, source * tile_rows + offset)
        )
        strip = lax.dynamic_slice_in_dim(part, strip_at, strip_wide, 1)
        term = lax.dot_general(
            strip, part, (((0,), (0,)), ((), ())), preferred_element_type=jnp.float32
        )
        state["right"] = term if state["right"] is None else state["right"] + term

    halves = [gradient[:piece], gradient[piece:]]
    going_up = list(halves)
    going_down = list(halves)
    last = count // 2
    for step in range(1, last + 1):
        if step < last:
            going_up = [lax.ppermute(part, "row", up) for part in going_up]
            going_down = [lax.ppermute(part, "row", down) for part in going_down]
        else:
            going_up = [lax.ppermute(going_up[0], "row", up)]
            going_down = [lax.ppermute(going_down[1], "row", down)]
        if step == 1:
            consume(halves[0], 0, 0)
            consume(halves[1], 0, piece)
        if step < last:
            for at in range(2):
                consume(going_up[at], step, at * piece)
                consume(going_down[at], -step, at * piece)
        else:
            consume(going_up[0], step, 0)
            consume(going_down[0], step, piece)

    width = count * tile_rows // 2
    gram_left = lax.dynamic_slice_in_dim(state["left"], my_col * width, width, 1)
    left_state = BETA * left_old + (1.0 - BETA) * gram_left
    left_fixed = left_state / denominator(left_counts)
    right_state = BETA * right_old + (1.0 - BETA) * state["right"][None]
    right_fixed = right_state / denominator(right_counts)[:, None, None]
    return (left_state, left_fixed, right_state, right_fixed)


GROUP = 64


def level_rows(rows):
    return -(-(rows // GROUP) // 16) * 16


def pack(values, out_ref, at):
    levels = []
    for first in range(0, values.shape[0], GROUP):
        block = values[first : first + GROUP]
        most = jnp.maximum(jnp.max(jnp.abs(block), axis=0, keepdims=True), 1e-34)
        level = jnp.ceil(jnp.log2(most) * 256.0)
        inverse = 32767.0 * jnp.exp2(level * (-1.0 / 256.0))
        coded = jnp.clip(jnp.round(block * inverse), -32767.0, 32767.0)
        out_ref[at + first : at + first + GROUP] = coded.astype(jnp.int32).astype(jnp.int16)
        levels.append(level)
    return levels


def put_levels(levels, out_ref, at):
    count = out_ref.shape[0] - at
    levels = levels + [jnp.zeros_like(levels[0])] * (count - len(levels))
    out_ref[at : at + count] = jnp.concatenate(levels, 0).astype(jnp.int32).astype(jnp.int16)


def step_of(level):
    return jnp.exp2(level.astype(jnp.int32).astype(jnp.float32) * (1.0 / 256.0)) * (1.0 / 32767.0)


def unpack(ref, index, rows, many):
    step = step_of(ref[many * rows : many * rows + level_rows(many * rows)])
    parts = []
    for group in range(rows // GROUP):
        at = index * rows + group * GROUP
        row = index * (rows // GROUP) + group
        block = ref[at : at + GROUP].astype(jnp.int32).astype(jnp.float32)
        parts.append(block * step[row : row + 1])
    return jnp.concatenate(parts, 0)


PARAMS = pltpu.CompilerParams(vmem_limit_bytes=48 * 2**20)
FREE = pl.CostEstimate(flops=1, bytes_accessed=1, transcendentals=0)
KEPT, START, THIRD, SAME_HALF, MIDDLE, CORE = range(6)


def spec(shape, index=None):
    if index is None:
        return pl.BlockSpec(shape, lambda k, flags: (0, 0))
    return pl.BlockSpec(shape, lambda k, flags: (0, index(k, flags)))


def whole(array):
    return spec(array.shape)


def kernel_call(body, flags, steps, ins, outs, aliases=None, scratch=()):
    results = pl.pallas_call(
        body,
        grid_spec=pltpu.PrefetchScalarGridSpec(
            num_scalar_prefetch=1,
            grid=(steps,),
            in_specs=[s for _, s in ins],
            out_specs=[s for _, _, s in outs],
            scratch_shapes=list(scratch),
        ),
        out_shape=[jax.ShapeDtypeStruct(shape, dtype) for shape, dtype, _ in outs],
        input_output_aliases=aliases or {},
        compiler_params=PARAMS,
        cost_estimate=FREE,
    )(flags, *[array for array, _ in ins])
    return list(results)


def pick(flag, size):
    return pl.multiple_of(flag * size, GROUP)


def blocks_from(at, choice=None):
    if choice is None:
        return lambda k, flags: k + flags[at]
    return lambda k, flags: jnp.where(flags[MIDDLE] == choice, k, 0) + flags[at]


def choice_of(options, index):
    return None if len(options) == 1 else index


def left_terms(flags, rows, slots, block, steps, at=START, before=None, last=True):
    many = len(slots)
    choices = [len(slot) for slot in slots]
    tall = rows[0].shape[0]
    size = 2 * tall

    def body(flag_ref, first_ref, second_ref, *refs):
        slots_in = []
        for count in choices:
            slots_in.append(refs[:count])
            refs = refs[count:]
        if before is not None:
            before_in, refs = refs[:many], refs[many:]
        outs = refs[:many]
        step = pl.program_id(0)

        @pl.when(step == 0)
        def _():
            for index in range(many):
                outs[index][...] = jnp.zeros_like(outs[index]) if before is None else before_in[index][...]

        def add(index, ref):
            for half, row_ref in enumerate((first_ref, second_ref)):
                outs[index][half * tall : (half + 1) * tall] += dot(row_ref[...], ref[...], 1, 1)

        for index in range(many):
            if choices[index] == 1:
                add(index, slots_in[index][0])
            else:
                for choice in range(2):
                    pl.when(flag_ref[MIDDLE] == choice)(
                        functools.partial(add, index, slots_in[index][choice])
                    )

        if last:

            @pl.when(step == pl.num_programs(0) - 1)
            def _():
                gone = 1 - flag_ref[KEPT]
                levels = []
                for index in range(many):
                    part = outs[index][pl.ds(pick(gone, tall), tall), :]
                    levels += pack(part, refs[many], index * tall)
                put_levels(levels, refs[many], many * tall)

    ins = [(part, spec((tall, block), blocks_from(at))) for part in rows]
    for slot in slots:
        ins += [
            (array, spec((tall, block), blocks_from(start, choice_of(slot, index))))
            for index, (array, start) in enumerate(slot)
        ]
    if before is not None:
        ins += [(part, whole(part)) for part in before]
    outs = [((size, tall), jnp.float32, spec((size, tall)))] * many
    if last:
        shape = (many * tall + level_rows(many * tall), tall)
        outs.append((shape, jnp.int16, spec(shape)))
    return kernel_call(body, flags, steps, ins, outs)


def right_terms(flags, strips, columns, block, steps, before=None, keep=True, last=False):
    wide = block * steps
    rows, strip = strips[0].shape
    many = len(strips)

    def body(flag_ref, *refs):
        strips_in, refs = refs[:many], refs[many:]
        columns_in = []
        for choice in columns:
            columns_in.append(refs[: len(choice)])
            refs = refs[len(choice) :]
        if before is not None:
            before_in, refs = refs[0], refs[1:]
        outs, turned = refs[: keep + last], refs[keep + last]
        total_ref = outs[0] if keep else refs[-1]

        @pl.when(pl.program_id(0) == 0)
        def _():
            for index in range(many):
                turned[index] = strips_in[index][...].T

        def add(choice):
            total = None if before is None else before_in[...]
            for index in range(many):
                refs_here = columns_in[index]
                ref = refs_here[choice if len(refs_here) == 2 else 0]
                term = dot(turned[index], ref[...], 1, 0)
                total = term if total is None else total + term
            total_ref[...] = total

        if max(len(choice) for choice in columns) == 1:
            add(0)
        else:
            for choice in range(2):
                pl.when(flag_ref[MIDDLE] == choice)(functools.partial(add, choice))
        if last:
            put_levels(pack(total_ref[...], outs[-1], 0), outs[-1], strip)

    here = lambda k, flags: k
    ins = [(part, whole(part)) for part in strips]
    for choice in columns:
        ins += [
            (array, spec((rows, block), blocks_from(start, choice_of(choice, index))))
            for index, (array, start) in enumerate(choice)
        ]
    if before is not None:
        ins.append((before, spec((strip, block), here)))
    outs = [((strip, wide), jnp.float32, spec((strip, block), here))] if keep else []
    if last:
        tall = strip + level_rows(strip)
        outs.append(((tall, wide), jnp.int16, spec((tall, block), here)))
    scratch = [pltpu.VMEM((many, strip, rows), jnp.bfloat16)]
    if not keep:
        scratch.append(pltpu.VMEM((strip, block), jnp.float32))
    return kernel_call(body, flags, steps, ins, outs, scratch=scratch)


def add_up(flags, products, coded):
    rows, wide = products[0].shape[0] // 2, products[0].shape[1]
    many = len(products)

    def body(flag_ref, *refs):
        coded_ref, total_ref, out_ref = refs[many:]
        levels = []
        for index in range(many):
            kept = refs[index][pl.ds(pick(flag_ref[KEPT], rows), rows), :]
            total = kept + unpack(coded_ref, index, rows, many)
            total_ref[index * rows : (index + 1) * rows] = total
            levels += pack(total, out_ref, index * rows)
        put_levels(levels, out_ref, many * rows)

    ins = [(array, whole(array)) for array in list(products) + [coded]]
    shapes = [((many * rows, wide), jnp.float32), ((many * rows + level_rows(many * rows), wide), jnp.int16)]
    return kernel_call(body, flags, 1, ins, [(s, d, spec(s)) for s, d in shapes])


def write_states(old_ref, gram, scale_ref, state_ref, fixed_ref):
    state = BETA * old_ref[...] + (1.0 - BETA) * gram
    state_ref[...] = state
    fixed_ref[...] = state * scale_ref[0]


def outputs_of(old, block, index, written, count):
    ins, aliases = [], None
    if written is not None:
        ins = [(array, pl.BlockSpec(memory_space=pl.ANY)) for array in written]
        aliases = {count + 1: 0, count + 2: 1}
    return ins, [(old.shape, jnp.float32, pl.BlockSpec(block, index))] * 2, aliases


def finish_right(flags, scale, old, value, coded, share, half, written=None):
    strip, wide = old.shape[0], old.shape[1] // 2

    def body(flag_ref, scale_ref, old_ref, value_ref, coded_ref, level_ref, share_ref, share_level_ref, *refs):
        group = pl.program_id(0)

        def decoded(ref, levels):
            rows = lax.broadcasted_iota(jnp.int32, levels.shape, 0)
            level = jnp.sum(
                jnp.where(rows == group, levels[...].astype(jnp.int32), 0), axis=0, keepdims=True
            )
            step = jnp.exp2(level.astype(jnp.float32) * (1.0 / 256.0)) * (1.0 / 32767.0)
            return ref[...].astype(jnp.int32).astype(jnp.float32) * step

        def put(gram):
            gram = gram + decoded(share_ref, share_level_ref)
            write_states(old_ref, gram, scale_ref, *refs[-2:])

        @pl.when(flag_ref[KEPT] == 0)
        def _():
            put(value_ref[...])

        @pl.when(flag_ref[KEPT] == 1)
        def _():
            put(decoded(coded_ref, level_ref))

    rows = (GROUP, wide)
    levels = (level_rows(strip), wide)
    last = strip // level_rows(strip)
    there = lambda k, flags: (k, half)
    ins = [
        (scale, pl.BlockSpec(memory_space=pltpu.SMEM)),
        (old, pl.BlockSpec(rows, there)),
        (value, pl.BlockSpec(rows, lambda k, flags: (k * (1 - flags[KEPT]), half))),
        (coded, pl.BlockSpec(rows, lambda k, flags: (k * flags[KEPT], 0))),
        (coded, pl.BlockSpec(levels, lambda k, flags: (last, 0))),
        (share, pl.BlockSpec(rows, there)),
        (share, pl.BlockSpec(levels, lambda k, flags: (last, half))),
    ]
    more, outs, aliases = outputs_of(old, rows, there, written, len(ins))
    return kernel_call(body, flags, strip // GROUP, ins + more, outs, aliases)


def finish_left(flags, scale, old, same_total, same_other, late_total, late_other, sent, inner, written=None):
    tall, wide = late_total.shape

    def body(flag_ref, scale_ref, old_ref, same_ref, same_other_ref, late_ref, late_other_ref, *refs):
        sent_refs = refs[:2]

        def put(value):
            write_states(old_ref, value, scale_ref, *refs[-2:])

        def put_same(index, mine):
            put(same_ref[index * tall : (index + 1) * tall] if mine else unpack(same_other_ref, index, tall, 3))

        def put_late(mine):
            put(late_ref[...] if mine else unpack(late_other_ref, 0, tall, 1))

        def put_sent(mine):
            put(unpack(sent_refs[0 if mine else 1], 0, tall, 1))

        same = flag_ref[SAME_HALF] == 1
        is_middle = flag_ref[MIDDLE] == 1
        for mine in (True, False):
            here = (flag_ref[CORE] == pl.program_id(0)) == mine
            at_middle = here & is_middle
            at_end = here & jnp.logical_not(is_middle)
            other = jnp.logical_not(same)
            pl.when(at_middle & same)(functools.partial(put_same, 0 if inner else 1, mine))
            pl.when(at_end & same)(functools.partial(put_same, 1 if inner else 0, mine))
            if inner:
                pl.when(at_middle & other)(functools.partial(put_same, 2, mine))
                pl.when(at_end & other)(functools.partial(put_late, mine))
            else:
                pl.when(at_middle & other)(functools.partial(put_late, mine))
                pl.when(at_end & other)(functools.partial(put_sent, mine))

    there = lambda k, flags: (0, 2 * (1 - flags[CORE] if inner else flags[CORE]) + k)
    ins = [(scale, pl.BlockSpec(memory_space=pltpu.SMEM)), (old, pl.BlockSpec((tall, wide), there))]
    ins += [(array, whole(array)) for array in (same_total, same_other, late_total, late_other) + sent]
    more, outs, aliases = outputs_of(old, (tall, wide), there, written, len(ins))
    return kernel_call(body, flags, 2, ins + more, outs, aliases)


def dot(a, b, a_dim, b_dim):
    return lax.dot_general(
        a, b, (((a_dim,), (b_dim,)), ((), ())), preferred_element_type=jnp.float32
    )


AXES = ("row", "col")
CHIPS = [(z, y) for z in range(4) for y in range(2)]


def at(z, y, c):
    return (z * 2 + y) * 2 + c


def send(value, rule):
    pairs = []
    for z, y in CHIPS:
        for c in range(2):
            dest = rule(z, y, c)
            if dest is not None:
                pairs.append((at(z, y, c), at(*dest)))
    return lax.ppermute(value, AXES, pairs)


def middle(z):
    return z in (1, 2)


def to_line(z, y, c):
    return (z, c, y) if c != y else None


def pair_line(z, y, c):
    return (z ^ 1, c, y)


def across_line(z, y, c):
    return (3 - z, c, y) if middle(z) else None


def across(z, y, c):
    return (3 - z, y, c) if middle(z) else None


def outward(z, y, c):
    return (z ^ 1, y, c) if middle(z) else None


def beside(z, y, c):
    return (z, y, 1 - c)


def other_y(z, y, c):
    return (z, 1 - y, c)


def share_out(z, y, c):
    return (z ^ 1, c, y) if middle(z) else None


def far_straight(z, y, c):
    return (z ^ 1, y, c) if middle(z) and c != z // 2 else None


def far_cross(z, y, c):
    return (z ^ 1, y, 1 - c) if middle(z) and c == z // 2 else None


def line_gather(gradient, left_old, right_old, left_counts, right_counts):
    tile_rows, half_wide = gradient.shape
    block = half_wide // 4
    strip = half_wide // 8
    my_row = lax.axis_index("row")
    c = lax.axis_index("col")
    z, y = my_row // 2, my_row % 2
    side = (z >= 2).astype(jnp.int32)
    is_middle = (z == 1) | (z == 2)
    straight = c == y
    flags = jnp.stack(
        [
            jnp.where(straight, 0, 1),
            0,
            2,
            (c == side).astype(jnp.int32),
            is_middle.astype(jnp.int32),
            c,
        ]
    ).astype(jnp.int32)
    strip_at = (2 * z + c) * strip

    def tie(*values):
        return lax.optimization_barrier(tuple(values))

    def strips_of(pair, at=strip_at):
        return [lax.dynamic_slice_in_dim(part, at, strip, 1) for part in pair]

    def one(array, at=START):
        return [(array, at)]

    mate = send(gradient, pair_line)
    cross = send(gradient, across_line)
    gradient_t, mate, cross = tie(gradient, mate, cross)
    far = send(mate, across)
    near = send(cross, outward)
    swapped = send(gradient_t, to_line)
    mates = (mate, send(mate, beside))
    crosses = (cross, send(cross, beside))
    [right] = right_terms(
        flags,
        strips_of(mates) + strips_of(crosses),
        [one(part) for part in mates + crosses],
        block,
        4,
    )
    right, swapped = tie(right, swapped)
    mine = jnp.where(straight, gradient, swapped)
    half = half_wide // 2
    own = (
        mine,
        jnp.concatenate([send(mine[:, :half], beside), send(mine[:, half:], beside)], 1),
    )
    *same_products, same_coded = left_terms(
        flags, own, [one(mine), one(mate), one(cross)], block, 4
    )
    same_got = send(same_coded, other_y)
    same_coded, own_o = tie(same_coded, own[1])
    own = (mine, own_o)
    [right] = right_terms(
        flags, strips_of(own), [one(part) for part in own], block, 4, before=right
    )

    right, near, far = tie(right, near, far)
    far_o = send(far, beside)
    near_o = send(near, beside)
    far_product, far_coded = left_terms(flags, mates, [one(far)], half, 2)
    far_got = send(far_coded, other_y)
    end_strips = strips_of((far, far_o), (2 * (z ^ 1) + c) * strip)

    far_coded, far_o = tie(far_coded, far_o)
    [share] = right_terms(
        flags, end_strips, [one(far), one(far_o)], block, 4, keep=False, last=True
    )
    share_got = send(share, share_out)
    share, near_o = tie(share, near_o)
    late_strips = [
        jnp.where(is_middle, a, b) for a, b in zip(strips_of((far, far_o)), strips_of((near, near_o)))
    ]
    right, right_coded = right_terms(
        flags,
        late_strips,
        [[(near, START), (far, START)], [(near_o, START), (far_o, START)]],
        block,
        4,
        before=right,
        last=True,
    )
    right_got = [send(right_coded[:, :half], to_line), send(right_coded[:, half:], to_line)]
    right_coded, far_got = tie(right_coded, far_got)
    far_out = add_up(flags, [far_product], far_got)[1]
    sent = (send(far_out, far_straight), send(far_out, far_cross))
    far_out, near = tie(far_out, near)
    late_product, late_coded = left_terms(
        flags, own, [[(near, START), (far, START)]], half, 2
    )
    late_got = send(late_coded, other_y)
    late_coded, same_got = tie(late_coded, same_got)
    same_total, same_out = add_up(flags, same_products, same_got)
    same_other = send(same_out, beside)
    same_out, late_got = tie(same_out, late_got)
    late_total, late_out = add_up(flags, [late_product], late_got)
    late_other = send(late_out, beside)

    left_scale = 1.0 / denominator(left_counts).reshape(1)
    right_scale = 1.0 / denominator(right_counts)
    old = right_old[0]
    late_out, same_other, late_other = tie(late_out, same_other, late_other)
    lefts = (same_total, same_other, late_total, late_other)
    left_done = finish_left(flags, left_scale, left_old, *lefts, (), True)
    left_done[0], *sent = tie(left_done[0], *sent)
    left_state, left_fixed = finish_left(
        flags, left_scale, left_old, *lefts, tuple(sent), False, left_done
    )
    left_state, share_got, *right_got = tie(left_state, share_got, *right_got)
    right_done = finish_right(flags, right_scale, old, right, right_got[0], share_got, 0)
    right_state, right_fixed = finish_right(
        flags, right_scale, old, right, right_got[1], share_got, 1, right_done
    )
    return (left_state, left_fixed, right_state[None], right_fixed[None])


def solution(mesh):
    local = line_gather if mesh.shape["row"] == 8 else ring
    return jax.shard_map(
        local,
        mesh=mesh,
        in_specs=(
            P(("groups", "row"), "col"),
            P(("groups", "row"), "col"),
            P(("groups", "col"), "row", None),
            P(("groups", "row"), "col"),
            P(("groups", "col")),
        ),
        out_specs=(
            P(("groups", "row"), "col"),
            P(("groups", "row"), "col"),
            P(("groups", "col"), "row", None),
            P(("groups", "col"), "row", None),
        ),
        check_vma=False,
    )
```

```python
import functools
import math

import jax
import jax.numpy as jnp
from jax import lax
from jax.experimental import pallas as pl
from jax.experimental.pallas import tpu as pltpu
from jax.sharding import PartitionSpec as P

BETA = 0.9


def denominator(counters):
    decay_power = jnp.power(jnp.float32(BETA), (counters + 1).astype(jnp.float32))
    return 1.0 - decay_power


def ring_order(count):
    if count == 8:
        return [0, 2, 4, 6, 7, 5, 3, 1]
    return list(range(count))


def ring(gradient, left_old, right_old, left_counts, right_counts):
    tile_rows, half_wide = gradient.shape
    count = lax.axis_size("row")
    strip_wide = half_wide // count
    order = ring_order(count)
    place = {row: at for at, row in enumerate(order)}
    my_row = lax.axis_index("row")
    my_col = lax.axis_index("col")
    up = [(order[at], order[(at + 1) % count]) for at in range(count)]
    down = [(dest, source) for source, dest in up]
    piece = tile_rows // 2
    strip_at = my_row * strip_wide

    state = {"left": jnp.zeros((tile_rows, count * tile_rows), jnp.float32), "right": None}

    def consume(part, step, offset):
        sources = [order[(place[row] - step) % count] for row in range(count)]
        source = jnp.asarray(sources, jnp.int32)[my_row]
        product = lax.dot_general(
            gradient, part, (((1,), (1,)), ((), ())), preferred_element_type=jnp.float32
        )
        pairs = []
        for row in range(count):
            keeper = sources[row] * 2 // count
            pairs.append((row * 2 + 1 - keeper, row * 2 + keeper))
        other = lax.ppermute(product, ("row", "col"), pairs)
        state["left"] = lax.dynamic_update_slice(
            state["left"], product + other, (0, source * tile_rows + offset)
        )
        strip = lax.dynamic_slice_in_dim(part, strip_at, strip_wide, 1)
        term = lax.dot_general(
            strip, part, (((0,), (0,)), ((), ())), preferred_element_type=jnp.float32
        )
        state["right"] = term if state["right"] is None else state["right"] + term

    halves = [gradient[:piece], gradient[piece:]]
    going_up = list(halves)
    going_down = list(halves)
    last = count // 2
    for step in range(1, last + 1):
        if step < last:
            going_up = [lax.ppermute(part, "row", up) for part in going_up]
            going_down = [lax.ppermute(part, "row", down) for part in going_down]
        else:
            going_up = [lax.ppermute(going_up[0], "row", up)]
            going_down = [lax.ppermute(going_down[1], "row", down)]
        if step == 1:
            consume(halves[0], 0, 0)
            consume(halves[1], 0, piece)
        if step < last:
            for at in range(2):
                consume(going_up[at], step, at * piece)
                consume(going_down[at], -step, at * piece)
        else:
            consume(going_up[0], step, 0)
            consume(going_down[0], step, piece)

    width = count * tile_rows // 2
    gram_left = lax.dynamic_slice_in_dim(state["left"], my_col * width, width, 1)
    left_state = BETA * left_old + (1.0 - BETA) * gram_left
    left_fixed = left_state / denominator(left_counts)
    right_state = BETA * right_old + (1.0 - BETA) * state["right"][None]
    right_fixed = right_state / denominator(right_counts)[:, None, None]
    return (left_state, left_fixed, right_state, right_fixed)


GROUP = 64
LEVELS = 16


def pack(values, out_ref, at):
    levels = []
    for first in range(0, values.shape[0], GROUP):
        block = values[first : first + GROUP]
        most = jnp.maximum(jnp.max(jnp.abs(block), axis=0, keepdims=True), 1e-34)
        level = jnp.ceil(jnp.log2(most) * 256.0)
        inverse = 32767.0 * jnp.exp2(level * (-1.0 / 256.0))
        coded = jnp.clip(jnp.round(block * inverse), -32767.0, 32767.0)
        out_ref[at + first : at + first + GROUP] = coded.astype(jnp.int32).astype(jnp.int16)
        levels.append(level)
    return levels


def put_levels(levels, out_ref, at):
    levels = levels + [jnp.zeros_like(levels[0])] * (LEVELS - len(levels))
    out_ref[at : at + LEVELS] = jnp.concatenate(levels, 0).astype(jnp.int32).astype(jnp.int16)


def unpack(ref, index, rows, many):
    level = ref[many * rows : many * rows + LEVELS].astype(jnp.int32).astype(jnp.float32)
    step = jnp.exp2(level * (1.0 / 256.0)) * (1.0 / 32767.0)
    parts = []
    for group in range(rows // GROUP):
        at = index * rows + group * GROUP
        row = index * (rows // GROUP) + group
        block = ref[at : at + GROUP].astype(jnp.int32).astype(jnp.float32)
        parts.append(block * step[row : row + 1])
    return jnp.concatenate(parts, 0)


def decode(coded, rows):
    wide = coded.shape[1]
    level = coded[rows : rows + rows // GROUP].astype(jnp.float32)
    step = jnp.exp2(level * (1.0 / 256.0)) * (1.0 / 32767.0)
    grouped = coded[:rows].astype(jnp.float32).reshape(rows // GROUP, GROUP, wide)
    return (grouped * step[:, None, :]).reshape(rows, wide)


PARAMS = pltpu.CompilerParams(vmem_limit_bytes=48 * 2**20)
FREE = pl.CostEstimate(flops=1, bytes_accessed=1, transcendentals=0)
KEPT, START, NEXT, HOME, AWAY, LAST, SAME_HALF, MIDDLE, CORE = range(9)


def spec(shape, index=None):
    if index is None:
        return pl.BlockSpec(shape, lambda k, flags: (0, 0))
    return pl.BlockSpec(shape, lambda k, flags: (0, index(k, flags)))


def whole(array):
    return spec(array.shape)


def kernel_call(body, flags, steps, ins, outs, aliases=None, scratch=()):
    results = pl.pallas_call(
        body,
        grid_spec=pltpu.PrefetchScalarGridSpec(
            num_scalar_prefetch=1,
            grid=(steps,),
            in_specs=[s for _, s in ins],
            out_specs=[s for _, _, s in outs],
            scratch_shapes=list(scratch),
        ),
        out_shape=[jax.ShapeDtypeStruct(shape, dtype) for shape, dtype, _ in outs],
        input_output_aliases=aliases or {},
        compiler_params=PARAMS,
        cost_estimate=FREE,
    )(flags, *[array for array, _ in ins])
    return list(results)


def pick(flag, size):
    return pl.multiple_of(flag * size, GROUP)


def blocks_from(at, choice=None):
    if choice is None:
        return lambda k, flags: k + flags[at]
    return lambda k, flags: jnp.where(flags[MIDDLE] == choice, k, 0) + flags[at]


def choice_of(options, index):
    return None if len(options) == 1 else index


def left_terms(flags, rows, slots, block, steps, at=START, before=None, last=True):
    many = len(slots)
    choices = [len(slot) for slot in slots]
    tall = rows[0].shape[0]
    size = 2 * tall

    def body(flag_ref, first_ref, second_ref, *refs):
        slots_in = []
        for count in choices:
            slots_in.append(refs[:count])
            refs = refs[count:]
        if before is not None:
            before_in, refs = refs[:many], refs[many:]
        outs = refs[:many]
        step = pl.program_id(0)

        @pl.when(step == 0)
        def _():
            for index in range(many):
                outs[index][...] = jnp.zeros_like(outs[index]) if before is None else before_in[index][...]

        def add(index, ref):
            for half, row_ref in enumerate((first_ref, second_ref)):
                outs[index][half * tall : (half + 1) * tall] += dot(row_ref[...], ref[...], 1, 1)

        for index in range(many):
            if choices[index] == 1:
                add(index, slots_in[index][0])
            else:
                for choice in range(2):
                    pl.when(flag_ref[MIDDLE] == choice)(
                        functools.partial(add, index, slots_in[index][choice])
                    )

        if last:

            @pl.when(step == pl.num_programs(0) - 1)
            def _():
                gone = 1 - flag_ref[KEPT]
                levels = []
                for index in range(many):
                    part = outs[index][pl.ds(pick(gone, tall), tall), :]
                    levels += pack(part, refs[many], index * tall)
                put_levels(levels, refs[many], many * tall)

    ins = [(part, spec((tall, block), blocks_from(at))) for part in rows]
    for slot in slots:
        ins += [
            (array, spec((tall, block), blocks_from(start, choice_of(slot, index))))
            for index, (array, start) in enumerate(slot)
        ]
    if before is not None:
        ins += [(part, whole(part)) for part in before]
    outs = [((size, tall), jnp.float32, spec((size, tall)))] * many
    if last:
        shape = (many * tall + LEVELS, tall)
        outs.append((shape, jnp.int16, spec(shape)))
    return kernel_call(body, flags, steps, ins, outs)


def right_terms(
    flags, strips, columns, block, steps, at=START, before=None, last=False, hand_on=False
):
    wide = block * steps
    given = not isinstance(strips, list)
    if given:
        many, strip, rows = strips.shape
        strips = [strips]
    else:
        rows, strip = strips[0].shape
        many = len(strips)

    def body(flag_ref, *refs):
        strips_in, refs = refs[: len(strips)], refs[len(strips) :]
        columns_in = []
        for choice in columns:
            columns_in.append(refs[: len(choice)])
            refs = refs[len(choice) :]
        if before is not None:
            before_in, refs = refs[0], refs[1:]
        if given:
            outs, turned = refs, strips_in[0]
        else:
            outs, turned = refs[:-1], refs[-1]

            @pl.when(pl.program_id(0) == 0)
            def _():
                for index in range(many):
                    turned[index] = strips_in[index][...].T

        def add(choice):
            total = None if before is None else before_in[...]
            for index in range(many):
                refs_here = columns_in[index]
                ref = refs_here[choice if len(refs_here) == 2 else 0]
                term = dot(turned[index], ref[...], 1, 0)
                total = term if total is None else total + term
            outs[0][...] = total

        if max(len(choice) for choice in columns) == 1:
            add(0)
        else:
            for choice in range(2):
                pl.when(flag_ref[MIDDLE] == choice)(functools.partial(add, choice))
        if last:
            put_levels(pack(outs[0][...], outs[1], 0), outs[1], strip)

    here = lambda k, flags: k
    shape = (many, strip, rows)
    still = pl.BlockSpec(shape, lambda k, flags: (0, 0, 0))
    ins = [(part, still if given else whole(part)) for part in strips]
    for choice in columns:
        ins += [
            (array, spec((rows, block), blocks_from(start, choice_of(choice, index))))
            for index, (array, start) in enumerate(choice)
        ]
    if before is not None:
        ins.append((before, spec((strip, block), blocks_from(at))))
    outs = [((strip, wide), jnp.float32, spec((strip, block), here))]
    if last:
        outs.append(((strip + LEVELS, wide), jnp.int16, spec((strip + LEVELS, block), here)))
    scratch = []
    if hand_on:
        outs.append((shape, jnp.bfloat16, still))
    elif not given:
        scratch = [pltpu.VMEM(shape, jnp.bfloat16)]
    return kernel_call(body, flags, steps, ins, outs, scratch=scratch)


def add_up(flags, products, coded):
    rows, wide = products[0].shape[0] // 2, products[0].shape[1]
    many = len(products)

    def body(flag_ref, *refs):
        coded_ref, total_ref, out_ref = refs[many:]
        levels = []
        for index in range(many):
            kept = refs[index][pl.ds(pick(flag_ref[KEPT], rows), rows), :]
            total = kept + unpack(coded_ref, index, rows, many)
            total_ref[index * rows : (index + 1) * rows] = total
            levels += pack(total, out_ref, index * rows)
        put_levels(levels, out_ref, many * rows)

    ins = [(array, whole(array)) for array in list(products) + [coded]]
    shapes = [((many * rows, wide), jnp.float32), ((many * rows + LEVELS, wide), jnp.int16)]
    return kernel_call(body, flags, 1, ins, [(s, d, spec(s)) for s, d in shapes])


def write_states(old, gram, scale, state_ref, fixed_ref, where):
    state = BETA * old + (1.0 - BETA) * gram
    state_ref[:, where] = state
    fixed_ref[:, where] = state * scale


def finish_right(flags, scale, old, value, coded, at, block, steps, written=None):
    strip, wide = old.shape

    def body(flag_ref, scale_ref, old_ref, value_ref, coded_ref, *refs):
        state_ref, fixed_ref = refs[-2:]
        everything = slice(None)

        @pl.when(flag_ref[KEPT] == 0)
        def _():
            write_states(old_ref[...], value_ref[...], scale_ref[0], state_ref, fixed_ref, everything)

        @pl.when(flag_ref[KEPT] == 1)
        def _():
            write_states(
                old_ref[...], unpack(coded_ref, 0, strip, 1), scale_ref[0], state_ref, fixed_ref, everything
            )

    part = block
    there = lambda k, flags: k + flags[at]
    ins = [
        (scale, pl.BlockSpec(memory_space=pltpu.SMEM)),
        (old, spec((strip, part), there)),
        (value, spec((strip, part), lambda k, flags: k * (1 - flags[KEPT]))),
        (coded, spec((strip + LEVELS, part), lambda k, flags: k * flags[KEPT])),
    ]
    aliases = None
    if written is not None:
        ins += [(array, pl.BlockSpec(memory_space=pl.ANY)) for array in written]
        aliases = {5: 0, 6: 1}
    outs = [((strip, wide), jnp.float32, spec((strip, part), there))] * 2
    return kernel_call(body, flags, steps, ins, outs, aliases)


def finish_left(flags, scale, old, same_total, same_other, total, other, inner, written=None):
    tall, wide = total.shape

    def body(flag_ref, scale_ref, old_ref, same_ref, same_other_ref, total_ref, other_ref, *refs):
        state_ref, fixed_ref = refs[-2:]

        def put(value):
            write_states(old_ref[...], value, scale_ref[0], state_ref, fixed_ref, slice(None))

        is_mate = 1 - flag_ref[MIDDLE] if inner else flag_ref[MIDDLE]
        mine = flag_ref[CORE] == pl.program_id(0)
        same = flag_ref[SAME_HALF] == 1

        @pl.when(mine & same)
        def _():
            put(same_ref[pl.ds(pick(is_mate, tall), tall), :])

        @pl.when(mine & jnp.logical_not(same))
        def _():
            put(total_ref[...])

        for index in range(2):

            @pl.when(jnp.logical_not(mine) & same & (is_mate == index))
            def _():
                put(unpack(same_other_ref, index, tall, 2))

        @pl.when(jnp.logical_not(mine) & jnp.logical_not(same))
        def _():
            put(unpack(other_ref, 0, tall, 1))

    there = lambda k, flags: 2 * (1 - flags[CORE] if inner else flags[CORE]) + k
    ins = [(scale, pl.BlockSpec(memory_space=pltpu.SMEM)), (old, spec((tall, wide), there))]
    ins += [(array, whole(array)) for array in (same_total, same_other, total, other)]
    aliases = None
    if written is not None:
        ins += [(array, pl.BlockSpec(memory_space=pl.ANY)) for array in written]
        aliases = {7: 0, 8: 1}
    outs = [(old.shape, jnp.float32, spec((tall, wide), there))] * 2
    return kernel_call(body, flags, 2, ins, outs, aliases)


def dot(a, b, a_dim, b_dim):
    return lax.dot_general(
        a, b, (((a_dim,), (b_dim,)), ((), ())), preferred_element_type=jnp.float32
    )


AXES = ("row", "col")
CHIPS = [(z, y) for z in range(4) for y in range(2)]


def at(z, y, c):
    return (z * 2 + y) * 2 + c


def send(value, rule):
    pairs = []
    for z, y in CHIPS:
        for c in range(2):
            dest = rule(z, y, c)
            if dest is not None:
                pairs.append((at(z, y, c), at(*dest)))
    return lax.ppermute(value, AXES, pairs)


def middle(z):
    return z in (1, 2)


def to_line(z, y, c):
    return (z, c, y) if c != y else None


def pair_line(z, y, c):
    return (z ^ 1, c, y)


def across_line(z, y, c):
    return (3 - z, c, y) if middle(z) else None


def across(z, y, c):
    return (3 - z, y, c) if middle(z) else None


def outward(z, y, c):
    return (z ^ 1, y, c) if middle(z) else None


def beside(z, y, c):
    return (z, y, 1 - c)


def other_y(z, y, c):
    return (z, 1 - y, c)


def to_home(z, y, c):
    return (z, y, 1 - c) if c != z // 2 else None


def to_away(z, y, c):
    return (z, y, 1 - c) if c == z // 2 else None


def line_gather(gradient, left_old, right_old, left_counts, right_counts):
    tile_rows, half_wide = gradient.shape
    block = half_wide // 4
    strip = half_wide // 8
    my_row = lax.axis_index("row")
    c = lax.axis_index("col")
    z, y = my_row // 2, my_row % 2
    side = (z >= 2).astype(jnp.int32)
    is_middle = (z == 1) | (z == 2)
    straight = c == y
    flags = jnp.stack(
        [
            jnp.where(straight, 0, 1),
            0,
            1,
            2 * side,
            2 * (1 - side),
            2 * (1 - side) + 1,
            (c == side).astype(jnp.int32),
            is_middle.astype(jnp.int32),
            c,
        ]
    ).astype(jnp.int32)
    strip_at = (2 * z + c) * strip

    def tie(*values):
        return lax.optimization_barrier(tuple(values))

    def columns(value, first, count):
        return lax.dynamic_slice_in_dim(value, first * block, count * block, 1)

    def strips_of(pair, first=0):
        return [lax.dynamic_slice_in_dim(part, strip_at - first, strip, 1) for part in pair]

    def one(array, at=START):
        return [(array, at)]

    mate = send(gradient, pair_line)
    cross = send(gradient, across_line)
    gradient_t, mate, cross = tie(gradient, mate, cross)
    far = send(mate, across)
    near = send(cross, outward)
    swapped = send(gradient_t, to_line)
    mates = (mate, send(mate, beside))
    crosses = (cross, send(cross, beside))
    [right] = right_terms(
        flags,
        strips_of(mates) + strips_of(crosses),
        [one(part) for part in mates + crosses],
        block,
        4,
    )
    right, swapped = tie(right, swapped)
    mine = jnp.where(straight, gradient, swapped)
    half = half_wide // 2
    own = (
        mine,
        jnp.concatenate([send(mine[:, :half], beside), send(mine[:, half:], beside)], 1),
    )
    own_product, mate_product, same_coded = left_terms(
        flags, own, [one(mine), one(mate)], half, 2
    )
    same_products = [own_product, mate_product]
    same_got = send(same_coded, other_y)
    same_coded, own_o = tie(same_coded, own[1])
    own = (mine, own_o)
    [right] = right_terms(
        flags, strips_of(own), [one(part) for part in own], block, 4, before=right
    )

    right, near, far = tie(right, near, far)
    end_home = send(columns(far, 2 * side, 2), outward)
    nears = (near, send(near, beside))
    far_o = send(far, beside)
    near_product, near_coded = left_terms(
        flags, own, [[(near, START), (cross, START)]], half, 2
    )
    near_got = send(near_coded, other_y)
    near_coded, near, near_o = tie(near_coded, *nears)
    nears = (near, near_o)
    [right] = right_terms(
        flags, strips_of(nears), [one(part) for part in nears], block, 4, before=right
    )
    same_got, right = tie(same_got, right)
    same_total, same_out = add_up(flags, same_products, same_got)
    same_other = send(same_out, to_home)
    same_out, near_got = tie(same_out, near_got)
    near_total, near_out = add_up(flags, [near_product], near_got)
    near_other = send(near_out, to_away)

    far_t, near_out = tie(far, near_out)
    far_away, near_out = tie(columns(far_t, 2 * (1 - side), 2), near_out)
    right, near_out, end_home, far_o = tie(right, near_out, end_home, far_o)
    far_away, end_home = tie(far_away, end_home)
    end_away = send(far_away, outward)
    end_home_o = send(end_home, beside)
    strips = [
        jnp.where(is_middle, strips_of([a])[0], strips_of([b], 2 * side * block)[0])
        for a, b in ((far, end_home), (far_o, end_home_o))
    ]

    def last_right(strips, end, end_o, start, at, steps):
        return right_terms(
            flags,
            strips,
            [[(end, start), (far, at)], [(end_o, start), (far_o, at)]],
            block,
            steps,
            at=at,
            before=right,
            last=True,
            hand_on=isinstance(strips, list),
        )

    right_home, home_coded, strips = last_right(strips, end_home, end_home_o, START, HOME, 2)
    home_got = send(home_coded, to_line)
    home_coded, end_home = tie(home_coded, end_home)
    [far_product] = left_terms(
        flags, own, [[(end_home, START), (far, HOME)]], block, 2, at=HOME, last=False
    )
    left_scale = 1.0 / denominator(left_counts).reshape(1)
    right_scale = 1.0 / denominator(right_counts)
    old = right_old[0]
    far_product, near_other, same_other = tie(far_product, near_other, same_other)
    left_done = finish_left(
        flags, left_scale, left_old, same_total, same_other, near_total, near_other, True
    )
    left_done[0], home_got = tie(left_done[0], home_got)
    right_done = finish_right(flags, right_scale, old, right_home, home_got, HOME, block, 2)

    right_done[0], far_product, end_away = tie(right_done[0], far_product, end_away)
    end_away_o = send(end_away, beside)
    far_product, far_coded = left_terms(
        flags, own, [[(end_away, START), (far, AWAY)]], block, 2, at=AWAY, before=[far_product]
    )
    far_got = send(far_coded, other_y)
    far_coded, end_away_o = tie(far_coded, end_away_o)
    right_away, away_coded = last_right(strips, end_away, end_away_o, START, AWAY, 1)
    away_got = send(away_coded, to_line)
    away_coded, end_away_o = tie(away_coded, end_away_o)
    right_last, last_coded = last_right(strips, end_away, end_away_o, NEXT, LAST, 1)
    last_got = send(last_coded, to_line)
    last_coded, far_got = tie(last_coded, far_got)
    far_total, far_out = add_up(flags, [far_product], far_got)
    far_other = send(far_out, to_away)
    far_out, away_got = tie(far_out, away_got)
    right_done = finish_right(
        flags, right_scale, old, right_away, away_got, AWAY, block, 1, right_done
    )
    right_done[0], far_other = tie(right_done[0], far_other)
    left_state, left_fixed = finish_left(
        flags, left_scale, left_old, same_total, same_other, far_total, far_other, False, left_done
    )
    left_state, last_got = tie(left_state, last_got)
    right_state, right_fixed = finish_right(
        flags, right_scale, old, right_last, last_got, LAST, block, 1, right_done
    )
    return (left_state, left_fixed, right_state[None], right_fixed[None])


def solution(mesh):
    local = line_gather if mesh.shape["row"] == 8 else ring
    return jax.shard_map(
        local,
        mesh=mesh,
        in_specs=(
            P(("groups", "row"), "col"),
            P(("groups", "row"), "col"),
            P(("groups", "col"), "row", None),
            P(("groups", "row"), "col"),
            P(("groups", "col")),
        ),
        out_specs=(
            P(("groups", "row"), "col"),
            P(("groups", "row"), "col"),
            P(("groups", "col"), "row", None),
            P(("groups", "col"), "row", None),
        ),
        check_vma=False,
    )
```

```python
import functools
import math

import jax
import jax.numpy as jnp
from jax import lax
from jax.experimental import pallas as pl
from jax.experimental.pallas import tpu as pltpu
from jax.sharding import PartitionSpec as P

BETA = 0.9


def denominator(counters):
    decay_power = jnp.power(jnp.float32(BETA), (counters + 1).astype(jnp.float32))
    return 1.0 - decay_power


def ring_order(count):
    if count == 8:
        return [0, 2, 4, 6, 7, 5, 3, 1]
    return list(range(count))


def ring(gradient, left_old, right_old, left_counts, right_counts):
    tile_rows, half_wide = gradient.shape
    count = lax.axis_size("row")
    strip_wide = half_wide // count
    order = ring_order(count)
    place = {row: at for at, row in enumerate(order)}
    my_row = lax.axis_index("row")
    my_col = lax.axis_index("col")
    up = [(order[at], order[(at + 1) % count]) for at in range(count)]
    down = [(dest, source) for source, dest in up]
    piece = tile_rows // 2
    strip_at = my_row * strip_wide

    state = {"left": jnp.zeros((tile_rows, count * tile_rows), jnp.float32), "right": None}

    def consume(part, step, offset):
        sources = [order[(place[row] - step) % count] for row in range(count)]
        source = jnp.asarray(sources, jnp.int32)[my_row]
        product = lax.dot_general(
            gradient, part, (((1,), (1,)), ((), ())), preferred_element_type=jnp.float32
        )
        pairs = []
        for row in range(count):
            keeper = sources[row] * 2 // count
            pairs.append((row * 2 + 1 - keeper, row * 2 + keeper))
        other = lax.ppermute(product, ("row", "col"), pairs)
        state["left"] = lax.dynamic_update_slice(
            state["left"], product + other, (0, source * tile_rows + offset)
        )
        strip = lax.dynamic_slice_in_dim(part, strip_at, strip_wide, 1)
        term = lax.dot_general(
            strip, part, (((0,), (0,)), ((), ())), preferred_element_type=jnp.float32
        )
        state["right"] = term if state["right"] is None else state["right"] + term

    halves = [gradient[:piece], gradient[piece:]]
    going_up = list(halves)
    going_down = list(halves)
    last = count // 2
    for step in range(1, last + 1):
        if step < last:
            going_up = [lax.ppermute(part, "row", up) for part in going_up]
            going_down = [lax.ppermute(part, "row", down) for part in going_down]
        else:
            going_up = [lax.ppermute(going_up[0], "row", up)]
            going_down = [lax.ppermute(going_down[1], "row", down)]
        if step == 1:
            consume(halves[0], 0, 0)
            consume(halves[1], 0, piece)
        if step < last:
            for at in range(2):
                consume(going_up[at], step, at * piece)
                consume(going_down[at], -step, at * piece)
        else:
            consume(going_up[0], step, 0)
            consume(going_down[0], step, piece)

    width = count * tile_rows // 2
    gram_left = lax.dynamic_slice_in_dim(state["left"], my_col * width, width, 1)
    left_state = BETA * left_old + (1.0 - BETA) * gram_left
    left_fixed = left_state / denominator(left_counts)
    right_state = BETA * right_old + (1.0 - BETA) * state["right"][None]
    right_fixed = right_state / denominator(right_counts)[:, None, None]
    return (left_state, left_fixed, right_state, right_fixed)


GROUP = 64
LEVELS = 16


def pack(values, out_ref, at):
    levels = []
    for first in range(0, values.shape[0], GROUP):
        block = values[first : first + GROUP]
        most = jnp.maximum(jnp.max(jnp.abs(block), axis=0, keepdims=True), 1e-34)
        level = jnp.ceil(jnp.log2(most) * 256.0)
        inverse = 32767.0 * jnp.exp2(level * (-1.0 / 256.0))
        coded = jnp.clip(jnp.round(block * inverse), -32767.0, 32767.0)
        out_ref[at + first : at + first + GROUP] = coded.astype(jnp.int32).astype(jnp.int16)
        levels.append(level)
    return levels


def put_levels(levels, out_ref, at):
    levels = levels + [jnp.zeros_like(levels[0])] * (LEVELS - len(levels))
    out_ref[at : at + LEVELS] = jnp.concatenate(levels, 0).astype(jnp.int32).astype(jnp.int16)


def unpack(ref, index, rows, many):
    level = ref[many * rows : many * rows + LEVELS].astype(jnp.int32).astype(jnp.float32)
    step = jnp.exp2(level * (1.0 / 256.0)) * (1.0 / 32767.0)
    parts = []
    for group in range(rows // GROUP):
        at = index * rows + group * GROUP
        row = index * (rows // GROUP) + group
        block = ref[at : at + GROUP].astype(jnp.int32).astype(jnp.float32)
        parts.append(block * step[row : row + 1])
    return jnp.concatenate(parts, 0)


def decode(coded, rows):
    wide = coded.shape[1]
    level = coded[rows : rows + rows // GROUP].astype(jnp.float32)
    step = jnp.exp2(level * (1.0 / 256.0)) * (1.0 / 32767.0)
    grouped = coded[:rows].astype(jnp.float32).reshape(rows // GROUP, GROUP, wide)
    return (grouped * step[:, None, :]).reshape(rows, wide)


PARAMS = pltpu.CompilerParams(vmem_limit_bytes=64 * 2**20)
FREE = pl.CostEstimate(flops=1, bytes_accessed=1, transcendentals=0)
KEPT, START, NEXT, HOME, AWAY, LAST, SAME_HALF, MIDDLE, CORE = range(9)


def spec(shape, index=None):
    if index is None:
        return pl.BlockSpec(shape, lambda k, flags: (0, 0))
    return pl.BlockSpec(shape, lambda k, flags: (0, index(k, flags)))


def whole(array):
    return spec(array.shape)


def kernel_call(body, flags, steps, ins, outs, aliases=None, scratch=()):
    results = pl.pallas_call(
        body,
        grid_spec=pltpu.PrefetchScalarGridSpec(
            num_scalar_prefetch=1,
            grid=(steps,),
            in_specs=[s for _, s in ins],
            out_specs=[s for _, _, s in outs],
            scratch_shapes=list(scratch),
        ),
        out_shape=[jax.ShapeDtypeStruct(shape, dtype) for shape, dtype, _ in outs],
        input_output_aliases=aliases or {},
        compiler_params=PARAMS,
        cost_estimate=FREE,
    )(flags, *[array for array, _ in ins])
    return list(results)


def pick(flag, size):
    return pl.multiple_of(flag * size, GROUP)


def blocks_from(at, choice=None):
    if choice is None:
        return lambda k, flags: k + flags[at]
    return lambda k, flags: jnp.where(flags[MIDDLE] == choice, k, 0) + flags[at]


def choice_of(options, index):
    return None if len(options) == 1 else index


def left_terms(flags, rows, slots, block, steps, at=START, before=None, last=True):
    many = len(slots)
    choices = [len(slot) for slot in slots]
    tall = rows[0].shape[0]
    size = 2 * tall

    def body(flag_ref, first_ref, second_ref, *refs):
        slots_in = []
        for count in choices:
            slots_in.append(refs[:count])
            refs = refs[count:]
        if before is not None:
            before_in, refs = refs[:many], refs[many:]
        outs = refs[:many]
        step = pl.program_id(0)

        @pl.when(step == 0)
        def _():
            for index in range(many):
                outs[index][...] = jnp.zeros_like(outs[index]) if before is None else before_in[index][...]

        def add(index, ref):
            for half, row_ref in enumerate((first_ref, second_ref)):
                outs[index][half * tall : (half + 1) * tall] += dot(row_ref[...], ref[...], 1, 1)

        for index in range(many):
            if choices[index] == 1:
                add(index, slots_in[index][0])
            else:
                for choice in range(2):
                    pl.when(flag_ref[MIDDLE] == choice)(
                        functools.partial(add, index, slots_in[index][choice])
                    )

        if last:

            @pl.when(step == pl.num_programs(0) - 1)
            def _():
                gone = 1 - flag_ref[KEPT]
                levels = []
                for index in range(many):
                    part = outs[index][pl.ds(pick(gone, tall), tall), :]
                    levels += pack(part, refs[many], index * tall)
                put_levels(levels, refs[many], many * tall)

    ins = [(part, spec((tall, block), blocks_from(at))) for part in rows]
    for slot in slots:
        ins += [
            (array, spec((tall, block), blocks_from(start, choice_of(slot, index))))
            for index, (array, start) in enumerate(slot)
        ]
    if before is not None:
        ins += [(part, whole(part)) for part in before]
    outs = [((size, tall), jnp.float32, spec((size, tall)))] * many
    if last:
        shape = (many * tall + LEVELS, tall)
        outs.append((shape, jnp.int16, spec(shape)))
    return kernel_call(body, flags, steps, ins, outs)


def right_terms(
    flags, strips, columns, block, steps, at=START, before=None, last=False, hand_on=False
):
    wide = block * steps
    given = not isinstance(strips, list)
    if given:
        many, strip, rows = strips.shape
        strips = [strips]
    else:
        rows, strip = strips[0].shape
        many = len(strips)

    def body(flag_ref, *refs):
        strips_in, refs = refs[: len(strips)], refs[len(strips) :]
        columns_in = []
        for choice in columns:
            columns_in.append(refs[: len(choice)])
            refs = refs[len(choice) :]
        if before is not None:
            before_in, refs = refs[0], refs[1:]
        if given:
            outs, turned = refs, strips_in[0]
        else:
            outs, turned = refs[:-1], refs[-1]

            @pl.when(pl.program_id(0) == 0)
            def _():
                for index in range(many):
                    turned[index] = strips_in[index][...].T

        def add(choice):
            total = None if before is None else before_in[...]
            for index in range(many):
                refs_here = columns_in[index]
                ref = refs_here[choice if len(refs_here) == 2 else 0]
                term = dot(turned[index], ref[...], 1, 0)
                total = term if total is None else total + term
            outs[0][...] = total

        if max(len(choice) for choice in columns) == 1:
            add(0)
        else:
            for choice in range(2):
                pl.when(flag_ref[MIDDLE] == choice)(functools.partial(add, choice))
        if last:
            put_levels(pack(outs[0][...], outs[1], 0), outs[1], strip)

    here = lambda k, flags: k
    shape = (many, strip, rows)
    still = pl.BlockSpec(shape, lambda k, flags: (0, 0, 0))
    ins = [(part, still if given else whole(part)) for part in strips]
    for choice in columns:
        ins += [
            (array, spec((rows, block), blocks_from(start, choice_of(choice, index))))
            for index, (array, start) in enumerate(choice)
        ]
    if before is not None:
        ins.append((before, spec((strip, block), blocks_from(at))))
    outs = [((strip, wide), jnp.float32, spec((strip, block), here))]
    if last:
        outs.append(((strip + LEVELS, wide), jnp.int16, spec((strip + LEVELS, block), here)))
    scratch = []
    if hand_on:
        outs.append((shape, jnp.bfloat16, still))
    elif not given:
        scratch = [pltpu.VMEM(shape, jnp.bfloat16)]
    return kernel_call(body, flags, steps, ins, outs, scratch=scratch)


def add_up(flags, products, coded):
    rows, wide = products[0].shape[0] // 2, products[0].shape[1]
    many = len(products)

    def body(flag_ref, *refs):
        coded_ref, total_ref, out_ref = refs[many:]
        levels = []
        for index in range(many):
            kept = refs[index][pl.ds(pick(flag_ref[KEPT], rows), rows), :]
            total = kept + unpack(coded_ref, index, rows, many)
            total_ref[index * rows : (index + 1) * rows] = total
            levels += pack(total, out_ref, index * rows)
        put_levels(levels, out_ref, many * rows)

    ins = [(array, whole(array)) for array in list(products) + [coded]]
    shapes = [((many * rows, wide), jnp.float32), ((many * rows + LEVELS, wide), jnp.int16)]
    return kernel_call(body, flags, 1, ins, [(s, d, spec(s)) for s, d in shapes])


def write_states(old, gram, scale, state_ref, fixed_ref, where):
    state = BETA * old + (1.0 - BETA) * gram
    state_ref[:, where] = state
    fixed_ref[:, where] = state * scale


def finish_right(flags, scale, old, value, coded, at, block, steps, written=None):
    strip, wide = old.shape

    def body(flag_ref, scale_ref, old_ref, value_ref, coded_ref, *refs):
        state_ref, fixed_ref = refs[-2:]
        everything = slice(None)

        @pl.when(flag_ref[KEPT] == 0)
        def _():
            write_states(old_ref[...], value_ref[...], scale_ref[0], state_ref, fixed_ref, everything)

        @pl.when(flag_ref[KEPT] == 1)
        def _():
            write_states(
                old_ref[...], unpack(coded_ref, 0, strip, 1), scale_ref[0], state_ref, fixed_ref, everything
            )

    part = block
    there = lambda k, flags: k + flags[at]
    ins = [
        (scale, pl.BlockSpec(memory_space=pltpu.SMEM)),
        (old, spec((strip, part), there)),
        (value, spec((strip, part), lambda k, flags: k * (1 - flags[KEPT]))),
        (coded, spec((strip + LEVELS, part), lambda k, flags: k * flags[KEPT])),
    ]
    aliases = None
    if written is not None:
        ins += [(array, pl.BlockSpec(memory_space=pl.ANY)) for array in written]
        aliases = {5: 0, 6: 1}
    outs = [((strip, wide), jnp.float32, spec((strip, part), there))] * 2
    return kernel_call(body, flags, steps, ins, outs, aliases)


def finish_left(flags, scale, old, same_total, same_other, total, other, inner, written=None):
    tall, wide = total.shape

    def body(flag_ref, scale_ref, old_ref, same_ref, same_other_ref, total_ref, other_ref, *refs):
        state_ref, fixed_ref = refs[-2:]

        def put(value):
            write_states(old_ref[...], value, scale_ref[0], state_ref, fixed_ref, slice(None))

        is_mate = 1 - flag_ref[MIDDLE] if inner else flag_ref[MIDDLE]
        mine = flag_ref[CORE] == pl.program_id(0)
        same = flag_ref[SAME_HALF] == 1

        @pl.when(mine & same)
        def _():
            put(same_ref[pl.ds(pick(is_mate, tall), tall), :])

        @pl.when(mine & jnp.logical_not(same))
        def _():
            put(total_ref[...])

        for index in range(2):

            @pl.when(jnp.logical_not(mine) & same & (is_mate == index))
            def _():
                put(unpack(same_other_ref, index, tall, 2))

        @pl.when(jnp.logical_not(mine) & jnp.logical_not(same))
        def _():
            put(unpack(other_ref, 0, tall, 1))

    there = lambda k, flags: 2 * (1 - flags[CORE] if inner else flags[CORE]) + k
    ins = [(scale, pl.BlockSpec(memory_space=pltpu.SMEM)), (old, spec((tall, wide), there))]
    ins += [(array, whole(array)) for array in (same_total, same_other, total, other)]
    aliases = None
    if written is not None:
        ins += [(array, pl.BlockSpec(memory_space=pl.ANY)) for array in written]
        aliases = {7: 0, 8: 1}
    outs = [(old.shape, jnp.float32, spec((tall, wide), there))] * 2
    return kernel_call(body, flags, 2, ins, outs, aliases)


def dot(a, b, a_dim, b_dim):
    return lax.dot_general(
        a, b, (((a_dim,), (b_dim,)), ((), ())), preferred_element_type=jnp.float32
    )


AXES = ("row", "col")
CHIPS = [(z, y) for z in range(4) for y in range(2)]


def at(z, y, c):
    return (z * 2 + y) * 2 + c


def send(value, rule):
    pairs = []
    for z, y in CHIPS:
        for c in range(2):
            dest = rule(z, y, c)
            if dest is not None:
                pairs.append((at(z, y, c), at(*dest)))
    return lax.ppermute(value, AXES, pairs)


def middle(z):
    return z in (1, 2)


def to_line(z, y, c):
    return (z, c, y) if c != y else None


def pair_line(z, y, c):
    return (z ^ 1, c, y)


def across_line(z, y, c):
    return (3 - z, c, y) if middle(z) else None


def across(z, y, c):
    return (3 - z, y, c) if middle(z) else None


def outward(z, y, c):
    return (z ^ 1, y, c) if middle(z) else None


def beside(z, y, c):
    return (z, y, 1 - c)


def other_y(z, y, c):
    return (z, 1 - y, c)


def to_home(z, y, c):
    return (z, y, 1 - c) if c != z // 2 else None


def to_away(z, y, c):
    return (z, y, 1 - c) if c == z // 2 else None


def line_gather(gradient, left_old, right_old, left_counts, right_counts):
    tile_rows, half_wide = gradient.shape
    block = half_wide // 4
    strip = half_wide // 8
    my_row = lax.axis_index("row")
    c = lax.axis_index("col")
    z, y = my_row // 2, my_row % 2
    side = (z >= 2).astype(jnp.int32)
    is_middle = (z == 1) | (z == 2)
    straight = c == y
    flags = jnp.stack(
        [
            jnp.where(straight, 0, 1),
            0,
            1,
            2 * side,
            2 * (1 - side),
            2 * (1 - side) + 1,
            (c == side).astype(jnp.int32),
            is_middle.astype(jnp.int32),
            c,
        ]
    ).astype(jnp.int32)
    strip_at = (2 * z + c) * strip

    def tie(*values):
        return lax.optimization_barrier(tuple(values))

    def columns(value, first, count):
        return lax.dynamic_slice_in_dim(value, first * block, count * block, 1)

    def strips_of(pair, first=0):
        return [lax.dynamic_slice_in_dim(part, strip_at - first, strip, 1) for part in pair]

    def one(array, at=START):
        return [(array, at)]

    mate = send(gradient, pair_line)
    cross = send(gradient, across_line)
    gradient_t, mate, cross = tie(gradient, mate, cross)
    far = send(mate, across)
    near = send(cross, outward)
    swapped = send(gradient_t, to_line)
    mates = (mate, send(mate, beside))
    crosses = (cross, send(cross, beside))
    [right] = right_terms(
        flags,
        strips_of(mates) + strips_of(crosses),
        [one(part) for part in mates + crosses],
        block,
        4,
    )
    right, swapped = tie(right, swapped)
    mine = jnp.where(straight, gradient, swapped)
    half = half_wide // 2
    own = (
        mine,
        jnp.concatenate([send(mine[:, :half], beside), send(mine[:, half:], beside)], 1),
    )
    own_product, mate_product, same_coded = left_terms(
        flags, own, [one(mine), one(mate)], half, 2
    )
    same_products = [own_product, mate_product]
    same_got = send(same_coded, other_y)
    same_coded, own_o = tie(same_coded, own[1])
    own = (mine, own_o)
    [right] = right_terms(
        flags, strips_of(own), [one(part) for part in own], block, 4, before=right
    )

    right, near, far = tie(right, near, far)
    end_home = send(columns(far, 2 * side, 2), outward)
    nears = (near, send(near, beside))
    far_o = send(far, beside)
    near_product, near_coded = left_terms(
        flags, own, [[(near, START), (cross, START)]], half, 2
    )
    near_got = send(near_coded, other_y)
    near_coded, near, near_o = tie(near_coded, *nears)
    nears = (near, near_o)
    [right] = right_terms(
        flags, strips_of(nears), [one(part) for part in nears], block, 4, before=right
    )
    far_t, right = tie(far, right)
    far_away, same_got, right = tie(columns(far_t, 2 * (1 - side), 2), same_got, right)
    same_total, same_out = add_up(flags, same_products, same_got)
    same_other = send(same_out, to_home)
    same_out, near_got = tie(same_out, near_got)
    near_total, near_out = add_up(flags, [near_product], near_got)
    near_other = send(near_out, to_away)

    right, near_out, end_home, far_o = tie(right, near_out, end_home, far_o)
    far_away, end_home = tie(far_away, end_home)
    end_away = send(far_away, outward)
    end_home_o = send(end_home, beside)
    strips = [
        jnp.where(is_middle, strips_of([a])[0], strips_of([b], 2 * side * block)[0])
        for a, b in ((far, end_home), (far_o, end_home_o))
    ]

    def last_right(strips, end, end_o, start, at, steps):
        return right_terms(
            flags,
            strips,
            [[(end, start), (far, at)], [(end_o, start), (far_o, at)]],
            block,
            steps,
            at=at,
            before=right,
            last=True,
            hand_on=isinstance(strips, list),
        )

    right_home, home_coded, strips = last_right(strips, end_home, end_home_o, START, HOME, 2)
    home_got = send(home_coded, to_line)
    home_coded, end_home = tie(home_coded, end_home)
    [far_product] = left_terms(
        flags, own, [[(end_home, START), (far, HOME)]], block, 2, at=HOME, last=False
    )
    left_scale = 1.0 / denominator(left_counts).reshape(1)
    right_scale = 1.0 / denominator(right_counts)
    old = right_old[0]
    far_product, near_other, same_other = tie(far_product, near_other, same_other)
    left_done = finish_left(
        flags, left_scale, left_old, same_total, same_other, near_total, near_other, True
    )
    left_done[0], home_got = tie(left_done[0], home_got)
    right_done = finish_right(flags, right_scale, old, right_home, home_got, HOME, block, 2)

    right_done[0], far_product, end_away = tie(right_done[0], far_product, end_away)
    end_away_o = send(end_away, beside)
    far_product, far_coded = left_terms(
        flags, own, [[(end_away, START), (far, AWAY)]], block, 2, at=AWAY, before=[far_product]
    )
    far_got = send(far_coded, other_y)
    far_coded, end_away_o = tie(far_coded, end_away_o)
    right_away, away_coded = last_right(strips, end_away, end_away_o, START, AWAY, 1)
    away_got = send(away_coded, to_line)
    away_coded, end_away_o = tie(away_coded, end_away_o)
    right_last, last_coded = last_right(strips, end_away, end_away_o, NEXT, LAST, 1)
    last_got = send(last_coded, to_line)
    last_coded, far_got = tie(last_coded, far_got)
    far_total, far_out = add_up(flags, [far_product], far_got)
    far_other = send(far_out, to_away)
    far_out, away_got = tie(far_out, away_got)
    right_done = finish_right(
        flags, right_scale, old, right_away, away_got, AWAY, block, 1, right_done
    )
    right_done[0], far_other = tie(right_done[0], far_other)
    left_state, left_fixed = finish_left(
        flags, left_scale, left_old, same_total, same_other, far_total, far_other, False, left_done
    )
    left_state, last_got = tie(left_state, last_got)
    right_state, right_fixed = finish_right(
        flags, right_scale, old, right_last, last_got, LAST, block, 1, right_done
    )
    return (left_state, left_fixed, right_state[None], right_fixed[None])


def solution(mesh):
    local = line_gather if mesh.shape["row"] == 8 else ring
    return jax.shard_map(
        local,
        mesh=mesh,
        in_specs=(
            P(("groups", "row"), "col"),
            P(("groups", "row"), "col"),
            P(("groups", "col"), "row", None),
            P(("groups", "row"), "col"),
            P(("groups", "col")),
        ),
        out_specs=(
            P(("groups", "row"), "col"),
            P(("groups", "row"), "col"),
            P(("groups", "col"), "row", None),
            P(("groups", "col"), "row", None),
        ),
        check_vma=False,
    )
```

```python
import functools
import math

import jax
import jax.numpy as jnp
from jax import lax
from jax.experimental import pallas as pl
from jax.experimental.pallas import tpu as pltpu
from jax.sharding import PartitionSpec as P

BETA = 0.9


def denominator(counters):
    decay_power = jnp.power(jnp.float32(BETA), (counters + 1).astype(jnp.float32))
    return 1.0 - decay_power


def ring_order(count):
    if count == 8:
        return [0, 2, 4, 6, 7, 5, 3, 1]
    return list(range(count))


def ring(gradient, left_old, right_old, left_counts, right_counts):
    tile_rows, half_wide = gradient.shape
    count = lax.axis_size("row")
    strip_wide = half_wide // count
    order = ring_order(count)
    place = {row: at for at, row in enumerate(order)}
    my_row = lax.axis_index("row")
    my_col = lax.axis_index("col")
    up = [(order[at], order[(at + 1) % count]) for at in range(count)]
    down = [(dest, source) for source, dest in up]
    piece = tile_rows // 2
    strip_at = my_row * strip_wide

    state = {"left": jnp.zeros((tile_rows, count * tile_rows), jnp.float32), "right": None}

    def consume(part, step, offset):
        sources = [order[(place[row] - step) % count] for row in range(count)]
        source = jnp.asarray(sources, jnp.int32)[my_row]
        product = lax.dot_general(
            gradient, part, (((1,), (1,)), ((), ())), preferred_element_type=jnp.float32
        )
        pairs = []
        for row in range(count):
            keeper = sources[row] * 2 // count
            pairs.append((row * 2 + 1 - keeper, row * 2 + keeper))
        other = lax.ppermute(product, ("row", "col"), pairs)
        state["left"] = lax.dynamic_update_slice(
            state["left"], product + other, (0, source * tile_rows + offset)
        )
        strip = lax.dynamic_slice_in_dim(part, strip_at, strip_wide, 1)
        term = lax.dot_general(
            strip, part, (((0,), (0,)), ((), ())), preferred_element_type=jnp.float32
        )
        state["right"] = term if state["right"] is None else state["right"] + term

    halves = [gradient[:piece], gradient[piece:]]
    going_up = list(halves)
    going_down = list(halves)
    last = count // 2
    for step in range(1, last + 1):
        if step < last:
            going_up = [lax.ppermute(part, "row", up) for part in going_up]
            going_down = [lax.ppermute(part, "row", down) for part in going_down]
        else:
            going_up = [lax.ppermute(going_up[0], "row", up)]
            going_down = [lax.ppermute(going_down[1], "row", down)]
        if step == 1:
            consume(halves[0], 0, 0)
            consume(halves[1], 0, piece)
        if step < last:
            for at in range(2):
                consume(going_up[at], step, at * piece)
                consume(going_down[at], -step, at * piece)
        else:
            consume(going_up[0], step, 0)
            consume(going_down[0], step, piece)

    width = count * tile_rows // 2
    gram_left = lax.dynamic_slice_in_dim(state["left"], my_col * width, width, 1)
    left_state = BETA * left_old + (1.0 - BETA) * gram_left
    left_fixed = left_state / denominator(left_counts)
    right_state = BETA * right_old + (1.0 - BETA) * state["right"][None]
    right_fixed = right_state / denominator(right_counts)[:, None, None]
    return (left_state, left_fixed, right_state, right_fixed)


GROUP = 64
LEVELS = 16


def pack(values, out_ref, at):
    levels = []
    for first in range(0, values.shape[0], GROUP):
        block = values[first : first + GROUP]
        most = jnp.maximum(jnp.max(jnp.abs(block), axis=0, keepdims=True), 1e-34)
        level = jnp.ceil(jnp.log2(most) * 256.0)
        inverse = 32767.0 * jnp.exp2(level * (-1.0 / 256.0))
        coded = jnp.clip(jnp.round(block * inverse), -32767.0, 32767.0)
        out_ref[at + first : at + first + GROUP] = coded.astype(jnp.int32).astype(jnp.int16)
        levels.append(level)
    return levels


def put_levels(levels, out_ref, at):
    levels = levels + [jnp.zeros_like(levels[0])] * (LEVELS - len(levels))
    out_ref[at : at + LEVELS] = jnp.concatenate(levels, 0).astype(jnp.int32).astype(jnp.int16)


def unpack(ref, index, rows, many):
    level = ref[many * rows : many * rows + LEVELS].astype(jnp.int32).astype(jnp.float32)
    step = jnp.exp2(level * (1.0 / 256.0)) * (1.0 / 32767.0)
    parts = []
    for group in range(rows // GROUP):
        at = index * rows + group * GROUP
        row = index * (rows // GROUP) + group
        block = ref[at : at + GROUP].astype(jnp.int32).astype(jnp.float32)
        parts.append(block * step[row : row + 1])
    return jnp.concatenate(parts, 0)


def decode(coded, rows):
    wide = coded.shape[1]
    level = coded[rows : rows + rows // GROUP].astype(jnp.float32)
    step = jnp.exp2(level * (1.0 / 256.0)) * (1.0 / 32767.0)
    grouped = coded[:rows].astype(jnp.float32).reshape(rows // GROUP, GROUP, wide)
    return (grouped * step[:, None, :]).reshape(rows, wide)


PARAMS = pltpu.CompilerParams(vmem_limit_bytes=24 * 2**20)
FREE = pl.CostEstimate(flops=1, bytes_accessed=1, transcendentals=0)
KEPT, START, NEXT, HOME, AWAY, LAST, SAME_HALF, MIDDLE, CORE = range(9)


def spec(shape, index=None):
    if index is None:
        return pl.BlockSpec(shape, lambda k, flags: (0, 0))
    return pl.BlockSpec(shape, lambda k, flags: (0, index(k, flags)))


def whole(array):
    return spec(array.shape)


def kernel_call(body, flags, steps, ins, outs, aliases=None, scratch=()):
    results = pl.pallas_call(
        body,
        grid_spec=pltpu.PrefetchScalarGridSpec(
            num_scalar_prefetch=1,
            grid=(steps,),
            in_specs=[s for _, s in ins],
            out_specs=[s for _, _, s in outs],
            scratch_shapes=list(scratch),
        ),
        out_shape=[jax.ShapeDtypeStruct(shape, dtype) for shape, dtype, _ in outs],
        input_output_aliases=aliases or {},
        compiler_params=PARAMS,
        cost_estimate=FREE,
    )(flags, *[array for array, _ in ins])
    return list(results)


def pick(flag, size):
    return pl.multiple_of(flag * size, GROUP)


def blocks_from(at, choice=None):
    if choice is None:
        return lambda k, flags: k + flags[at]
    return lambda k, flags: jnp.where(flags[MIDDLE] == choice, k, 0) + flags[at]


def choice_of(options, index):
    return None if len(options) == 1 else index


def left_terms(flags, rows, slots, block, steps, at=START, before=None, last=True):
    many = len(slots)
    choices = [len(slot) for slot in slots]
    tall = rows[0].shape[0]
    size = 2 * tall

    def body(flag_ref, first_ref, second_ref, *refs):
        slots_in = []
        for count in choices:
            slots_in.append(refs[:count])
            refs = refs[count:]
        if before is not None:
            before_in, refs = refs[:many], refs[many:]
        outs = refs[:many]
        step = pl.program_id(0)

        @pl.when(step == 0)
        def _():
            for index in range(many):
                outs[index][...] = jnp.zeros_like(outs[index]) if before is None else before_in[index][...]

        def add(index, ref):
            for half, row_ref in enumerate((first_ref, second_ref)):
                outs[index][half * tall : (half + 1) * tall] += dot(row_ref[...], ref[...], 1, 1)

        for index in range(many):
            if choices[index] == 1:
                add(index, slots_in[index][0])
            else:
                for choice in range(2):
                    pl.when(flag_ref[MIDDLE] == choice)(
                        functools.partial(add, index, slots_in[index][choice])
                    )

        if last:

            @pl.when(step == pl.num_programs(0) - 1)
            def _():
                gone = 1 - flag_ref[KEPT]
                levels = []
                for index in range(many):
                    part = outs[index][pl.ds(pick(gone, tall), tall), :]
                    levels += pack(part, refs[many], index * tall)
                put_levels(levels, refs[many], many * tall)

    ins = [(part, spec((tall, block), blocks_from(at))) for part in rows]
    for slot in slots:
        ins += [
            (array, spec((tall, block), blocks_from(start, choice_of(slot, index))))
            for index, (array, start) in enumerate(slot)
        ]
    if before is not None:
        ins += [(part, whole(part)) for part in before]
    outs = [((size, tall), jnp.float32, spec((size, tall)))] * many
    if last:
        shape = (many * tall + LEVELS, tall)
        outs.append((shape, jnp.int16, spec(shape)))
    return kernel_call(body, flags, steps, ins, outs)


def right_terms(
    flags, strips, columns, block, steps, at=START, before=None, last=False, hand_on=False
):
    wide = block * steps
    given = not isinstance(strips, list)
    if given:
        many, strip, rows = strips.shape
        strips = [strips]
    else:
        rows, strip = strips[0].shape
        many = len(strips)

    def body(flag_ref, *refs):
        strips_in, refs = refs[: len(strips)], refs[len(strips) :]
        columns_in = []
        for choice in columns:
            columns_in.append(refs[: len(choice)])
            refs = refs[len(choice) :]
        if before is not None:
            before_in, refs = refs[0], refs[1:]
        if given:
            outs, turned = refs, strips_in[0]
        else:
            outs, turned = refs[:-1], refs[-1]

            @pl.when(pl.program_id(0) == 0)
            def _():
                for index in range(many):
                    turned[index] = strips_in[index][...].T

        def add(choice):
            total = None if before is None else before_in[...]
            for index in range(many):
                refs_here = columns_in[index]
                ref = refs_here[choice if len(refs_here) == 2 else 0]
                term = dot(turned[index], ref[...], 1, 0)
                total = term if total is None else total + term
            outs[0][...] = total

        if max(len(choice) for choice in columns) == 1:
            add(0)
        else:
            for choice in range(2):
                pl.when(flag_ref[MIDDLE] == choice)(functools.partial(add, choice))
        if last:
            put_levels(pack(outs[0][...], outs[1], 0), outs[1], strip)

    here = lambda k, flags: k
    shape = (many, strip, rows)
    still = pl.BlockSpec(shape, lambda k, flags: (0, 0, 0))
    ins = [(part, still if given else whole(part)) for part in strips]
    for choice in columns:
        ins += [
            (array, spec((rows, block), blocks_from(start, choice_of(choice, index))))
            for index, (array, start) in enumerate(choice)
        ]
    if before is not None:
        ins.append((before, spec((strip, block), blocks_from(at))))
    outs = [((strip, wide), jnp.float32, spec((strip, block), here))]
    if last:
        outs.append(((strip + LEVELS, wide), jnp.int16, spec((strip + LEVELS, block), here)))
    scratch = []
    if hand_on:
        outs.append((shape, jnp.bfloat16, still))
    elif not given:
        scratch = [pltpu.VMEM(shape, jnp.bfloat16)]
    return kernel_call(body, flags, steps, ins, outs, scratch=scratch)


def add_up(flags, products, coded):
    rows, wide = products[0].shape[0] // 2, products[0].shape[1]
    many = len(products)

    def body(flag_ref, *refs):
        coded_ref, total_ref, out_ref = refs[many:]
        levels = []
        for index in range(many):
            kept = refs[index][pl.ds(pick(flag_ref[KEPT], rows), rows), :]
            total = kept + unpack(coded_ref, index, rows, many)
            total_ref[index * rows : (index + 1) * rows] = total
            levels += pack(total, out_ref, index * rows)
        put_levels(levels, out_ref, many * rows)

    ins = [(array, whole(array)) for array in list(products) + [coded]]
    shapes = [((many * rows, wide), jnp.float32), ((many * rows + LEVELS, wide), jnp.int16)]
    return kernel_call(body, flags, 1, ins, [(s, d, spec(s)) for s, d in shapes])


def write_states(old, gram, scale, state_ref, fixed_ref, where):
    state = BETA * old + (1.0 - BETA) * gram
    state_ref[:, where] = state
    fixed_ref[:, where] = state * scale


def finish_right(flags, scale, old, value, coded, at, block, steps, written=None):
    strip, wide = old.shape

    def body(flag_ref, scale_ref, old_ref, value_ref, coded_ref, *refs):
        state_ref, fixed_ref = refs[-2:]
        everything = slice(None)

        @pl.when(flag_ref[KEPT] == 0)
        def _():
            write_states(old_ref[...], value_ref[...], scale_ref[0], state_ref, fixed_ref, everything)

        @pl.when(flag_ref[KEPT] == 1)
        def _():
            write_states(
                old_ref[...], unpack(coded_ref, 0, strip, 1), scale_ref[0], state_ref, fixed_ref, everything
            )

    part = block
    there = lambda k, flags: k + flags[at]
    ins = [
        (scale, pl.BlockSpec(memory_space=pltpu.SMEM)),
        (old, spec((strip, part), there)),
        (value, spec((strip, part), lambda k, flags: k * (1 - flags[KEPT]))),
        (coded, spec((strip + LEVELS, part), lambda k, flags: k * flags[KEPT])),
    ]
    aliases = None
    if written is not None:
        ins += [(array, pl.BlockSpec(memory_space=pl.ANY)) for array in written]
        aliases = {5: 0, 6: 1}
    outs = [((strip, wide), jnp.float32, spec((strip, part), there))] * 2
    return kernel_call(body, flags, steps, ins, outs, aliases)


def finish_left(flags, scale, old, same_total, same_other, total, other, inner, written=None):
    tall, wide = total.shape

    def body(flag_ref, scale_ref, old_ref, same_ref, same_other_ref, total_ref, other_ref, *refs):
        state_ref, fixed_ref = refs[-2:]

        def put(value):
            write_states(old_ref[...], value, scale_ref[0], state_ref, fixed_ref, slice(None))

        is_mate = 1 - flag_ref[MIDDLE] if inner else flag_ref[MIDDLE]
        mine = flag_ref[CORE] == pl.program_id(0)
        same = flag_ref[SAME_HALF] == 1

        @pl.when(mine & same)
        def _():
            put(same_ref[pl.ds(pick(is_mate, tall), tall), :])

        @pl.when(mine & jnp.logical_not(same))
        def _():
            put(total_ref[...])

        for index in range(2):

            @pl.when(jnp.logical_not(mine) & same & (is_mate == index))
            def _():
                put(unpack(same_other_ref, index, tall, 2))

        @pl.when(jnp.logical_not(mine) & jnp.logical_not(same))
        def _():
            put(unpack(other_ref, 0, tall, 1))

    there = lambda k, flags: 2 * (1 - flags[CORE] if inner else flags[CORE]) + k
    ins = [(scale, pl.BlockSpec(memory_space=pltpu.SMEM)), (old, spec((tall, wide), there))]
    ins += [(array, whole(array)) for array in (same_total, same_other, total, other)]
    aliases = None
    if written is not None:
        ins += [(array, pl.BlockSpec(memory_space=pl.ANY)) for array in written]
        aliases = {7: 0, 8: 1}
    outs = [(old.shape, jnp.float32, spec((tall, wide), there))] * 2
    return kernel_call(body, flags, 2, ins, outs, aliases)


def dot(a, b, a_dim, b_dim):
    return lax.dot_general(
        a, b, (((a_dim,), (b_dim,)), ((), ())), preferred_element_type=jnp.float32
    )


AXES = ("row", "col")
CHIPS = [(z, y) for z in range(4) for y in range(2)]


def at(z, y, c):
    return (z * 2 + y) * 2 + c


def send(value, rule):
    pairs = []
    for z, y in CHIPS:
        for c in range(2):
            dest = rule(z, y, c)
            if dest is not None:
                pairs.append((at(z, y, c), at(*dest)))
    return lax.ppermute(value, AXES, pairs)


def middle(z):
    return z in (1, 2)


def to_line(z, y, c):
    return (z, c, y) if c != y else None


def pair_line(z, y, c):
    return (z ^ 1, c, y)


def across_line(z, y, c):
    return (3 - z, c, y) if middle(z) else None


def across(z, y, c):
    return (3 - z, y, c) if middle(z) else None


def outward(z, y, c):
    return (z ^ 1, y, c) if middle(z) else None


def beside(z, y, c):
    return (z, y, 1 - c)


def other_y(z, y, c):
    return (z, 1 - y, c)


def to_home(z, y, c):
    return (z, y, 1 - c) if c != z // 2 else None


def to_away(z, y, c):
    return (z, y, 1 - c) if c == z // 2 else None


def line_gather(gradient, left_old, right_old, left_counts, right_counts):
    tile_rows, half_wide = gradient.shape
    block = half_wide // 4
    strip = half_wide // 8
    my_row = lax.axis_index("row")
    c = lax.axis_index("col")
    z, y = my_row // 2, my_row % 2
    side = (z >= 2).astype(jnp.int32)
    is_middle = (z == 1) | (z == 2)
    straight = c == y
    flags = jnp.stack(
        [
            jnp.where(straight, 0, 1),
            0,
            1,
            2 * side,
            2 * (1 - side),
            2 * (1 - side) + 1,
            (c == side).astype(jnp.int32),
            is_middle.astype(jnp.int32),
            c,
        ]
    ).astype(jnp.int32)
    strip_at = (2 * z + c) * strip

    def tie(*values):
        return lax.optimization_barrier(tuple(values))

    def columns(value, first, count):
        return lax.dynamic_slice_in_dim(value, first * block, count * block, 1)

    def strips_of(pair, first=0):
        return [lax.dynamic_slice_in_dim(part, strip_at - first, strip, 1) for part in pair]

    def one(array, at=START):
        return [(array, at)]

    mate = send(gradient, pair_line)
    cross = send(gradient, across_line)
    gradient_t, mate, cross = tie(gradient, mate, cross)
    far = send(mate, across)
    near = send(cross, outward)
    swapped = send(gradient_t, to_line)
    mates = (mate, send(mate, beside))
    crosses = (cross, send(cross, beside))
    [right] = right_terms(
        flags,
        strips_of(mates) + strips_of(crosses),
        [one(part) for part in mates + crosses],
        block,
        4,
    )
    right, swapped = tie(right, swapped)
    mine = jnp.where(straight, gradient, swapped)
    half = half_wide // 2
    own = (
        mine,
        jnp.concatenate([send(mine[:, :half], beside), send(mine[:, half:], beside)], 1),
    )
    own_product, mate_product, same_coded = left_terms(
        flags, own, [one(mine), one(mate)], half, 2
    )
    same_products = [own_product, mate_product]
    same_got = send(same_coded, other_y)
    same_coded, own_o = tie(same_coded, own[1])
    own = (mine, own_o)
    [right] = right_terms(
        flags, strips_of(own), [one(part) for part in own], block, 4, before=right
    )

    right, near, far = tie(right, near, far)
    end_home = send(columns(far, 2 * side, 2), outward)
    nears = (near, send(near, beside))
    far_o = send(far, beside)
    near_product, near_coded = left_terms(
        flags, own, [[(near, START), (cross, START)]], half, 2
    )
    near_got = send(near_coded, other_y)
    near_coded, near, near_o = tie(near_coded, *nears)
    nears = (near, near_o)
    [right] = right_terms(
        flags, strips_of(nears), [one(part) for part in nears], block, 4, before=right
    )
    far_t, right = tie(far, right)
    far_away, same_got, right = tie(columns(far_t, 2 * (1 - side), 2), same_got, right)
    same_total, same_out = add_up(flags, same_products, same_got)
    same_other = send(same_out, to_home)
    same_out, near_got = tie(same_out, near_got)
    near_total, near_out = add_up(flags, [near_product], near_got)
    near_other = send(near_out, to_away)

    right, near_out, end_home, far_o = tie(right, near_out, end_home, far_o)
    far_away, end_home = tie(far_away, end_home)
    end_away = send(far_away, outward)
    end_home_o = send(end_home, beside)
    strips = [
        jnp.where(is_middle, strips_of([a])[0], strips_of([b], 2 * side * block)[0])
        for a, b in ((far, end_home), (far_o, end_home_o))
    ]

    def last_right(strips, end, end_o, start, at, steps):
        return right_terms(
            flags,
            strips,
            [[(end, start), (far, at)], [(end_o, start), (far_o, at)]],
            block,
            steps,
            at=at,
            before=right,
            last=True,
            hand_on=isinstance(strips, list),
        )

    right_home, home_coded, strips = last_right(strips, end_home, end_home_o, START, HOME, 2)
    home_got = send(home_coded, to_line)
    home_coded, end_home = tie(home_coded, end_home)
    [far_product] = left_terms(
        flags, own, [[(end_home, START), (far, HOME)]], block, 2, at=HOME, last=False
    )
    left_scale = 1.0 / denominator(left_counts).reshape(1)
    right_scale = 1.0 / denominator(right_counts)
    old = right_old[0]
    far_product, near_other, same_other = tie(far_product, near_other, same_other)
    left_done = finish_left(
        flags, left_scale, left_old, same_total, same_other, near_total, near_other, True
    )
    left_done[0], home_got = tie(left_done[0], home_got)
    right_done = finish_right(flags, right_scale, old, right_home, home_got, HOME, block, 2)

    right_done[0], far_product, end_away = tie(right_done[0], far_product, end_away)
    end_away_o = send(end_away, beside)
    far_product, far_coded = left_terms(
        flags, own, [[(end_away, START), (far, AWAY)]], block, 2, at=AWAY, before=[far_product]
    )
    far_got = send(far_coded, other_y)
    far_coded, end_away_o = tie(far_coded, end_away_o)
    right_away, away_coded = last_right(strips, end_away, end_away_o, START, AWAY, 1)
    away_got = send(away_coded, to_line)
    away_coded, end_away_o = tie(away_coded, end_away_o)
    right_last, last_coded = last_right(strips, end_away, end_away_o, NEXT, LAST, 1)
    last_got = send(last_coded, to_line)
    last_coded, far_got = tie(last_coded, far_got)
    far_total, far_out = add_up(flags, [far_product], far_got)
    far_other = send(far_out, to_away)
    far_out, away_got = tie(far_out, away_got)
    right_done = finish_right(
        flags, right_scale, old, right_away, away_got, AWAY, block, 1, right_done
    )
    right_done[0], far_other = tie(right_done[0], far_other)
    left_state, left_fixed = finish_left(
        flags, left_scale, left_old, same_total, same_other, far_total, far_other, False, left_done
    )
    left_state, last_got = tie(left_state, last_got)
    right_state, right_fixed = finish_right(
        flags, right_scale, old, right_last, last_got, LAST, block, 1, right_done
    )
    return (left_state, left_fixed, right_state[None], right_fixed[None])


def solution(mesh):
    local = line_gather if mesh.shape["row"] == 8 else ring
    return jax.shard_map(
        local,
        mesh=mesh,
        in_specs=(
            P(("groups", "row"), "col"),
            P(("groups", "row"), "col"),
            P(("groups", "col"), "row", None),
            P(("groups", "row"), "col"),
            P(("groups", "col")),
        ),
        out_specs=(
            P(("groups", "row"), "col"),
            P(("groups", "row"), "col"),
            P(("groups", "col"), "row", None),
            P(("groups", "col"), "row", None),
        ),
        check_vma=False,
    )
```

```python
import functools
import math

import jax
import jax.numpy as jnp
from jax import lax
from jax.experimental import pallas as pl
from jax.experimental.pallas import tpu as pltpu
from jax.sharding import PartitionSpec as P

BETA = 0.9


def denominator(counters):
    decay_power = jnp.power(jnp.float32(BETA), (counters + 1).astype(jnp.float32))
    return 1.0 - decay_power


def ring_order(count):
    if count == 8:
        return [0, 2, 4, 6, 7, 5, 3, 1]
    return list(range(count))


def ring(gradient, left_old, right_old, left_counts, right_counts):
    tile_rows, half_wide = gradient.shape
    count = lax.axis_size("row")
    strip_wide = half_wide // count
    order = ring_order(count)
    place = {row: at for at, row in enumerate(order)}
    my_row = lax.axis_index("row")
    my_col = lax.axis_index("col")
    up = [(order[at], order[(at + 1) % count]) for at in range(count)]
    down = [(dest, source) for source, dest in up]
    piece = tile_rows // 2
    strip_at = my_row * strip_wide

    state = {"left": jnp.zeros((tile_rows, count * tile_rows), jnp.float32), "right": None}

    def consume(part, step, offset):
        sources = [order[(place[row] - step) % count] for row in range(count)]
        source = jnp.asarray(sources, jnp.int32)[my_row]
        product = lax.dot_general(
            gradient, part, (((1,), (1,)), ((), ())), preferred_element_type=jnp.float32
        )
        pairs = []
        for row in range(count):
            keeper = sources[row] * 2 // count
            pairs.append((row * 2 + 1 - keeper, row * 2 + keeper))
        other = lax.ppermute(product, ("row", "col"), pairs)
        state["left"] = lax.dynamic_update_slice(
            state["left"], product + other, (0, source * tile_rows + offset)
        )
        strip = lax.dynamic_slice_in_dim(part, strip_at, strip_wide, 1)
        term = lax.dot_general(
            strip, part, (((0,), (0,)), ((), ())), preferred_element_type=jnp.float32
        )
        state["right"] = term if state["right"] is None else state["right"] + term

    halves = [gradient[:piece], gradient[piece:]]
    going_up = list(halves)
    going_down = list(halves)
    last = count // 2
    for step in range(1, last + 1):
        if step < last:
            going_up = [lax.ppermute(part, "row", up) for part in going_up]
            going_down = [lax.ppermute(part, "row", down) for part in going_down]
        else:
            going_up = [lax.ppermute(going_up[0], "row", up)]
            going_down = [lax.ppermute(going_down[1], "row", down)]
        if step == 1:
            consume(halves[0], 0, 0)
            consume(halves[1], 0, piece)
        if step < last:
            for at in range(2):
                consume(going_up[at], step, at * piece)
                consume(going_down[at], -step, at * piece)
        else:
            consume(going_up[0], step, 0)
            consume(going_down[0], step, piece)

    width = count * tile_rows // 2
    gram_left = lax.dynamic_slice_in_dim(state["left"], my_col * width, width, 1)
    left_state = BETA * left_old + (1.0 - BETA) * gram_left
    left_fixed = left_state / denominator(left_counts)
    right_state = BETA * right_old + (1.0 - BETA) * state["right"][None]
    right_fixed = right_state / denominator(right_counts)[:, None, None]
    return (left_state, left_fixed, right_state, right_fixed)


GROUP = 64
LEVELS = 16


def pack(values, out_ref, at):
    levels = []
    for first in range(0, values.shape[0], GROUP):
        block = values[first : first + GROUP]
        most = jnp.maximum(jnp.max(jnp.abs(block), axis=0, keepdims=True), 1e-34)
        level = jnp.ceil(jnp.log2(most) * 256.0)
        inverse = 32767.0 * jnp.exp2(level * (-1.0 / 256.0))
        coded = jnp.clip(jnp.round(block * inverse), -32767.0, 32767.0)
        out_ref[at + first : at + first + GROUP] = coded.astype(jnp.int32).astype(jnp.int16)
        levels.append(level)
    return levels


def put_levels(levels, out_ref, at):
    levels = levels + [jnp.zeros_like(levels[0])] * (LEVELS - len(levels))
    out_ref[at : at + LEVELS] = jnp.concatenate(levels, 0).astype(jnp.int32).astype(jnp.int16)


def unpack(ref, index, rows, many):
    level = ref[many * rows : many * rows + LEVELS].astype(jnp.int32).astype(jnp.float32)
    step = jnp.exp2(level * (1.0 / 256.0)) * (1.0 / 32767.0)
    parts = []
    for group in range(rows // GROUP):
        at = index * rows + group * GROUP
        row = index * (rows // GROUP) + group
        block = ref[at : at + GROUP].astype(jnp.int32).astype(jnp.float32)
        parts.append(block * step[row : row + 1])
    return jnp.concatenate(parts, 0)


def decode(coded, rows):
    wide = coded.shape[1]
    level = coded[rows : rows + rows // GROUP].astype(jnp.float32)
    step = jnp.exp2(level * (1.0 / 256.0)) * (1.0 / 32767.0)
    grouped = coded[:rows].astype(jnp.float32).reshape(rows // GROUP, GROUP, wide)
    return (grouped * step[:, None, :]).reshape(rows, wide)


PARAMS = pltpu.CompilerParams(vmem_limit_bytes=24 * 2**20)
FREE = pl.CostEstimate(flops=1, bytes_accessed=1, transcendentals=0)
KEPT, START, NEXT, HOME, AWAY, LAST, SAME_HALF, MIDDLE, CORE = range(9)


def spec(shape, index=None):
    if index is None:
        return pl.BlockSpec(shape, lambda k, flags: (0, 0))
    return pl.BlockSpec(shape, lambda k, flags: (0, index(k, flags)))


def whole(array):
    return spec(array.shape)


def kernel_call(body, flags, steps, ins, outs, aliases=None, scratch=()):
    results = pl.pallas_call(
        body,
        grid_spec=pltpu.PrefetchScalarGridSpec(
            num_scalar_prefetch=1,
            grid=(steps,),
            in_specs=[s for _, s in ins],
            out_specs=[s for _, _, s in outs],
            scratch_shapes=list(scratch),
        ),
        out_shape=[jax.ShapeDtypeStruct(shape, dtype) for shape, dtype, _ in outs],
        input_output_aliases=aliases or {},
        compiler_params=PARAMS,
        cost_estimate=FREE,
    )(flags, *[array for array, _ in ins])
    return list(results)


def pick(flag, size):
    return pl.multiple_of(flag * size, GROUP)


def blocks_from(at, choice=None):
    if choice is None:
        return lambda k, flags: k + flags[at]
    return lambda k, flags: jnp.where(flags[MIDDLE] == choice, k, 0) + flags[at]


def choice_of(options, index):
    return None if len(options) == 1 else index


def left_terms(flags, rows, slots, block, steps, at=START, before=None, last=True):
    many = len(slots)
    choices = [len(slot) for slot in slots]
    tall = rows[0].shape[0]
    size = 2 * tall

    def body(flag_ref, first_ref, second_ref, *refs):
        slots_in = []
        for count in choices:
            slots_in.append(refs[:count])
            refs = refs[count:]
        if before is not None:
            before_in, refs = refs[:many], refs[many:]
        outs = refs[:many]
        step = pl.program_id(0)

        @pl.when(step == 0)
        def _():
            for index in range(many):
                outs[index][...] = jnp.zeros_like(outs[index]) if before is None else before_in[index][...]

        def add(index, ref):
            for half, row_ref in enumerate((first_ref, second_ref)):
                outs[index][half * tall : (half + 1) * tall] += dot(row_ref[...], ref[...], 1, 1)

        for index in range(many):
            if choices[index] == 1:
                add(index, slots_in[index][0])
            else:
                for choice in range(2):
                    pl.when(flag_ref[MIDDLE] == choice)(
                        functools.partial(add, index, slots_in[index][choice])
                    )

        if last:

            @pl.when(step == pl.num_programs(0) - 1)
            def _():
                gone = 1 - flag_ref[KEPT]
                levels = []
                for index in range(many):
                    part = outs[index][pl.ds(pick(gone, tall), tall), :]
                    levels += pack(part, refs[many], index * tall)
                put_levels(levels, refs[many], many * tall)

    ins = [(part, spec((tall, block), blocks_from(at))) for part in rows]
    for slot in slots:
        ins += [
            (array, spec((tall, block), blocks_from(start, choice_of(slot, index))))
            for index, (array, start) in enumerate(slot)
        ]
    if before is not None:
        ins += [(part, whole(part)) for part in before]
    outs = [((size, tall), jnp.float32, spec((size, tall)))] * many
    if last:
        shape = (many * tall + LEVELS, tall)
        outs.append((shape, jnp.int16, spec(shape)))
    return kernel_call(body, flags, steps, ins, outs)


def right_terms(
    flags, strips, columns, block, steps, at=START, before=None, last=False, hand_on=False
):
    wide = block * steps
    given = not isinstance(strips, list)
    if given:
        many, strip, rows = strips.shape
        strips = [strips]
    else:
        rows, strip = strips[0].shape
        many = len(strips)

    def body(flag_ref, *refs):
        strips_in, refs = refs[: len(strips)], refs[len(strips) :]
        columns_in = []
        for choice in columns:
            columns_in.append(refs[: len(choice)])
            refs = refs[len(choice) :]
        if before is not None:
            before_in, refs = refs[0], refs[1:]
        if given:
            outs, turned = refs, strips_in[0]
        else:
            outs, turned = refs[:-1], refs[-1]

            @pl.when(pl.program_id(0) == 0)
            def _():
                for index in range(many):
                    turned[index] = strips_in[index][...].T

        def add(choice):
            total = None if before is None else before_in[...]
            for index in range(many):
                refs_here = columns_in[index]
                ref = refs_here[choice if len(refs_here) == 2 else 0]
                term = dot(turned[index], ref[...], 1, 0)
                total = term if total is None else total + term
            outs[0][...] = total

        if max(len(choice) for choice in columns) == 1:
            add(0)
        else:
            for choice in range(2):
                pl.when(flag_ref[MIDDLE] == choice)(functools.partial(add, choice))
        if last:
            put_levels(pack(outs[0][...], outs[1], 0), outs[1], strip)

    here = lambda k, flags: k
    shape = (many, strip, rows)
    still = pl.BlockSpec(shape, lambda k, flags: (0, 0, 0))
    ins = [(part, still if given else whole(part)) for part in strips]
    for choice in columns:
        ins += [
            (array, spec((rows, block), blocks_from(start, choice_of(choice, index))))
            for index, (array, start) in enumerate(choice)
        ]
    if before is not None:
        ins.append((before, spec((strip, block), blocks_from(at))))
    outs = [((strip, wide), jnp.float32, spec((strip, block), here))]
    if last:
        outs.append(((strip + LEVELS, wide), jnp.int16, spec((strip + LEVELS, block), here)))
    scratch = []
    if hand_on:
        outs.append((shape, jnp.bfloat16, still))
    elif not given:
        scratch = [pltpu.VMEM(shape, jnp.bfloat16)]
    return kernel_call(body, flags, steps, ins, outs, scratch=scratch)


def add_up(flags, products, coded):
    rows, wide = products[0].shape[0] // 2, products[0].shape[1]
    many = len(products)

    def body(flag_ref, *refs):
        coded_ref, total_ref, out_ref = refs[many:]
        levels = []
        for index in range(many):
            kept = refs[index][pl.ds(pick(flag_ref[KEPT], rows), rows), :]
            total = kept + unpack(coded_ref, index, rows, many)
            total_ref[index * rows : (index + 1) * rows] = total
            levels += pack(total, out_ref, index * rows)
        put_levels(levels, out_ref, many * rows)

    ins = [(array, whole(array)) for array in list(products) + [coded]]
    shapes = [((many * rows, wide), jnp.float32), ((many * rows + LEVELS, wide), jnp.int16)]
    return kernel_call(body, flags, 1, ins, [(s, d, spec(s)) for s, d in shapes])


def write_states(old, gram, scale, state_ref, fixed_ref, where):
    state = BETA * old + (1.0 - BETA) * gram
    state_ref[:, where] = state
    fixed_ref[:, where] = state * scale


def finish_right(flags, scale, old, value, coded, at, block, steps, written=None):
    strip, wide = old.shape

    def body(flag_ref, scale_ref, old_ref, value_ref, coded_ref, *refs):
        state_ref, fixed_ref = refs[-2:]
        everything = slice(None)

        @pl.when(flag_ref[KEPT] == 0)
        def _():
            write_states(old_ref[...], value_ref[...], scale_ref[0], state_ref, fixed_ref, everything)

        @pl.when(flag_ref[KEPT] == 1)
        def _():
            write_states(
                old_ref[...], unpack(coded_ref, 0, strip, 1), scale_ref[0], state_ref, fixed_ref, everything
            )

    part = block
    there = lambda k, flags: k + flags[at]
    ins = [
        (scale, pl.BlockSpec(memory_space=pltpu.SMEM)),
        (old, spec((strip, part), there)),
        (value, spec((strip, part), lambda k, flags: k * (1 - flags[KEPT]))),
        (coded, spec((strip + LEVELS, part), lambda k, flags: k * flags[KEPT])),
    ]
    aliases = None
    if written is not None:
        ins += [(array, pl.BlockSpec(memory_space=pl.ANY)) for array in written]
        aliases = {5: 0, 6: 1}
    outs = [((strip, wide), jnp.float32, spec((strip, part), there))] * 2
    return kernel_call(body, flags, steps, ins, outs, aliases)


def finish_left(flags, scale, old, same_total, same_other, total, other, inner, written=None):
    tall, wide = total.shape

    def body(flag_ref, scale_ref, old_ref, same_ref, same_other_ref, total_ref, other_ref, *refs):
        state_ref, fixed_ref = refs[-2:]

        def put(value):
            write_states(old_ref[...], value, scale_ref[0], state_ref, fixed_ref, slice(None))

        is_mate = 1 - flag_ref[MIDDLE] if inner else flag_ref[MIDDLE]
        mine = flag_ref[CORE] == pl.program_id(0)
        same = flag_ref[SAME_HALF] == 1

        @pl.when(mine & same)
        def _():
            put(same_ref[pl.ds(pick(is_mate, tall), tall), :])

        @pl.when(mine & jnp.logical_not(same))
        def _():
            put(total_ref[...])

        for index in range(2):

            @pl.when(jnp.logical_not(mine) & same & (is_mate == index))
            def _():
                put(unpack(same_other_ref, index, tall, 2))

        @pl.when(jnp.logical_not(mine) & jnp.logical_not(same))
        def _():
            put(unpack(other_ref, 0, tall, 1))

    there = lambda k, flags: 2 * (1 - flags[CORE] if inner else flags[CORE]) + k
    ins = [(scale, pl.BlockSpec(memory_space=pltpu.SMEM)), (old, spec((tall, wide), there))]
    ins += [(array, whole(array)) for array in (same_total, same_other, total, other)]
    aliases = None
    if written is not None:
        ins += [(array, pl.BlockSpec(memory_space=pl.ANY)) for array in written]
        aliases = {7: 0, 8: 1}
    outs = [(old.shape, jnp.float32, spec((tall, wide), there))] * 2
    return kernel_call(body, flags, 2, ins, outs, aliases)


def dot(a, b, a_dim, b_dim):
    return lax.dot_general(
        a, b, (((a_dim,), (b_dim,)), ((), ())), preferred_element_type=jnp.float32
    )


AXES = ("row", "col")
CHIPS = [(z, y) for z in range(4) for y in range(2)]


def at(z, y, c):
    return (z * 2 + y) * 2 + c


def send(value, rule):
    pairs = []
    for z, y in CHIPS:
        for c in range(2):
            dest = rule(z, y, c)
            if dest is not None:
                pairs.append((at(z, y, c), at(*dest)))
    return lax.ppermute(value, AXES, pairs)


def middle(z):
    return z in (1, 2)


def to_line(z, y, c):
    return (z, c, y) if c != y else None


def pair_line(z, y, c):
    return (z ^ 1, c, y)


def across_line(z, y, c):
    return (3 - z, c, y) if middle(z) else None


def across(z, y, c):
    return (3 - z, y, c) if middle(z) else None


def outward(z, y, c):
    return (z ^ 1, y, c) if middle(z) else None


def beside(z, y, c):
    return (z, y, 1 - c)


def other_y(z, y, c):
    return (z, 1 - y, c)


def to_home(z, y, c):
    return (z, y, 1 - c) if c != z // 2 else None


def to_away(z, y, c):
    return (z, y, 1 - c) if c == z // 2 else None


def line_gather(gradient, left_old, right_old, left_counts, right_counts):
    tile_rows, half_wide = gradient.shape
    block = half_wide // 4
    strip = half_wide // 8
    my_row = lax.axis_index("row")
    c = lax.axis_index("col")
    z, y = my_row // 2, my_row % 2
    side = (z >= 2).astype(jnp.int32)
    is_middle = (z == 1) | (z == 2)
    straight = c == y
    flags = jnp.stack(
        [
            jnp.where(straight, 0, 1),
            0,
            1,
            2 * side,
            2 * (1 - side),
            2 * (1 - side) + 1,
            (c == side).astype(jnp.int32),
            is_middle.astype(jnp.int32),
            c,
        ]
    ).astype(jnp.int32)
    strip_at = (2 * z + c) * strip

    def tie(*values):
        return lax.optimization_barrier(tuple(values))

    def columns(value, first, count):
        return lax.dynamic_slice_in_dim(value, first * block, count * block, 1)

    def strips_of(pair, first=0):
        return [lax.dynamic_slice_in_dim(part, strip_at - first, strip, 1) for part in pair]

    def one(array, at=START):
        return [(array, at)]

    mate = send(gradient, pair_line)
    cross = send(gradient, across_line)
    gradient_t, mate, cross = tie(gradient, mate, cross)
    far = send(mate, across)
    near = send(cross, outward)
    swapped = send(gradient_t, to_line)
    mates = (mate, send(mate, beside))
    crosses = (cross, send(cross, beside))
    [right] = right_terms(
        flags,
        strips_of(mates) + strips_of(crosses),
        [one(part) for part in mates + crosses],
        block,
        4,
    )
    right, swapped = tie(right, swapped)
    mine = jnp.where(straight, gradient, swapped)
    half = half_wide // 2
    own = (
        mine,
        jnp.concatenate([send(mine[:, :half], beside), send(mine[:, half:], beside)], 1),
    )
    own_product, mate_product, same_coded = left_terms(
        flags, own, [one(mine), one(mate)], half, 2
    )
    same_products = [own_product, mate_product]
    same_got = send(same_coded, other_y)
    same_coded, own_o = tie(same_coded, own[1])
    own = (mine, own_o)
    [right] = right_terms(
        flags, strips_of(own), [one(part) for part in own], block, 4, before=right
    )

    right, near, far = tie(right, near, far)
    end_home = send(columns(far, 2 * side, 2), outward)
    nears = (near, send(near, beside))
    far_o = send(far, beside)
    near_product, near_coded = left_terms(
        flags, own, [[(near, START), (cross, START)]], half, 2
    )
    near_got = send(near_coded, other_y)
    near_coded, near, near_o = tie(near_coded, *nears)
    nears = (near, near_o)
    [right] = right_terms(
        flags, strips_of(nears), [one(part) for part in nears], block, 4, before=right
    )
    far_t, right = tie(far, right)
    far_away, same_got, right = tie(columns(far_t, 2 * (1 - side), 2), same_got, right)
    same_total, same_out = add_up(flags, same_products, same_got)
    same_other = send(same_out, to_home)
    same_out, near_got = tie(same_out, near_got)
    near_total, near_out = add_up(flags, [near_product], near_got)
    near_other = send(near_out, to_away)

    right, near_out, end_home, far_o = tie(right, near_out, end_home, far_o)
    far_away, end_home = tie(far_away, end_home)
    end_away = send(far_away, outward)
    end_home_o = send(end_home, beside)
    strips = [
        jnp.where(is_middle, strips_of([a])[0], strips_of([b], 2 * side * block)[0])
        for a, b in ((far, end_home), (far_o, end_home_o))
    ]

    def last_right(strips, end, end_o, start, at, steps):
        return right_terms(
            flags,
            strips,
            [[(end, start), (far, at)], [(end_o, start), (far_o, at)]],
            block,
            steps,
            at=at,
            before=right,
            last=True,
            hand_on=isinstance(strips, list),
        )

    right_home, home_coded, strips = last_right(strips, end_home, end_home_o, START, HOME, 2)
    home_got = send(home_coded, to_line)
    home_coded, end_home = tie(home_coded, end_home)
    [far_product] = left_terms(
        flags, own, [[(end_home, START), (far, HOME)]], block, 2, at=HOME, last=False
    )
    left_scale = 1.0 / denominator(left_counts).reshape(1)
    right_scale = 1.0 / denominator(right_counts)
    old = right_old[0]
    far_product, near_other, same_other = tie(far_product, near_other, same_other)
    left_done = finish_left(
        flags, left_scale, left_old, same_total, same_other, near_total, near_other, True
    )
    left_done[0], far_product, end_away, home_got = tie(
        left_done[0], far_product, end_away, home_got
    )
    end_away_o = send(end_away, beside)
    far_product, far_coded = left_terms(
        flags, own, [[(end_away, START), (far, AWAY)]], block, 2, at=AWAY, before=[far_product]
    )
    far_got = send(far_coded, other_y)
    far_coded, end_away_o = tie(far_coded, end_away_o)
    right_away, away_coded = last_right(strips, end_away, end_away_o, START, AWAY, 1)
    away_got = send(away_coded, to_line)
    away_coded, end_away_o = tie(away_coded, end_away_o)
    right_last, last_coded = last_right(strips, end_away, end_away_o, NEXT, LAST, 1)
    last_got = send(last_coded, to_line)
    last_coded, far_got = tie(last_coded, far_got)
    far_total, far_out = add_up(flags, [far_product], far_got)
    far_other = send(far_out, to_away)
    far_out, home_got = tie(far_out, home_got)
    right_done = finish_right(flags, right_scale, old, right_home, home_got, HOME, block, 2)
    right_done[0], away_got = tie(right_done[0], away_got)
    right_done = finish_right(
        flags, right_scale, old, right_away, away_got, AWAY, block, 1, right_done
    )
    right_done[0], far_other = tie(right_done[0], far_other)
    left_state, left_fixed = finish_left(
        flags, left_scale, left_old, same_total, same_other, far_total, far_other, False, left_done
    )
    left_state, last_got = tie(left_state, last_got)
    right_state, right_fixed = finish_right(
        flags, right_scale, old, right_last, last_got, LAST, block, 1, right_done
    )
    return (left_state, left_fixed, right_state[None], right_fixed[None])


def solution(mesh):
    local = line_gather if mesh.shape["row"] == 8 else ring
    return jax.shard_map(
        local,
        mesh=mesh,
        in_specs=(
            P(("groups", "row"), "col"),
            P(("groups", "row"), "col"),
            P(("groups", "col"), "row", None),
            P(("groups", "row"), "col"),
            P(("groups", "col")),
        ),
        out_specs=(
            P(("groups", "row"), "col"),
            P(("groups", "row"), "col"),
            P(("groups", "col"), "row", None),
            P(("groups", "col"), "row", None),
        ),
        check_vma=False,
    )
```
